32 devices in a mesh: blk: 8 (over y, x, core), head: 4 (over z).
Axes of the slice: x: 2, y: 2, z: 4, core: 2. Of those that a mesh axis runs over, the one named last changes fastest.
Arguments:
- tokens: bfloat16 [16384, 1024], P(('blk', 'head')), may hold values from -6 to 6
- cotangent: bfloat16 [16384, 1024], P(('blk', 'head')), may hold values from -6 to 6
- lengths: int32 [32], replicated, may hold values from 1 to 14407, as said below
- valid_count: int32 [1], replicated, may hold values from 14337 to 16256
- first_gain: bfloat16 [1024], P(('blk', 'head')), may hold values from 0.25 to 1.75
- first_shift: bfloat16 [1024], P(('blk', 'head')), may hold values from -1.75 to 1.75
- joined_weight: bfloat16 [1024, 3072], P(('blk', 'head')), as said below
- joined_bias: bfloat16 [2048], P(('blk', 'head')), may hold values from -1.75 to 1.75
- dense_weight: bfloat16 [1024, 1024], P(('blk', 'head')), may hold values from -0.5 to 0.5
- dense_bias: bfloat16 [1024], P(('blk', 'head')), may hold values from -1.75 to 1.75
- second_gain: bfloat16 [1024], P(('blk', 'head')), may hold values from 0.25 to 1.75
- second_shift: bfloat16 [1024], P(('blk', 'head')), may hold values from -1.75 to 1.75
- up_weight: bfloat16 [1024, 4096], P(('blk', 'head')), may hold values from -0.1875 to 0.1875
- up_bias: bfloat16 [4096], P(('blk', 'head')), may hold values from -1.75 to 1.75
- down_weight: bfloat16 [4096, 1024], P(('blk', 'head')), may hold values from -0.09375 to 0.09375
- down_bias: bfloat16 [1024], P(('blk', 'head')), may hold values from -1.75 to 1.75
Outputs:
- layer_output: bfloat16 [16384, 1024], P(('blk', 'head'))
- input_grad: bfloat16 [16384, 1024], P(('blk', 'head'))
- first_gain_grad: float32 [1024], P(('blk', 'head'))
- first_shift_grad: float32 [1024], P(('blk', 'head'))
- joined_weight_grad: float32 [1024, 3072], P(('blk', 'head'))
- joined_bias_grad: float32 [2048], P(('blk', 'head'))
- dense_weight_grad: float32 [1024, 1024], P(('blk', 'head'))
- dense_bias_grad: float32 [1024], P(('blk', 'head'))
- second_gain_grad: float32 [1024], P(('blk', 'head'))
- second_shift_grad: float32 [1024], P(('blk', 'head'))
- up_weight_grad: float32 [1024, 4096], P(('blk', 'head'))
- up_bias_grad: float32 [4096], P(('blk', 'head'))
- down_weight_grad: float32 [4096, 1024], P(('blk', 'head'))
- down_bias_grad: float32 [1024], P(('blk', 'head'))
The draws below stay inside these ranges and needn't reach their ends.
Inputs may be any that keep to these rules, and one draw needn't show every extreme that they name: The lengths sum to 16384; the longest document stands at index 16. `joined_weight`: entries are independent, of mean 0, within 6 * (2 / 1024)^(1/2) in magnitude.
All inputs are finite; a program needn't handle non-finite values.
Results may differ from the reference program's by a relative error of at most 0.013.
Values may be sent and summed in bfloat16 or wider, within the bound.
No kernel may reach another device: no remote copies, remote signals or barrier semaphores. Data moves between devices by JAX's collectives and lax.ppermute only.
A program may use at most 256 MiB of HBM per device.

```python
import jax
import jax.numpy as jnp
from jax import lax

D = 1024
HEADS = 16
HEAD_DIM = 64
FF = 4096
WINDOW = 1024
TOK_DEV = 512
NDOCS = 32
BLOCK = 2048
TOKENS = 16384


def paired_group(key, count):
    pair_total = BLOCK // count
    pair_count = count // 2
    key_pick, key_order = jax.random.split(key)
    picked = jax.random.randint(key_pick, (pair_count,), 1, pair_total).astype(jnp.int32)
    partner = (pair_total - picked).astype(jnp.int32)
    single = jnp.ones((count % 2,), jnp.int32)
    group = jnp.concatenate([picked, partner, single]).astype(jnp.int32)
    order = jax.random.permutation(key_order, count)
    return group[order].astype(jnp.int32)


def draw_lengths(key, part):
    key = jax.random.fold_in(key, 11)
    head_count = NDOCS // 2
    tail_count = NDOCS - 1 - head_count
    key_head, key_tail = jax.random.split(key)
    head_docs = paired_group(key_head, head_count)
    tail_docs = paired_group(key_tail, tail_count)
    longest = (TOKENS - jnp.sum(head_docs) - jnp.sum(tail_docs)).astype(jnp.int32)
    return jnp.concatenate([head_docs, longest[None], tail_docs]).astype(jnp.int32)


def column_scales():
    column = jnp.arange(3 * D, dtype=jnp.int32)
    kind = column // HEAD_DIM % 3
    factor = jnp.where(kind < 2, jnp.sqrt(jnp.float32(2.0)), jnp.float32(1.0))
    return factor * jnp.float32(D) ** (-0.5)


def draw_joined_weight(key, part):
    key = jax.random.fold_in(key, 23)
    unit = jax.random.truncated_normal(key, -6.0, 6.0, (D, 3 * D), jnp.float32)
    return (unit * column_scales()[None, :]).astype(jnp.bfloat16)


def level_of(stream_key, shape, cuts, smallest, high):
    def one(dim, parts):
        steps = jax.random.uniform(jax.random.fold_in(jax.random.fold_in(stream_key, 6), dim), (parts,), jnp.float32, smallest / len(cuts), high / len(cuts))
        return jnp.repeat(jnp.exp(steps), shape[dim] // parts).reshape((-1,) + (1,) * (len(shape) - dim - 1))

    factor_of = one(*cuts[0])
    for cut in cuts[1:]:
        factor_of = factor_of * one(*cut)
    return factor_of


def scatter_about(stream_key, shape, scale, limit, cuts=(), kind=jnp.bfloat16):
    entries = jax.random.normal(stream_key, shape, jnp.float32) * scale
    if len(cuts) > 0:
        entries = level_of(stream_key, shape, cuts, -0.22, 0.18) * entries
    return jnp.clip(entries, min=-limit, max=limit).astype(kind)


def setup_inputs(seed: int = 0) -> dict:
    arg_keys = jax.random.split(jax.random.key(seed), 17)
    tokens = scatter_about(arg_keys[0], (TOKENS, D), 1.0, 6.0, ((0, 32),))
    cotangent = scatter_about(arg_keys[1], (TOKENS, D), 1.0, 6.0, ((0, 32),))
    lengths = draw_lengths(jax.random.fold_in(arg_keys[16], 71), 0)
    valid_count = jax.random.randint(arg_keys[3], (1,), TOKENS - BLOCK + 1, TOKENS - TOK_DEV // 4 + 1).astype(jnp.int32)
    first_gain = jnp.clip(1.0 + 0.15 * jax.random.normal(arg_keys[4], (D,), jnp.float32), 0.25, 1.75).astype(jnp.bfloat16)
    first_shift = scatter_about(arg_keys[5], (D,), 0.3, 1.75, ((0, 32),))
    joined_weight = draw_joined_weight(jax.random.fold_in(arg_keys[16], 71), 0)
    joined_bias = scatter_about(arg_keys[7], (2 * D,), 0.3, 1.75, ((0, 32),))
    dense_weight = scatter_about(arg_keys[8], (D, D), (D // 8) ** -0.5, 0.5, ((0, 32),))
    dense_bias = scatter_about(arg_keys[9], (D,), 0.3, 1.75, ((0, 32),))
    second_gain = jnp.clip(1.0 + 0.15 * jax.random.normal(arg_keys[10], (D,), jnp.float32), 0.25, 1.75).astype(jnp.bfloat16)
    second_shift = scatter_about(arg_keys[11], (D,), 0.3, 1.75, ((0, 32),))
    up_weight = scatter_about(arg_keys[12], (D, FF), D ** -0.5, 0.1875, ((0, 32),))
    up_bias = scatter_about(arg_keys[13], (FF,), 0.3, 1.75, ((0, 32),))
    down_weight = scatter_about(arg_keys[14], (FF, D), FF ** -0.5, 0.09375, ((0, 32),))
    down_bias = scatter_about(arg_keys[15], (D,), 0.3, 1.75, ((0, 32),))
    return {"tokens": tokens, "cotangent": cotangent, "lengths": lengths, "valid_count": valid_count, "first_gain": first_gain, "first_shift": first_shift, "joined_weight": joined_weight, "joined_bias": joined_bias, "dense_weight": dense_weight, "dense_bias": dense_bias, "second_gain": second_gain, "second_shift": second_shift, "up_weight": up_weight, "up_bias": up_bias, "down_weight": down_weight, "down_bias": down_bias}


@jax.custom_vjp
def low(v):
    return lax.optimization_barrier(v.astype(jnp.bfloat16)).astype(jnp.float32)

@jax.custom_vjp
def low_back(v):
    return v

def low_keep(v):
    return (low(v), None)

def low_pass(kept, grad):
    return (grad,)

def back_keep(v):
    return (v, None)

def back_low(kept, grad):
    return (low(grad),)
low.defvjp(low_keep, low_pass)
low_back.defvjp(back_keep, back_low)
norm_eps = 1e-05
highest = lax.Precision.HIGHEST

def layer_norm(values, gain_row, shift_row):
    centred = values - lax.optimization_barrier(jnp.mean(values, axis=-1, keepdims=True))
    spread = lax.optimization_barrier(jnp.mean(centred * centred, axis=-1, keepdims=True))
    return centred * lax.rsqrt(spread + norm_eps) * gain_row + shift_row

def segment_ids(lengths, valid_count, positions):
    doc_ends = jnp.cumsum(lengths).astype(jnp.int32)
    passed = lax.optimization_barrier(jnp.sum((doc_ends[None, :] <= positions[:, None]).astype(jnp.int32), axis=1)).astype(jnp.int32)
    inside = jnp.where(positions < valid_count[0], passed, NDOCS)
    return jnp.where(positions < 0, -1, inside).astype(jnp.int32)

def head_slopes(first_head, head_group):
    order = first_head + jnp.arange(head_group, dtype=jnp.int32)
    return jnp.exp2(-8.0 * (order.astype(jnp.float32) + 1.0) / HEADS)

def widen_bias(joined_bias):
    pair_view = joined_bias.reshape(HEADS, 2, HEAD_DIM)
    key_zeros = jnp.zeros_like(pair_view[:, :1])
    return jnp.concatenate([pair_view[:, :1], key_zeros, pair_view[:, 1:]], axis=1).reshape(3 * HEADS * HEAD_DIM)

def attention(joined, seg_ext):
    heads_view = joined.reshape(TOKENS, HEADS, 3, HEAD_DIM)
    queries = heads_view[:, :, 0]
    key_pad = jnp.zeros((WINDOW, HEADS, 2, HEAD_DIM), joined.dtype)
    pairs_ext = jnp.concatenate([key_pad, heads_view[:, :, 1:]], axis=0)
    query_rows = min(512, TOKENS)
    slopes = head_slopes(0, HEADS)
    row_index = jnp.arange(query_rows, dtype=jnp.int32)
    key_index = jnp.arange(query_rows + WINDOW, dtype=jnp.int32)
    gap_size = row_index[:, None] + WINDOW - key_index[None, :]
    offsets = (-gap_size).astype(jnp.float32)
    scale = HEAD_DIM ** (-0.5)

    def one_block(start):
        query_block = lax.dynamic_slice_in_dim(queries, start, query_rows, 0)
        pair_block = lax.dynamic_slice_in_dim(pairs_ext, start, query_rows + WINDOW, 0)
        seg_query = lax.dynamic_slice_in_dim(seg_ext, (start + WINDOW).astype(jnp.int32), query_rows, 0)
        seg_keys = lax.dynamic_slice_in_dim(seg_ext, start, query_rows + WINDOW, 0)
        allowed = (seg_query[:, None] == seg_keys[None, :]) & (gap_size >= 0) & (gap_size < WINDOW)
        raw = jnp.einsum('qhd,khd->hqk', query_block, pair_block[:, :, 0], precision=highest) * scale
        raw = raw + slopes[:, None, None] * offsets[None]
        scores = low_back(jnp.where(allowed[None], raw, -1e+30))
        attend_prob = low(jax.nn.softmax(scores, axis=-1))
        return jnp.einsum('hqk,khd->qhd', attend_prob, pair_block[:, :, 1], precision=highest)
    starts = jnp.arange(TOKENS // query_rows, dtype=jnp.int32) * query_rows
    blocks = lax.map(jax.checkpoint(one_block), starts)
    return blocks.reshape(TOKENS, HEADS * HEAD_DIM)

def forward(values, first_gain, first_shift, joined_weight, joined_bias, dense_weight, dense_bias, second_gain, second_shift, up_weight, up_bias, down_weight, down_bias, seg_ext, live_rows):
    normed_one = low(layer_norm(values, first_gain, first_shift))
    joined = jnp.dot(normed_one, joined_weight, precision=highest) + widen_bias(joined_bias)
    joined = low_back(low(joined))
    context = low_back(low(attention(joined, seg_ext)))
    branch_one = low_back(jnp.dot(context, dense_weight, precision=highest) + dense_bias)
    middle = values + branch_one
    normed_two = low(layer_norm(middle, second_gain, second_shift))

    def feed_forward(row_block):
        pre_act = low_back(jnp.dot(row_block, up_weight, precision=highest) + up_bias)
        hidden = low(jax.nn.gelu(pre_act, approximate=True))
        return jnp.dot(hidden, down_weight, precision=highest) + down_bias
    group_rows = min(4096, TOKENS)
    pieces = normed_two.reshape(TOKENS // group_rows, group_rows, D)
    branch_two = lax.map(jax.checkpoint(feed_forward), pieces).reshape(TOKENS, D)
    return jnp.where(live_rows[:, None], middle + branch_two, 0.0)

def reference(tokens, cotangent, lengths, valid_count, first_gain, first_shift, joined_weight, joined_bias, dense_weight, dense_bias, second_gain, second_shift, up_weight, up_bias, down_weight, down_bias):
    positions = jnp.arange(TOKENS, dtype=jnp.int32)
    seg_ext = jnp.concatenate([jnp.full((WINDOW,), -1, jnp.int32), segment_ids(lengths, valid_count, positions)])
    live_rows = positions < valid_count[0]
    param_list = (first_gain, first_shift, joined_weight, joined_bias, dense_weight, dense_bias, second_gain, second_shift, up_weight, up_bias, down_weight, down_bias)
    floats = tuple((member.astype(jnp.float32) for member in param_list))

    def run_layer(values, weights_in):
        return forward(values, *weights_in, seg_ext, live_rows)
    result, pullback = jax.vjp(run_layer, tokens.astype(jnp.float32), floats)
    input_change, grads = pullback(cotangent.astype(jnp.float32))
    return (result.astype(jnp.bfloat16), input_change.astype(jnp.bfloat16), grads[0], grads[1], grads[2], grads[3], grads[4], grads[5], grads[6], grads[7], grads[8], grads[9], grads[10], grads[11])
```

```python
import functools

import jax
import jax.numpy as jnp
import numpy as np
from jax import lax
from jax.experimental import pallas as pl
from jax.experimental.pallas import tpu as pltpu
from jax.sharding import PartitionSpec as P

HEADS = 16
HEAD_DIM = 64
WINDOW = 1024
NDOCS = 32

BOTH = ("blk", "head")
norm_eps = 1e-05
bf16 = jnp.bfloat16
f32 = jnp.float32

MASKED = -1e30
TILE = 256
LANES = 128
SLOPE_LANE = NDOCS + 1
ROW_LANE = SLOPE_LANE + 6
SCALE = HEAD_DIM**-0.5


class Grid:
    def __init__(self):
        blocks, heads = lax.axis_size("blk"), lax.axis_size("head")
        self.count = blocks * heads
        self.size = (2, blocks // 4, 2, heads)
        blk, z = lax.axis_index("blk"), lax.axis_index("head")
        self.here = (blk // (2 * self.size[1]), blk // 2 % self.size[1], blk % 2, z)
        self.linear = blk * heads + z

    def next_along(self, axis):
        places = np.arange(self.count).reshape(self.size)
        return list(zip(places.ravel().tolist(), np.roll(places, -1, axis).ravel().tolist()))

    def shift(self, block, axis):
        return lax.ppermute(block, BOTH, self.next_along(axis))

    def to_later(self, block):
        return lax.ppermute(block, BOTH, [(i, i + 1) for i in range(self.count - 1)])

    def to_earlier(self, block):
        return lax.ppermute(block, BOTH, [(i + 1, i) for i in range(self.count - 1)])


Y, X, CORE, Z = range(4)


def ring_gather(grid, block, axis):
    pieces = [block]
    for _ in range(grid.size[axis] - 1):
        pieces.append(grid.shift(pieces[-1], axis))
    return pieces


def gather(grid, shard):
    rows, width = shard.shape
    size = grid.size
    y, x, core, z = grid.here
    half = size[Z] // 2
    line = jnp.zeros((size[Z], rows, width), shard.dtype)
    for step, piece in enumerate(ring_gather(grid, shard, Z)):
        line = lax.dynamic_update_slice(line, piece[None], ((z - step) % size[Z], 0, 0))
    whole = jnp.zeros((*size, rows, width), shard.dtype)
    for part, (one, two) in enumerate(((X, Y), (Y, X))):
        near = jnp.stack(ring_gather(grid, line[part * half : (part + 1) * half], one))
        for far_step, piece in enumerate(ring_gather(grid, near, two)):
            other = grid.shift(piece, CORE)
            for near_step in range(size[one]):
                at = {one: (grid.here[one] - near_step) % size[one], two: (grid.here[two] - far_step) % size[two]}
                for block, which in ((piece, core), (other, 1 - core)):
                    whole = lax.dynamic_update_slice(
                        whole, block[near_step][None, None, None], (at[Y], at[X], which, part * half, 0, 0)
                    )
    return whole.reshape(grid.count * rows, width)


def ring_reduce(grid, terms, axis, dim, last_type=bf16):
    count, place = grid.size[axis], grid.here[axis]

    def term(step):
        return lax.dynamic_index_in_dim(terms, (place - step) % count, dim, keepdims=False)

    total = term(1)
    for step in range(2, count + 1):
        arrived = grid.shift(total, axis)
        total = (arrived.astype(f32) + term(step).astype(f32)).astype(last_type if step == count else terms.dtype)
    return total


def reduce_scatter(grid, terms):
    rows, width = terms.shape[0] // grid.count, terms.shape[1]
    terms = ring_reduce(grid, terms.reshape(*grid.size, rows, width), CORE, 2, terms.dtype)
    half = grid.size[Z] // 2
    one = ring_reduce(grid, terms[:, :, :half], X, 1, terms.dtype)
    one = ring_reduce(grid, one, Y, 0, terms.dtype)
    two = ring_reduce(grid, terms[:, :, half:], Y, 0, terms.dtype)
    two = ring_reduce(grid, two, X, 0, terms.dtype)
    return ring_reduce(grid, jnp.concatenate([one, two], axis=0), Z, 0, f32)


def reduce_scatter_small(grid, terms):
    terms = terms.reshape(*grid.size, terms.shape[1])
    for axis, dim in ((CORE, 2), (X, 1), (Y, 0), (Z, 0)):
        terms = ring_reduce(grid, terms, axis, dim, terms.dtype)
    return terms


def dot_nn(left, right):
    return lax.dot_general(left, right, (((1,), (0,)), ((), ())), preferred_element_type=f32)


def dot_nt(left, right):
    return lax.dot_general(left, right, (((1,), (1,)), ((), ())), preferred_element_type=f32)


def dot_tn(left, right):
    return lax.dot_general(left, right, (((0,), (0,)), ((), ())), preferred_element_type=f32)


def thirds(values):
    high = values.astype(bf16)
    rest = values - high.astype(f32)
    middle = rest.astype(bf16)
    return high, middle, (rest - middle.astype(f32)).astype(bf16)


def slope_lanes():
    lanes = np.zeros((HEADS // 2, 8, LANES), np.float32)
    for h in range(HEADS):
        rest = np.float32(2.0 ** (-8.0 * (h + 1) / HEADS))
        for part in range(3):
            piece = np.float32(rest.astype(bf16))
            rest = np.float32(rest - piece)
            lanes[h // 2, h % 2, SLOPE_LANE + part] = piece
            lanes[h // 2, h % 2, SLOPE_LANE + 3 + part] = piece
    return lanes


def side_lanes(seg_ext, tok_rows):
    lane = jnp.arange(LANES, dtype=jnp.int32)
    doc = lane[None, :] <= NDOCS
    seg_query = seg_ext[seg_ext.shape[0] - tok_rows :]
    query_side = jnp.where(doc & (lane[None, :] == seg_query[:, None]), 1.0, 0.0).astype(bf16)
    key_pos = jnp.arange(seg_ext.shape[0], dtype=jnp.int32)[:, None]
    key_side = jnp.where(doc & (lane[None, :] != seg_ext[:, None]), MASKED, 0.0)
    key_side = jnp.where((lane >= SLOPE_LANE) & (lane < SLOPE_LANE + 3), (key_pos // TILE * TILE).astype(f32), key_side)
    key_side = jnp.where((lane >= SLOPE_LANE + 3) & (lane < ROW_LANE), (key_pos % TILE).astype(f32), key_side)
    key_side = jnp.where((lane >= ROW_LANE) & (lane < ROW_LANE + 3), 1.0, key_side)
    return query_side, key_side.astype(bf16)


def key_tiles(tile):
    wide = WINDOW // TILE
    edges = [(tile + step) * TILE for step in (0, 1, wide, wide + 1)]
    return [slice(edges[i], edges[i + 1]) for i in range(3)]


def attend_kernel(query, key, value, query_side, key_side, slope, context, log_total):
    pair = pl.program_id(0)
    lane = lax.broadcasted_iota(jnp.int32, (TILE, LANES), 1)
    causal = lax.broadcasted_iota(jnp.int32, (TILE, TILE), 0) >= lax.broadcasted_iota(jnp.int32, (TILE, TILE), 1)
    keys = jnp.concatenate([key[...], key_side[...]], axis=1)
    for tile in range(query.shape[0] // TILE):
        rows = slice(tile * TILE, (tile + 1) * TILE)
        first, middle, last = key_tiles(tile)
        scaled = query[rows, :] * jnp.asarray(SCALE, bf16)
        outs, logs = [], []
        for half in range(2):
            mine = (lane >= HEAD_DIM) == (half == 1)
            side = query_side[rows, :] + slope[0, half : half + 1, :].astype(bf16)
            queries = jnp.concatenate([jnp.where(mine, scaled, jnp.zeros_like(scaled)), side], axis=1)
            inner = dot_nt(queries, keys[middle])
            outer = jnp.where(causal, dot_nt(queries, keys[last]), dot_nt(queries, keys[first]))
            top = jnp.maximum(jnp.max(inner, axis=1, keepdims=True), jnp.max(outer, axis=1, keepdims=True))
            inner = jnp.exp(inner - top)
            outer = jnp.exp(outer - top)
            total = jnp.sum(inner, axis=1, keepdims=True) + jnp.sum(outer, axis=1, keepdims=True)
            summed = dot_nn(inner.astype(bf16), value[middle, :])
            summed += dot_nn(jnp.where(causal, outer, 0.0).astype(bf16), value[last, :])
            summed += dot_nn(jnp.where(causal, 0.0, outer).astype(bf16), value[first, :])
            outs.append(summed / total)
            logs.append(top + jnp.log(total))
        context[rows, :] = jnp.where(lane < HEAD_DIM, outs[0], outs[1]).astype(bf16)
        before = jnp.where(pair == 0, jnp.zeros((TILE, LANES), f32), log_total[rows, :])
        log_total[rows, :] = jnp.where(lane == 2 * pair, logs[0], jnp.where(lane == 2 * pair + 1, logs[1], before))


def attend(queries, pairs, query_side, key_side, slopes):
    tok_rows, width = queries.shape
    key_rows = pairs.shape[0]
    steps = HEADS // 2
    return pl.pallas_call(
        attend_kernel,
        grid=(steps,),
        in_specs=[
            pl.BlockSpec((tok_rows, LANES), lambda p: (0, p)),
            pl.BlockSpec((key_rows, LANES), lambda p: (0, p)),
            pl.BlockSpec((key_rows, LANES), lambda p: (0, steps + p)),
            pl.BlockSpec((tok_rows, LANES), lambda p: (0, 0)),
            pl.BlockSpec((key_rows, LANES), lambda p: (0, 0)),
            pl.BlockSpec((1, 8, LANES), lambda p: (p, 0, 0)),
        ],
        out_specs=[
            pl.BlockSpec((tok_rows, LANES), lambda p: (0, p)),
            pl.BlockSpec((tok_rows, LANES), lambda p: (0, 0)),
        ],
        out_shape=[
            jax.ShapeDtypeStruct((tok_rows, width), bf16),
            jax.ShapeDtypeStruct((tok_rows, LANES), f32),
        ],
        compiler_params=pltpu.CompilerParams(vmem_limit_bytes=40 * 2**20),
        cost_estimate=pl.CostEstimate(
            flops=HEADS * tok_rows * 1280 * 1024,
            bytes_accessed=4 * (key_rows + tok_rows) * width,
            transcendentals=HEADS * tok_rows * WINDOW,
        ),
    )(queries, pairs, pairs, query_side, key_side, slopes)


def attend_back_kernel(
    query, key, value, change, context, log_total, query_side, key_side, slope,
    query_change, key_change, value_change, key_sum, value_sum,
):
    pair = pl.program_id(0)
    lane = lax.broadcasted_iota(jnp.int32, (TILE, LANES), 1)
    causal = lax.broadcasted_iota(jnp.int32, (TILE, TILE), 0) <= lax.broadcasted_iota(jnp.int32, (TILE, TILE), 1)
    keys = jnp.concatenate([key[...], key_side[...]], axis=1)
    values = jnp.concatenate([value[...], key_side[...]], axis=1)
    keys_across = key[...].T
    key_sum[...] = jnp.zeros_like(key_sum)
    value_sum[...] = jnp.zeros_like(value_sum)

    def row_lanes(column):
        high, middle, low = thirds(column)
        lanes = jnp.where(lane == ROW_LANE + 2, low, jnp.zeros((TILE, LANES), bf16))
        return jnp.where(lane == ROW_LANE, high, jnp.where(lane == ROW_LANE + 1, middle, lanes))

    for tile in range(query.shape[0] // TILE):
        rows = slice(tile * TILE, (tile + 1) * TILE)
        first, middle, last = key_tiles(tile)
        scaled = query[rows, :] * jnp.asarray(SCALE, bf16)
        changed = change[rows, :]
        product = changed.astype(f32) * context[rows, :].astype(f32)
        logs = log_total[rows, :]
        parts = []
        for half in range(2):
            mine = (lane >= HEAD_DIM) == (half == 1)
            asked = jnp.where(mine, scaled, jnp.zeros_like(scaled))
            moved = jnp.where(mine, changed, jnp.zeros_like(changed))
            log_row = jnp.sum(jnp.where(lane == 2 * pair + half, logs, 0.0), axis=1, keepdims=True)
            inner_row = jnp.sum(jnp.where(mine, product, 0.0), axis=1, keepdims=True)
            side = query_side[rows, :] + slope[0, half : half + 1, :].astype(bf16) + row_lanes(-log_row)
            queries = jnp.concatenate([asked, side], axis=1)
            changes = jnp.concatenate([moved, row_lanes(-inner_row)], axis=1)
            prob = jnp.exp(dot_nt(keys[middle], queries))
            prob_edge = jnp.exp(jnp.where(causal, dot_nt(keys[last], queries), dot_nt(keys[first], queries)))
            score = (prob * dot_nt(values[middle], changes)).astype(bf16)
            score_edge = prob_edge * jnp.where(causal, dot_nt(values[last], changes), dot_nt(values[first], changes))
            score_last = jnp.where(causal, score_edge, 0.0).astype(bf16)
            score_first = jnp.where(causal, 0.0, score_edge).astype(bf16)
            value_sum[middle, :] += dot_nn(prob.astype(bf16), moved)
            value_sum[last, :] += dot_nn(jnp.where(causal, prob_edge, 0.0).astype(bf16), moved)
            value_sum[first, :] += dot_nn(jnp.where(causal, 0.0, prob_edge).astype(bf16), moved)
            key_sum[middle, :] += dot_nn(score, asked)
            key_sum[last, :] += dot_nn(score_last, asked)
            key_sum[first, :] += dot_nn(score_first, asked)
            parts.append(
                dot_nn(keys_across[:, middle], score)
                + dot_nn(keys_across[:, last], score_last)
                + dot_nn(keys_across[:, first], score_first)
            )
        entry = lax.broadcasted_iota(jnp.int32, (LANES, TILE), 0)
        query_change[rows, :] = (jnp.where(entry < HEAD_DIM, parts[0], parts[1]).T * SCALE).astype(bf16)
    key_change[...] = key_sum[...].astype(bf16)
    value_change[...] = value_sum[...].astype(bf16)


def attend_back(queries, pairs, change, context, log_total, query_side, key_side, slopes):
    tok_rows, width = queries.shape
    key_rows = pairs.shape[0]
    steps = HEADS // 2
    by_query = pl.BlockSpec((tok_rows, LANES), lambda p: (0, p))
    by_key = pl.BlockSpec((key_rows, LANES), lambda p: (0, p))
    return pl.pallas_call(
        attend_back_kernel,
        grid=(steps,),
        in_specs=[
            by_query,
            by_key,
            pl.BlockSpec((key_rows, LANES), lambda p: (0, steps + p)),
            by_query,
            by_query,
            pl.BlockSpec((tok_rows, LANES), lambda p: (0, 0)),
            pl.BlockSpec((tok_rows, LANES), lambda p: (0, 0)),
            pl.BlockSpec((key_rows, LANES), lambda p: (0, 0)),
            pl.BlockSpec((1, 8, LANES), lambda p: (p, 0, 0)),
        ],
        out_specs=[by_query, by_key, by_key],
        out_shape=[
            jax.ShapeDtypeStruct((tok_rows, width), bf16),
            jax.ShapeDtypeStruct((key_rows, width), bf16),
            jax.ShapeDtypeStruct((key_rows, width), bf16),
        ],
        scratch_shapes=[pltpu.VMEM((key_rows, LANES), f32), pltpu.VMEM((key_rows, LANES), f32)],
        compiler_params=pltpu.CompilerParams(vmem_limit_bytes=40 * 2**20),
        cost_estimate=pl.CostEstimate(
            flops=HEADS * tok_rows * 1280 * 2560,
            bytes_accessed=8 * (key_rows + tok_rows) * width,
            transcendentals=HEADS * tok_rows * WINDOW,
        ),
    )(queries, pairs, pairs, change, context, log_total, query_side, key_side, slopes)


def segment_ids(lengths, valid_count, positions):
    doc_ends = jnp.cumsum(lengths)
    passed = jnp.sum((doc_ends[None, :] <= positions[:, None]).astype(jnp.int32), axis=1)
    inside = jnp.where(positions < valid_count[0], passed, NDOCS)
    return jnp.where(positions < 0, -1, inside)


def normalize(values):
    centred = values - jnp.mean(values, axis=-1, keepdims=True)
    inverse = lax.rsqrt(jnp.mean(centred * centred, axis=-1, keepdims=True) + norm_eps)
    return centred * inverse, inverse


def norm_back(change, normal, inverse, gain):
    scaled = change * gain
    mean_one = jnp.mean(scaled, axis=-1, keepdims=True)
    mean_two = jnp.mean(scaled * normal, axis=-1, keepdims=True)
    return inverse * (scaled - mean_one - normal * mean_two)


ROOT = np.sqrt(2.0 / np.pi).astype(np.float32)


def gelu_parts(values):
    square = values * values
    bent = jnp.tanh(ROOT * (values + 0.044715 * (values * square)))
    rise = 0.5 * (1.0 + bent)
    slope = rise + 0.5 * values * (1.0 - bent * bent) * (ROOT * (1.0 + 3.0 * 0.044715 * square))
    return values * rise, slope


def to_kinds(columns):
    rows = columns.shape[0]
    return columns.reshape(rows, HEADS, 3, HEAD_DIM).swapaxes(1, 2).reshape(rows, 3 * HEADS * HEAD_DIM)


def from_kinds(columns):
    rows = columns.shape[0]
    return columns.reshape(rows, 3, HEADS, HEAD_DIM).swapaxes(1, 2).reshape(rows, 3 * HEADS * HEAD_DIM)


def on_device(
    tokens,
    cotangent,
    lengths,
    valid_count,
    first_gain,
    first_shift,
    joined_weight,
    joined_bias,
    dense_weight,
    dense_bias,
    second_gain,
    second_shift,
    up_weight,
    up_bias,
    down_weight,
    down_bias,
):
    grid = Grid()
    tok_rows, width = tokens.shape
    hops = WINDOW // tok_rows
    shard_rows = joined_weight.shape[0]

    vectors = (first_gain, first_shift, joined_bias, dense_bias, second_gain, second_shift, up_bias, down_bias)
    counts = [v.shape[0] for v in vectors]
    riders = jnp.concatenate(vectors).reshape(shard_rows, -1)
    rider_width = riders.shape[1]
    riders = jnp.pad(riders, ((0, 0), (0, -rider_width % LANES)))
    joined_all = gather(grid, jnp.concatenate([to_kinds(joined_weight), riders], axis=1))
    before = [tokens]
    for _ in range(hops):
        before.append(grid.to_later(before[-1]))
    dense_mat = gather(grid, dense_weight)
    up_mat = gather(grid, up_weight)
    down_mat = gather(grid, down_weight)
    joined_mat = joined_all[:, : 3 * width]
    rows_of = joined_all[:, 3 * width : 3 * width + rider_width].reshape(grid.count, -1).astype(f32)
    cuts = np.cumsum([0] + counts)
    gain_one, shift_one, joined_vec, dense_vec, gain_two, shift_two, up_vec, down_vec = (
        rows_of[:, cuts[i] : cuts[i + 1]].reshape(-1) for i in range(len(counts))
    )
    joined_pairs = joined_vec.reshape(HEADS, 2, HEAD_DIM)
    query_vec = joined_pairs[:, 0].reshape(-1)
    pair_vec = jnp.concatenate([jnp.zeros_like(query_vec), joined_pairs[:, 1].reshape(-1)])

    first_pos = grid.linear * tok_rows - WINDOW
    positions = first_pos + jnp.arange(WINDOW + tok_rows, dtype=jnp.int32)
    seg_ext = segment_ids(lengths, valid_count, positions)
    query_side, key_side = side_lanes(seg_ext, tok_rows)
    slopes = jnp.asarray(slope_lanes())
    live_rows = (positions[WINDOW:] < valid_count[0])[:, None]

    values = tokens.astype(f32)
    normal_ext, inverse_ext = normalize(jnp.concatenate(before[::-1], axis=0).astype(f32))
    normed_ext = (normal_ext * gain_one + shift_one).astype(bf16)
    normed_one = normed_ext[WINDOW:]
    queries = (dot_nn(normed_one, joined_mat[:, :width]) + query_vec).astype(bf16)
    pairs = (dot_nn(normed_ext, joined_mat[:, width:]) + pair_vec).astype(bf16)
    context, log_total = attend(queries, pairs, query_side, key_side, slopes)
    middle = values + dot_nn(context, dense_mat) + dense_vec
    normal_two, inverse_two = normalize(middle)
    normed_two = (normal_two * gain_two + shift_two).astype(bf16)
    pre_act = dot_nn(normed_two, up_mat) + up_vec
    hidden, slope = gelu_parts(pre_act)
    hidden = hidden.astype(bf16)
    layer_output = jnp.where(live_rows, middle + (dot_nn(hidden, down_mat) + down_vec), 0.0).astype(bf16)

    change_low = jnp.where(live_rows, cotangent, jnp.zeros_like(cotangent))
    out_change = change_low.astype(f32)
    down_vec_grad = jnp.sum(out_change, axis=0)
    down_grad = reduce_scatter(grid, dot_tn(hidden, change_low).astype(bf16))
    pre_change = (dot_nt(change_low, down_mat) * slope).astype(bf16)
    up_vec_grad = jnp.sum(pre_change.astype(f32), axis=0)
    up_grad = reduce_scatter(grid, dot_tn(normed_two, pre_change).astype(bf16))
    normed_change = dot_nt(pre_change, up_mat)
    gain_two_grad = jnp.sum(normed_change * normal_two, axis=0)
    shift_two_grad = jnp.sum(normed_change, axis=0)
    middle_change = out_change + norm_back(normed_change, normal_two, inverse_two, gain_two)
    branch_change = middle_change.astype(bf16)
    dense_vec_grad = jnp.sum(branch_change.astype(f32), axis=0)
    dense_grad = reduce_scatter(grid, dot_tn(context, branch_change).astype(bf16))
    context_change = dot_nt(branch_change, dense_mat).astype(bf16)
    query_change, key_change, value_change = attend_back(
        queries, pairs, context_change, context, log_total, query_side, key_side, slopes
    )
    ext_change = dot_nt(key_change, joined_mat[:, width : 2 * width]) + dot_nt(value_change, joined_mat[:, 2 * width :])
    own_change = ext_change[WINDOW:] + dot_nt(query_change, joined_mat[:, :width])
    returned = jnp.zeros((tok_rows, width), f32)
    for hop in range(hops):
        returned = returned + ext_change[hop * tok_rows : (hop + 1) * tok_rows]
        returned = grid.to_earlier(returned.astype(bf16)).astype(f32)
    joined_grad = reduce_scatter(
        grid,
        jnp.concatenate(
            [dot_tn(normed_one, query_change), dot_tn(normed_ext, key_change), dot_tn(normed_ext, value_change)], axis=1
        ).astype(bf16),
    )
    part_change = jnp.concatenate([ext_change[:WINDOW], own_change], axis=0)
    gain_one_grad = jnp.sum(part_change * normal_ext, axis=0)
    shift_one_grad = jnp.sum(part_change, axis=0)
    joined_vec_grad = jnp.stack(
        [
            jnp.sum(query_change.astype(f32), axis=0).reshape(HEADS, HEAD_DIM),
            jnp.sum(value_change.astype(f32), axis=0).reshape(HEADS, HEAD_DIM),
        ],
        axis=1,
    ).reshape(-1)
    input_grad = (
        middle_change + norm_back(own_change + returned, normal_ext[WINDOW:], inverse_ext[WINDOW:], gain_one)
    ).astype(bf16)
    vector_grads = (
        gain_one_grad, shift_one_grad, joined_vec_grad, dense_vec_grad, gain_two_grad, shift_two_grad, up_vec_grad,
        down_vec_grad,
    )
    owned = reduce_scatter_small(grid, jnp.concatenate([v.reshape(grid.count, -1) for v in vector_grads], axis=1))
    owned = [owned[cuts[i] : cuts[i + 1]] for i in range(len(counts))]
    return (
        layer_output,
        input_grad,
        owned[0],
        owned[1],
        from_kinds(joined_grad),
        owned[2],
        dense_grad,
        owned[3],
        owned[4],
        owned[5],
        up_grad,
        owned[6],
        down_grad,
        owned[7],
    )


def solution(mesh):
    rows, vector, same = P(BOTH, None), P(BOTH), P()
    return jax.shard_map(
        on_device,
        mesh=mesh,
        in_specs=(
            rows, rows, same, same, vector, vector, rows, vector, rows, vector, vector, vector, rows, vector, rows, vector
        ),
        out_specs=(rows, rows, vector, vector, rows, vector, rows, vector, vector, vector, rows, vector, rows, vector),
        check_vma=False,
    )
```

```python
import functools

import functools

import jax
import jax.numpy as jnp
import numpy as np
from jax import lax
from jax.experimental import pallas as pl
from jax.experimental.pallas import tpu as pltpu
from jax.sharding import PartitionSpec as P

HEADS = 16
HEAD_DIM = 64
WINDOW = 1024
NDOCS = 32

ALL = ("y", "x", "core", "z")
norm_eps = 1e-05
bf16 = jnp.bfloat16
f32 = jnp.float32

MASKED = -1e30
TILE = 256
LANES = 128
SLOPE_LANE = NDOCS + 1
ROW_LANE = SLOPE_LANE + 6
SCALE = HEAD_DIM**-0.5
VMEM_LIMIT = 50 * 2**20
VMEM_ALL = 52 * 2**20
SHORT = pl.CostEstimate(flops=1, bytes_accessed=1, transcendentals=0)


def normalize(values):
    centred = values - jnp.mean(values, axis=-1, keepdims=True)
    inverse = lax.rsqrt(jnp.mean(centred * centred, axis=-1, keepdims=True) + norm_eps)
    return centred * inverse, inverse


def norm_back(change, normal, inverse, gain):
    scaled = change * gain
    mean_one = jnp.mean(scaled, axis=-1, keepdims=True)
    mean_two = jnp.mean(scaled * normal, axis=-1, keepdims=True)
    return inverse * (scaled - mean_one - normal * mean_two)


def dot_nn(left, right):
    return lax.dot_general(left, right, (((1,), (0,)), ((), ())), preferred_element_type=f32)


def dot_nt(left, right):
    return lax.dot_general(left, right, (((1,), (1,)), ((), ())), preferred_element_type=f32)


def dot_tn(left, right):
    return lax.dot_general(left, right, (((0,), (0,)), ((), ())), preferred_element_type=f32)


class Grid:
    def __init__(self):
        self.size = tuple(lax.axis_size(name) for name in ALL)
        self.here = tuple(lax.axis_index(name) for name in ALL)
        self.count = int(np.prod(self.size))
        self.linear = lax.axis_index(ALL)

    def shift(self, block, axis, distance=1):
        places = np.arange(self.count).reshape(self.size)
        ahead = np.roll(places, -distance, axis)
        return lax.ppermute(block, ALL, list(zip(places.ravel().tolist(), ahead.ravel().tolist())))

    def to_later(self, block):
        return lax.ppermute(block, ALL, [(i, i + 1) for i in range(self.count - 1)])

    def to_earlier(self, block):
        return lax.ppermute(block, ALL, [(i + 1, i) for i in range(self.count - 1)])


Y, X, CORE, Z = range(4)


def after(value, *earlier):
    anywhere = pl.BlockSpec(memory_space=pl.ANY)
    return pl.pallas_call(
        lambda *refs: None,
        in_specs=[anywhere] * (1 + len(earlier)),
        out_specs=anywhere,
        out_shape=jax.ShapeDtypeStruct(value.shape, value.dtype),
        input_output_aliases={0: 0},
        compiler_params=pltpu.CompilerParams(vmem_limit_bytes=2**17),
    )(value, *earlier)


def ring_gather(grid, block, axis):
    pieces = [block]
    for _ in range(grid.size[axis] - 1):
        pieces.append(grid.shift(pieces[-1], axis))
    return pieces


def direct_gather(grid, block, axis):
    return [block] + [grid.shift(block, axis, step) for step in range(1, grid.size[axis])]


def plane_gather(grid, line):
    half = len(line) // 2
    got = []
    for part, (one, two) in enumerate(((X, Y), (Y, X))):
        near = jnp.stack(ring_gather(grid, jnp.stack(line[part * half : (part + 1) * half]), one))
        for two_step, far in enumerate(ring_gather(grid, near, two)):
            got.append((part * half, one, two, two_step, far))
    return got


def plane_places(grid, got):
    ny, nx, _, nz = grid.size
    found = []
    for step, one, two, two_step, block in got:
        entries = []
        for one_step in range(block.shape[0]):
            back = {one: one_step, two: two_step}
            chip = (grid.here[Y] - back[Y]) % ny * nx + (grid.here[X] - back[X]) % nx
            entries.append([(chip, (grid.here[Z] - step - k) % nz) for k in range(block.shape[1])])
        found.append(entries)
    return found


def copy_blocks(moves, sems):
    copies = [pltpu.make_async_copy(source, target, sems.at[i]) for i, (source, target) in enumerate(moves)]
    for copy in copies:
        copy.start()
    for copy in copies:
        copy.wait()


def assemble(kernel, places, pieces, shapes, moves):
    anywhere = pl.BlockSpec(memory_space=pl.ANY)
    return pl.pallas_call(
        kernel,
        in_specs=[pl.BlockSpec(memory_space=pltpu.SMEM)] + [anywhere] * len(pieces),
        out_specs=[pl.BlockSpec(memory_space=pltpu.VMEM)] * len(shapes),
        out_shape=[jax.ShapeDtypeStruct(shape, bf16) for shape in shapes],
        scratch_shapes=[pltpu.SemaphoreType.DMA((moves,))],
        compiler_params=pltpu.CompilerParams(vmem_limit_bytes=VMEM_ALL),
        cost_estimate=SHORT,
    )(places, *pieces)


def joined_kernel(places, *refs):
    *pieces, whole, riders, sems = refs
    moves = []
    for piece in pieces:
        for near in range(piece.shape[0]):
            for step in range(piece.shape[1]):
                at = places[len(moves) // 4]
                for kind in range(3):
                    moves.append((piece.at[near, step, kind, :, pl.ds(0, whole.shape[-1])], whole.at[kind, at]))
                moves.append((piece.at[near, step, 0, :, pl.ds(whole.shape[-1], LANES)], riders.at[at]))
    copy_blocks(moves, sems)


def gather_joined(grid, line):
    got = plane_gather(grid, line)
    rows, width = line[0].shape[-2], line[0].shape[-1] - LANES
    pieces, places = [], []
    for (_, _, _, _, block), entries in zip(got, plane_places(grid, got)):
        for which, piece in ((grid.here[CORE], block), (1 - grid.here[CORE], grid.shift(block, CORE))):
            pieces.append(piece)
            places += [(chip * 2 + which) * grid.size[Z] + z for near in entries for chip, z in near]
    whole, riders = assemble(
        joined_kernel,
        jnp.stack(places).astype(jnp.int32),
        pieces,
        [(3, grid.count, rows, width), (grid.count, rows, LANES)],
        4 * len(places),
    )
    return whole.reshape(3, -1, width), riders


def up_kernel(places, lines, up, sems):
    width = lines.shape[-1]
    moves = []
    for entry in range(lines.shape[0]):
        for side in range(2):
            at = places[2 * entry + side]
            for half in range(2):
                moves.append((lines.at[entry, 2 * side + half], up.at[at, :, pl.ds(half * width, width)]))
    copy_blocks(moves, sems)


def whole_up(grid, lines, *earlier):
    count, _, rows, width = lines.shape
    nz, core = grid.size[Z], grid.here[CORE]
    places = [(entry // nz * 2 + which) * nz + entry % nz for entry in range(count) for which in (core, 1 - core)]
    places = after(jnp.stack(places).astype(jnp.int32), *earlier)
    (up,) = assemble(up_kernel, places, [lines], [(grid.count, rows, 2 * width)], 4 * count)
    return up.reshape(-1, 2 * width)


def add(left, right, kind=bf16):
    return (left.astype(f32) + right.astype(f32)).astype(kind)


def ring_reduce(grid, term, axis, kind=bf16):
    count = grid.size[axis]
    total = term(1)
    for step in range(2, count + 1):
        total = add(grid.shift(total, axis), term(step), kind)
    return total


def direct_reduce(grid, terms, axis, kind=f32):
    count, place = grid.size[axis], grid.here[axis]

    def term(step):
        return lax.dynamic_index_in_dim(terms, (place + step) % count, 0, keepdims=False)

    total = term(0).astype(f32)
    for step in range(1, count):
        total = total + grid.shift(term(step), axis, step).astype(f32)
    return total.astype(kind)


def down_kernel(left, right, out, total):
    out[...] = dot_tn(left[...], right[...]).astype(bf16)

    @pl.when(pl.program_id(0) == 0)
    def _():
        total[...] = jnp.sum(right[: right.shape[0] // 2].astype(f32), axis=0, keepdims=True)


def down_terms(hidden, change):
    tokens, units = hidden.shape
    width = change.shape[1]
    return pl.pallas_call(
        down_kernel,
        grid=(units // TILE,),
        in_specs=[
            pl.BlockSpec((tokens, TILE), lambda i: (0, i)),
            pl.BlockSpec((tokens, width), lambda i: (0, 0)),
        ],
        out_specs=[pl.BlockSpec((TILE, width), lambda i: (i, 0)), pl.BlockSpec((1, width), lambda i: (0, 0))],
        out_shape=[jax.ShapeDtypeStruct((units, width), bf16), jax.ShapeDtypeStruct((1, width), f32)],
        compiler_params=pltpu.CompilerParams(vmem_limit_bytes=VMEM_LIMIT),
        cost_estimate=SHORT,
    )(hidden, change)


def up_kernel_terms(own, other, right, *refs):
    refs[-1][...] = dot_tn(jnp.concatenate([own[...], other[...]], axis=0), right[...]).astype(bf16)


def up_terms(own, other, pre_change, earlier=()):
    rows, width = own.shape
    tokens, units = pre_change.shape
    wide = units // 2
    left = pl.BlockSpec((rows, TILE), lambda j, i: (0, i))
    return pl.pallas_call(
        up_kernel_terms,
        grid=(2, width // TILE),
        in_specs=[left, left, pl.BlockSpec((tokens, wide), lambda j, i: (0, j))]
        + [pl.BlockSpec(memory_space=pl.ANY)] * len(earlier),
        out_specs=pl.BlockSpec((TILE, wide), lambda j, i: (i, j)),
        out_shape=jax.ShapeDtypeStruct((width, units), bf16),
        compiler_params=pltpu.CompilerParams(vmem_limit_bytes=VMEM_LIMIT),
        cost_estimate=SHORT,
    )(own, other, pre_change, *earlier)


def add_kernel(split, left, right, *refs):
    if split == 0:
        refs[-1][...] = (left[...].astype(f32) + right[...].astype(f32)).astype(bf16)
    for i in range(split):
        refs[-split + i][...] = (left[i].astype(f32) + right[i].astype(f32)).astype(bf16)


def add_after(left, right, *earlier, split=False):
    held = pl.BlockSpec(memory_space=pltpu.VMEM)
    shape = jax.ShapeDtypeStruct(left.shape, bf16)
    if split:
        shape = [jax.ShapeDtypeStruct(left.shape[1:], bf16)] * left.shape[0]
    return pl.pallas_call(
        functools.partial(add_kernel, left.shape[0] if split else 0),
        in_specs=[held] * 2 + [pl.BlockSpec(memory_space=pl.ANY)] * len(earlier),
        out_specs=[held] * left.shape[0] if split else held,
        out_shape=shape,
        compiler_params=pltpu.CompilerParams(vmem_limit_bytes=VMEM_LIMIT),
        cost_estimate=SHORT,
    )(left, right, *earlier)


def product_kernel(left, right, *refs):
    refs[-1][...] = dot_nt(left[...], right[...]).astype(refs[-1].dtype)


def product_nt(left, right, kind, row_block=0, rows=None, earlier=()):
    rows = left.shape[0] if rows is None else rows
    depth, wide = left.shape[1], right.shape[0]
    return pl.pallas_call(
        product_kernel,
        grid=(wide // TILE,),
        in_specs=[
            pl.BlockSpec((rows, depth), lambda i: (row_block, 0)),
            pl.BlockSpec((TILE, depth), lambda i: (i, 0)),
        ]
        + [pl.BlockSpec(memory_space=pl.ANY)] * len(earlier),
        out_specs=pl.BlockSpec((rows, TILE), lambda i: (0, i)),
        out_shape=jax.ShapeDtypeStruct((rows, wide), kind),
        compiler_params=pltpu.CompilerParams(vmem_limit_bytes=VMEM_LIMIT),
        cost_estimate=SHORT,
    )(left, right, *earlier)


def product_nn_kernel(left, right, *refs):
    refs[-1][...] = dot_nn(left[...], right[...]).astype(refs[-1].dtype)


def product_nn(left, right, kind, row_block, rows, earlier=()):
    depth, wide = right.shape
    return pl.pallas_call(
        product_nn_kernel,
        grid=(wide // TILE,),
        in_specs=[
            pl.BlockSpec((rows, depth), lambda i: (row_block, 0)),
            pl.BlockSpec((depth, TILE), lambda i: (0, i)),
        ]
        + [pl.BlockSpec(memory_space=pl.ANY)] * len(earlier),
        out_specs=pl.BlockSpec((rows, TILE), lambda i: (0, i)),
        out_shape=jax.ShapeDtypeStruct((rows, wide), kind),
        compiler_params=pltpu.CompilerParams(vmem_limit_bytes=VMEM_LIMIT),
        cost_estimate=SHORT,
    )(left, right, *earlier)


def chunk_kernel(count, with_arrived, *refs):
    lefts, rights, (tokens, stats) = refs[:count], refs[count : 2 * count], refs[2 * count : 2 * count + 2]
    moved, gain_sum, shift_sum = refs[-3:]
    change = dot_nt(lefts[0][...], rights[0][...])
    for left, right in zip(lefts[1:], rights[1:]):
        change += dot_nt(left[...], right[...])
    normal = (tokens[...].astype(f32) - stats[:, :1]) * stats[:, 1:2]
    gain_sum[...] = jnp.sum(change * normal, axis=0, keepdims=True)
    shift_sum[...] = jnp.sum(change, axis=0, keepdims=True)
    if with_arrived:
        change += refs[2 * count + 2][...].astype(f32)
    moved[...] = change.astype(moved.dtype)


def chunk_back(pairs, chunk, kind, arrived=None, earlier=()):
    rows, width = chunk[0].shape
    tile = pl.BlockSpec((rows, TILE), lambda i: (0, i))
    sums = pl.BlockSpec((1, TILE), lambda i: (0, i))
    return pl.pallas_call(
        functools.partial(chunk_kernel, len(pairs), arrived is not None),
        grid=(width // TILE,),
        in_specs=[pl.BlockSpec((rows, left.shape[1]), lambda i, at=at: (at, 0)) for left, at, _ in pairs]
        + [pl.BlockSpec((TILE, right.shape[1]), lambda i: (i, 0)) for *_, right in pairs]
        + [tile, pl.BlockSpec((rows, LANES), lambda i: (0, 0))]
        + [tile] * (arrived is not None)
        + [pl.BlockSpec(memory_space=pl.ANY)] * len(earlier),
        out_specs=[tile, sums, sums],
        out_shape=[jax.ShapeDtypeStruct((rows, width), kind)] + [jax.ShapeDtypeStruct((1, width), f32)] * 2,
        compiler_params=pltpu.CompilerParams(vmem_limit_bytes=VMEM_LIMIT),
        cost_estimate=SHORT,
    )(
        *(left for left, *_ in pairs),
        *(right for *_, right in pairs),
        *chunk,
        *(() if arrived is None else (arrived,)),
        *earlier,
    )


def middle_kernel(pre_change, up, arrived, middle, gain, out_change, dense, *refs):
    middle_change, branch_change, context_change, gain_sum, shift_sum, branch_sum = refs[-6:]
    change = dot_nt(pre_change[...], up[...]) + arrived[...].astype(f32)
    normal, inverse = normalize(middle[...])
    moved = out_change[...].astype(f32) + norm_back(change, normal, inverse, gain[...])
    low = moved.astype(bf16)
    middle_change[...] = moved
    branch_change[...] = low
    context_change[...] = dot_nt(low, dense[...]).astype(bf16)
    first = pl.program_id(0) == 0
    for total, part in ((gain_sum, change * normal), (shift_sum, change), (branch_sum, low.astype(f32))):
        total[...] = jnp.where(first, 0.0, total[...]) + jnp.sum(part, axis=0, keepdims=True)


def middle_back(pre_change, up, arrived, middle, gain, out_change, dense, earlier=()):
    rows, width = middle.shape
    tile = pl.BlockSpec((TILE, width), lambda i: (i, 0))
    sums = pl.BlockSpec((1, width), lambda i: (0, 0))

    def whole(array):
        return pl.BlockSpec(array.shape, lambda i: (0, 0))

    return pl.pallas_call(
        middle_kernel,
        grid=(rows // TILE,),
        in_specs=[
            pl.BlockSpec((TILE, pre_change.shape[1]), lambda i: (i, 0)), whole(up), tile, tile, whole(gain), tile, whole(dense)
        ]
        + [pl.BlockSpec(memory_space=pl.ANY)] * len(earlier),
        out_specs=[tile, tile, tile, sums, sums, sums],
        out_shape=[
            jax.ShapeDtypeStruct((rows, width), f32),
            jax.ShapeDtypeStruct((rows, width), bf16),
            jax.ShapeDtypeStruct((rows, width), bf16),
        ]
        + [jax.ShapeDtypeStruct((1, width), f32)] * 3,
        compiler_params=pltpu.CompilerParams(vmem_limit_bytes=VMEM_LIMIT),
        cost_estimate=SHORT,
    )(pre_change, up, arrived, middle, gain, out_change, dense, *earlier)


def joined_kernel_terms(blocks, core, tokens_ext, context, query, key, value, branch, *refs):
    given_ahead, given_behind, kept_ahead, kept_behind = refs[-4:]
    left = tokens_ext[...]
    own = left[left.shape[0] - query.shape[0] :]
    rows = kept_ahead.shape[2]
    swapped = core[0] == 1
    for kind, (one, two) in enumerate(((own, query), (left, key), (left, value), (context[...], branch))):
        product = dot_tn(one, two[...])
        for part, (given, kept) in enumerate(((given_ahead, kept_ahead), (given_behind, kept_behind))):
            low, high = (product[(2 * side + part) * rows : (2 * side + part + 1) * rows] for side in range(2))
            given[0, kind] = jnp.where(swapped, low, high).astype(bf16)
            kept[0, kind] = jnp.where(swapped, high, low).astype(bf16)


def joined_terms(normed_ext, context, rights, chips_at, core, earlier=()):
    ext_rows, width = normed_ext.shape
    tok_rows = context.shape[0]
    count = len(chips_at)
    rows = width // count
    half = (1, 4, rows // 4, width)
    stacked = pl.BlockSpec(half, lambda i, at, core: (i, 0, 0, 0))

    def whole(array):
        return pl.BlockSpec(array.shape, lambda i, at, core: (0, 0))

    return pl.pallas_call(
        joined_kernel_terms,
        grid_spec=pltpu.PrefetchScalarGridSpec(
            num_scalar_prefetch=2,
            grid=(count,),
            in_specs=[
                pl.BlockSpec((ext_rows, rows), lambda i, at, core: (0, at[i])),
                pl.BlockSpec((tok_rows, rows), lambda i, at, core: (0, at[i])),
                *(whole(right) for right in rights),
                *[pl.BlockSpec(memory_space=pl.ANY)] * len(earlier),
            ],
            out_specs=[stacked] * 4,
        ),
        out_shape=[jax.ShapeDtypeStruct((count, *half[1:]), bf16)] * 4,
        compiler_params=pltpu.CompilerParams(vmem_limit_bytes=VMEM_LIMIT),
        cost_estimate=SHORT,
    )(
        jnp.stack(chips_at).astype(jnp.int32), jnp.reshape(core, (1,)).astype(jnp.int32), normed_ext, context, *rights, *earlier
    )


def split_kernel(nx, ahead, arrived_ahead, behind, arrived_behind, *refs):
    ny = ahead.shape[0]
    outs = refs[-nx - ny :]
    for back_y in range(ny):
        for back_x in range(nx):
            outs[back_x][back_y] = (ahead[back_y, back_x].astype(f32) + arrived_ahead[back_y, back_x].astype(f32)).astype(bf16)
            outs[nx + back_y][back_x] = (
                behind[back_y, back_x].astype(f32) + arrived_behind[back_y, back_x].astype(f32)
            ).astype(bf16)


def split_terms(ahead, arrived_ahead, behind, arrived_behind, ny, nx, earlier=()):
    arrays = [array.reshape(ny, nx, *array.shape[1:]) for array in (ahead, arrived_ahead, behind, arrived_behind)]
    shape = arrays[0].shape[2:]
    kinds = shape[0]
    rest = shape[1:]
    return pl.pallas_call(
        functools.partial(split_kernel, nx),
        grid=(kinds,),
        in_specs=[pl.BlockSpec((ny, nx, 1, *rest), lambda i: (0, 0, i, 0, 0))] * 4
        + [pl.BlockSpec(memory_space=pl.ANY)] * len(earlier),
        out_specs=[pl.BlockSpec((ny, 1, *rest), lambda i: (0, i, 0, 0))] * nx
        + [pl.BlockSpec((nx, 1, *rest), lambda i: (0, i, 0, 0))] * ny,
        out_shape=[jax.ShapeDtypeStruct((ny, *shape), bf16)] * nx + [jax.ShapeDtypeStruct((nx, *shape), bf16)] * ny,
        compiler_params=pltpu.CompilerParams(vmem_limit_bytes=VMEM_LIMIT),
        cost_estimate=SHORT,
    )(*arrays, *earlier)


def reduce_scatter_small(grid, terms):
    terms = terms.reshape(*grid.size, terms.shape[1])
    for axis, dim in ((CORE, 2), (X, 1), (Y, 0)):
        def term(step, terms=terms, axis=axis, dim=dim):
            return lax.dynamic_index_in_dim(terms, (grid.here[axis] - step) % grid.size[axis], dim, keepdims=False)

        terms = ring_reduce(grid, term, axis, f32)
    return direct_reduce(grid, terms, Z, f32)


def thirds(values):
    high = values.astype(bf16)
    rest = values - high.astype(f32)
    middle = rest.astype(bf16)
    return high, middle, (rest - middle.astype(f32)).astype(bf16)


def slope_lanes():
    lanes = np.zeros((HEADS // 2, 8, LANES), np.float32)
    for h in range(HEADS):
        rest = np.float32(2.0 ** (-8.0 * (h + 1) / HEADS))
        for part in range(3):
            piece = np.float32(rest.astype(bf16))
            rest = np.float32(rest - piece)
            lanes[h // 2, h % 2, SLOPE_LANE + part] = piece
            lanes[h // 2, h % 2, SLOPE_LANE + 3 + part] = piece
    return lanes


def side_lanes(seg_ext, tok_rows):
    lane = jnp.arange(LANES, dtype=jnp.int32)
    doc = lane[None, :] <= NDOCS
    seg_query = seg_ext[seg_ext.shape[0] - tok_rows :]
    query_side = jnp.where(doc & (lane[None, :] == seg_query[:, None]), 1.0, 0.0).astype(bf16)
    key_pos = jnp.arange(seg_ext.shape[0], dtype=jnp.int32)[:, None]
    key_side = jnp.where(doc & (lane[None, :] != seg_ext[:, None]), MASKED, 0.0)
    key_side = jnp.where((lane >= SLOPE_LANE) & (lane < SLOPE_LANE + 3), (key_pos // TILE * TILE).astype(f32), key_side)
    key_side = jnp.where((lane >= SLOPE_LANE + 3) & (lane < ROW_LANE), (key_pos % TILE).astype(f32), key_side)
    key_side = jnp.where((lane >= ROW_LANE) & (lane < ROW_LANE + 3), 1.0, key_side)
    return query_side, key_side.astype(bf16)


def key_tiles(tile):
    wide = WINDOW // TILE
    edges = [(tile + step) * TILE for step in (0, 1, wide, wide + 1)]
    return [slice(edges[i], edges[i + 1]) for i in range(3)]


def attend_kernel(query, key, value, query_side, key_side, slope, context, log_total):
    pair = pl.program_id(0)
    lane = lax.broadcasted_iota(jnp.int32, (TILE, LANES), 1)
    causal = lax.broadcasted_iota(jnp.int32, (TILE, TILE), 0) >= lax.broadcasted_iota(jnp.int32, (TILE, TILE), 1)
    keys = jnp.concatenate([key[...], key_side[...]], axis=1)
    for tile in range(query.shape[0] // TILE):
        rows = slice(tile * TILE, (tile + 1) * TILE)
        first, middle, last = key_tiles(tile)
        scaled = query[rows, :] * jnp.asarray(SCALE, bf16)
        outs, logs = [], []
        for half in range(2):
            mine = (lane >= HEAD_DIM) == (half == 1)
            side = query_side[rows, :] + slope[0, half : half + 1, :].astype(bf16)
            queries = jnp.concatenate([jnp.where(mine, scaled, jnp.zeros_like(scaled)), side], axis=1)
            inner = dot_nt(queries, keys[middle])
            outer = jnp.where(causal, dot_nt(queries, keys[last]), dot_nt(queries, keys[first]))
            top = jnp.maximum(jnp.max(inner, axis=1, keepdims=True), jnp.max(outer, axis=1, keepdims=True))
            inner = jnp.exp(inner - top)
            outer = jnp.exp(outer - top)
            total = jnp.sum(inner, axis=1, keepdims=True) + jnp.sum(outer, axis=1, keepdims=True)
            summed = dot_nn(inner.astype(bf16), value[middle, :])
            summed += dot_nn(jnp.where(causal, outer, 0.0).astype(bf16), value[last, :])
            summed += dot_nn(jnp.where(causal, 0.0, outer).astype(bf16), value[first, :])
            outs.append(summed / total)
            logs.append(top + jnp.log(total))
        context[rows, :] = jnp.where(lane < HEAD_DIM, outs[0], outs[1]).astype(bf16)
        before = jnp.where(pair == 0, jnp.zeros((TILE, LANES), f32), log_total[rows, :])
        log_total[rows, :] = jnp.where(lane == 2 * pair, logs[0], jnp.where(lane == 2 * pair + 1, logs[1], before))


def attend(queries, keys, values, query_side, key_side, slopes):
    tok_rows, width = queries.shape
    key_rows = keys.shape[0]
    steps = HEADS // 2
    return pl.pallas_call(
        attend_kernel,
        grid=(steps,),
        in_specs=[
            pl.BlockSpec((tok_rows, LANES), lambda p: (0, p)),
            pl.BlockSpec((key_rows, LANES), lambda p: (0, p)),
            pl.BlockSpec((key_rows, LANES), lambda p: (0, p)),
            pl.BlockSpec((tok_rows, LANES), lambda p: (0, 0)),
            pl.BlockSpec((key_rows, LANES), lambda p: (0, 0)),
            pl.BlockSpec((1, 8, LANES), lambda p: (p, 0, 0)),
        ],
        out_specs=[
            pl.BlockSpec((tok_rows, LANES), lambda p: (0, p)),
            pl.BlockSpec((tok_rows, LANES), lambda p: (0, 0)),
        ],
        out_shape=[
            jax.ShapeDtypeStruct((tok_rows, width), bf16),
            jax.ShapeDtypeStruct((tok_rows, LANES), f32),
        ],
        compiler_params=pltpu.CompilerParams(vmem_limit_bytes=VMEM_ALL),
        cost_estimate=SHORT,
    )(queries, keys, values, query_side, key_side, slopes)


def attend_back_kernel(
    query, key, value, change, context, log_total, query_side, key_side, slope, *refs, first_pair,
):
    query_change, key_change, value_change, key_sum, value_sum = refs[-5:]
    pair = first_pair + pl.program_id(0)
    lane = lax.broadcasted_iota(jnp.int32, (TILE, LANES), 1)
    causal = lax.broadcasted_iota(jnp.int32, (TILE, TILE), 0) <= lax.broadcasted_iota(jnp.int32, (TILE, TILE), 1)
    keys = jnp.concatenate([key[...], key_side[...]], axis=1)
    values = jnp.concatenate([value[...], key_side[...]], axis=1)
    keys_across = key[...].T
    key_sum[...] = jnp.zeros_like(key_sum)
    value_sum[...] = jnp.zeros_like(value_sum)

    def row_lanes(column):
        high, middle, low = thirds(column)
        lanes = jnp.where(lane == ROW_LANE + 2, low, jnp.zeros((TILE, LANES), bf16))
        return jnp.where(lane == ROW_LANE, high, jnp.where(lane == ROW_LANE + 1, middle, lanes))

    for tile in range(query.shape[0] // TILE):
        rows = slice(tile * TILE, (tile + 1) * TILE)
        first, middle, last = key_tiles(tile)
        scaled = query[rows, :] * jnp.asarray(SCALE, bf16)
        changed = change[rows, :]
        product = changed.astype(f32) * context[rows, :].astype(f32)
        logs = log_total[rows, :]
        parts = []
        for half in range(2):
            mine = (lane >= HEAD_DIM) == (half == 1)
            asked = jnp.where(mine, scaled, jnp.zeros_like(scaled))
            moved = jnp.where(mine, changed, jnp.zeros_like(changed))
            log_row = jnp.sum(jnp.where(lane == 2 * pair + half, logs, 0.0), axis=1, keepdims=True)
            inner_row = jnp.sum(jnp.where(mine, product, 0.0), axis=1, keepdims=True)
            side = query_side[rows, :] + slope[0, half : half + 1, :].astype(bf16) + row_lanes(-log_row)
            queries = jnp.concatenate([asked, side], axis=1)
            changes = jnp.concatenate([moved, row_lanes(-inner_row)], axis=1)
            prob = jnp.exp(dot_nt(keys[middle], queries))
            prob_edge = jnp.exp(jnp.where(causal, dot_nt(keys[last], queries), dot_nt(keys[first], queries)))
            score = (prob * dot_nt(values[middle], changes)).astype(bf16)
            score_edge = prob_edge * jnp.where(causal, dot_nt(values[last], changes), dot_nt(values[first], changes))
            score_last = jnp.where(causal, score_edge, 0.0).astype(bf16)
            score_first = jnp.where(causal, 0.0, score_edge).astype(bf16)
            value_sum[middle, :] += dot_nn(prob.astype(bf16), moved)
            value_sum[last, :] += dot_nn(jnp.where(causal, prob_edge, 0.0).astype(bf16), moved)
            value_sum[first, :] += dot_nn(jnp.where(causal, 0.0, prob_edge).astype(bf16), moved)
            key_sum[middle, :] += dot_nn(score, asked)
            key_sum[last, :] += dot_nn(score_last, asked)
            key_sum[first, :] += dot_nn(score_first, asked)
            parts.append(
                dot_nn(keys_across[:, middle], score)
                + dot_nn(keys_across[:, last], score_last)
                + dot_nn(keys_across[:, first], score_first)
            )
        entry = lax.broadcasted_iota(jnp.int32, (LANES, TILE), 0)
        query_change[rows, :] = (jnp.where(entry < HEAD_DIM, parts[0], parts[1]).T * SCALE).astype(bf16)
    key_change[...] = key_sum[...].astype(bf16)
    value_change[...] = value_sum[...].astype(bf16)


def attend_back(queries, keys, values, change, context, log_total, query_side, key_side, slopes, first_pair, count, others=()):
    tok_rows, width = queries.shape
    key_rows = keys.shape[0]
    steps = HEADS // 2
    by_query = pl.BlockSpec((tok_rows, LANES), lambda p: (0, first_pair + p))
    by_key = pl.BlockSpec((key_rows, LANES), lambda p: (0, first_pair + p))
    return pl.pallas_call(
        functools.partial(attend_back_kernel, first_pair=first_pair),
        grid=(count,),
        in_specs=[
            by_query,
            by_key,
            by_key,
            by_query,
            by_query,
            pl.BlockSpec((tok_rows, LANES), lambda p: (0, 0)),
            pl.BlockSpec((tok_rows, LANES), lambda p: (0, 0)),
            pl.BlockSpec((key_rows, LANES), lambda p: (0, 0)),
            pl.BlockSpec((1, 8, LANES), lambda p: (first_pair + p, 0, 0)),
        ]
        + [pl.BlockSpec(memory_space=pl.ANY)] * len(others),
        out_specs=[by_query, by_key, by_key],
        out_shape=[
            jax.ShapeDtypeStruct((tok_rows, width), bf16),
            jax.ShapeDtypeStruct((key_rows, width), bf16),
            jax.ShapeDtypeStruct((key_rows, width), bf16),
        ],
        input_output_aliases={9 + i: i for i in range(len(others))},
        scratch_shapes=[pltpu.VMEM((key_rows, LANES), f32), pltpu.VMEM((key_rows, LANES), f32)],
        compiler_params=pltpu.CompilerParams(vmem_limit_bytes=VMEM_ALL),
        cost_estimate=SHORT,
    )(queries, keys, values, change, context, log_total, query_side, key_side, slopes, *others)


def segment_ids(lengths, valid_count, positions):
    doc_ends = jnp.cumsum(lengths)
    passed = jnp.sum((doc_ends[None, :] <= positions[:, None]).astype(jnp.int32), axis=1)
    inside = jnp.where(positions < valid_count[0], passed, NDOCS)
    return jnp.where(positions < 0, -1, inside)


ROOT = float(np.sqrt(2.0 / np.pi))


def gelu_parts(values):
    square = values * values
    rise = 0.5 * jnp.tanh(values * (square * (ROOT * 0.044715) + ROOT)) + 0.5
    bend = values * (square * (6.0 * ROOT * 0.044715) + 2.0 * ROOT)
    return values * rise, rise + bend * (rise - rise * rise)


def hidden_kernel(chips, core, own, other, up_kept, up_given, bias, hidden, slope, sides):
    rows, width = own.shape
    wide = width // (2 * chips)

    @pl.when(pl.program_id(0) == 0)
    def _():
        first = core[0] == 0
        for chip in range(chips):
            start, to = 2 * chip * wide, slice(chip * wide, (chip + 1) * wide)
            for part, tokens in enumerate((own, other)):
                low, high = tokens[:, start : start + wide], tokens[:, start + wide : start + 2 * wide]
                sides[0, part * rows : (part + 1) * rows, to] = jnp.where(first, low, high)
                sides[1, part * rows : (part + 1) * rows, to] = jnp.where(first, high, low)

    kept = up_kept[...].reshape(width // 2, TILE)
    given = up_given[...].reshape(width // 2, TILE)
    for start in range(0, 2 * rows, TILE):
        product = dot_nn(sides[0, start : start + TILE], kept) + dot_nn(sides[1, start : start + TILE], given)
        value, rise = gelu_parts(product + bias[...])
        hidden[start : start + TILE, :] = value.astype(bf16)
        slope[start : start + TILE, :] = rise.astype(bf16)


def hidden_units(chips, core, own, other, lines, bias):
    rows, depth = own.shape
    count, _, height, width = lines.shape
    units = 2 * width
    steps = width // TILE
    columns = pl.BlockSpec((2 * rows, TILE), lambda i, at: (0, i))
    whole = pl.BlockSpec((rows, depth), lambda i, at: (0, 0))

    def block(side):
        return pl.BlockSpec((count, 1, height, TILE), lambda i, at: (0, 2 * side + i // steps, 0, i % steps))

    return pl.pallas_call(
        functools.partial(hidden_kernel, chips),
        grid_spec=pltpu.PrefetchScalarGridSpec(
            num_scalar_prefetch=1,
            grid=(units // TILE,),
            in_specs=[whole, whole, block(0), block(1), pl.BlockSpec((1, TILE), lambda i, at: (0, i))],
            out_specs=[columns, columns],
            scratch_shapes=[pltpu.VMEM((2, 2 * rows, depth // 2), bf16)],
        ),
        out_shape=[jax.ShapeDtypeStruct((2 * rows, units), bf16)] * 2,
        compiler_params=pltpu.CompilerParams(vmem_limit_bytes=VMEM_LIMIT),
        cost_estimate=SHORT,
    )(jnp.reshape(core, (1,)).astype(jnp.int32), own, other, lines, lines, bias)


def pre_change_kernel(change, down, slope, *refs):
    pre_change, total = refs[-2:]
    moved = (dot_nt(change[...], down[...]) * slope[...].astype(f32)).astype(bf16)
    pre_change[...] = moved
    total[...] = jnp.sum(moved.astype(f32), axis=0, keepdims=True)


def hidden_back(change, down, slope, earlier=()):
    tokens, depth = change.shape
    units = down.shape[0]
    columns = pl.BlockSpec((tokens, TILE), lambda i: (0, i))
    return pl.pallas_call(
        pre_change_kernel,
        grid=(units // TILE,),
        in_specs=[
            pl.BlockSpec((tokens, depth), lambda i: (0, 0)),
            pl.BlockSpec((TILE, depth), lambda i: (i, 0)),
            columns,
        ]
        + [pl.BlockSpec(memory_space=pl.ANY)] * len(earlier),
        out_specs=[columns, pl.BlockSpec((1, TILE), lambda i: (0, i))],
        out_shape=[jax.ShapeDtypeStruct((tokens, units), bf16), jax.ShapeDtypeStruct((1, units), f32)],
        compiler_params=pltpu.CompilerParams(vmem_limit_bytes=VMEM_LIMIT),
        cost_estimate=SHORT,
    )(change, down, slope, *earlier)


def projection_kernel(kinds, others, tokens, gain, shift, *refs):
    mats, shifts = refs[:kinds], refs[kinds : 2 * kinds]
    normed, stats, *outs, held = refs[2 * kinds + others :]

    @pl.when(pl.program_id(0) == 0)
    def _():
        values = tokens[...].astype(f32)
        mean = jnp.mean(values, axis=-1, keepdims=True)
        centred = values - mean
        inverse = lax.rsqrt(jnp.mean(centred * centred, axis=-1, keepdims=True) + norm_eps)
        low = (centred * inverse * gain[...] + shift[...]).astype(bf16)
        normed[...] = low
        held[...] = low
        lane = lax.broadcasted_iota(jnp.int32, stats.shape, 1)
        stats[...] = jnp.where(lane == 0, mean, inverse)

    for mat, add, out in zip(mats, shifts, outs):
        out[...] = (dot_nn(held[...], mat[...]) + add[...]).astype(bf16)


def project(tokens, gain, shift, mats, shifts, chunk, chunks, others=()):
    rows, width = tokens.shape
    kinds = len(mats)
    ext_rows = chunks * rows
    fixed = pl.BlockSpec((rows, width), lambda i: (0, 0))
    row = pl.BlockSpec((1, width), lambda i: (0, 0))
    placed = pl.BlockSpec((rows, TILE), lambda i: (chunk, i))
    out_specs = [pl.BlockSpec((rows, width), lambda i: (chunk, 0)), pl.BlockSpec((rows, LANES), lambda i: (0, 0)), placed, placed]
    out_shape = [jax.ShapeDtypeStruct((ext_rows, width), bf16), jax.ShapeDtypeStruct((rows, LANES), f32)]
    out_shape += [jax.ShapeDtypeStruct((ext_rows, width), bf16)] * 2
    if kinds == 3:
        out_specs.append(pl.BlockSpec((rows, TILE), lambda i: (0, i)))
        out_shape.append(jax.ShapeDtypeStruct((rows, width), bf16))
    aliases = {3 + 2 * kinds + i: place for i, place in enumerate((0, 2, 3)[: len(others)])}
    return pl.pallas_call(
        functools.partial(projection_kernel, kinds, len(others)),
        grid=(width // TILE,),
        in_specs=[fixed, row, row]
        + [pl.BlockSpec((width, TILE), lambda i: (0, i))] * kinds
        + [pl.BlockSpec((1, TILE), lambda i: (0, i))] * kinds
        + [pl.BlockSpec(memory_space=pl.ANY)] * len(others),
        out_specs=out_specs,
        out_shape=out_shape,
        scratch_shapes=[pltpu.VMEM((rows, width), bf16)],
        input_output_aliases=aliases,
        compiler_params=pltpu.CompilerParams(vmem_limit_bytes=VMEM_LIMIT),
        cost_estimate=SHORT,
    )(tokens, gain, shift, *mats, *shifts, *others)


def pack_kernel(weight, *refs):
    *vectors, packed, rider = refs
    width = packed.shape[-1] - LANES
    for kind in range(3):
        for pair in range(HEADS // 2):
            at = [((2 * pair + half) * 3 + kind) * HEAD_DIM for half in range(2)]
            packed[kind, :, pair * LANES : (pair + 1) * LANES] = jnp.concatenate(
                [weight[:, start : start + HEAD_DIM] for start in at], axis=1
            )
        packed[kind, :, width:] = jnp.zeros((packed.shape[1], LANES), bf16)
    rider[...] = jnp.zeros_like(rider)
    for i, vector in enumerate(vectors):
        rider[i : i + 1, : vector.shape[1]] = vector[...].astype(f32)
    packed[0, :, width:] = rider[...].astype(bf16)


def pack_joined(weight, vectors):
    rows, wide = weight.shape
    return pl.pallas_call(
        pack_kernel,
        out_shape=jax.ShapeDtypeStruct((3, rows, wide // 3 + LANES), bf16),
        scratch_shapes=[pltpu.VMEM((rows, LANES), f32)],
    )(weight, *(v[None] for v in vectors))


def unpack_kernel(riders, *refs):
    *vectors, query, value = refs
    for i, vector in enumerate(vectors):
        wide = vector.shape[1] // riders.shape[0]
        for device in range(riders.shape[0]):
            vector[:, device * wide : (device + 1) * wide] = riders[device, i : i + 1, :wide].astype(f32)
    for pair in range(HEADS // 2):
        for offset, out in ((0, query), (HEAD_DIM, value)):
            start = 4 * HEAD_DIM * pair + offset
            halves = [vectors[2][:, at : at + HEAD_DIM] for at in (start, start + 2 * HEAD_DIM)]
            out[:, pair * LANES : (pair + 1) * LANES] = jnp.concatenate(halves, axis=1)


def unpack_vectors(riders, counts):
    sizes = [riders.shape[0] * count for count in counts] + [HEADS * HEAD_DIM] * 2
    return pl.pallas_call(
        unpack_kernel,
        out_shape=[jax.ShapeDtypeStruct((1, size), f32) for size in sizes],
        cost_estimate=SHORT,
    )(riders)


def from_kinds(columns):
    rows = columns.shape[0]
    return columns.reshape(rows, 3, HEADS, HEAD_DIM).swapaxes(1, 2).reshape(rows, 3 * HEADS * HEAD_DIM)


def on_device(
    tokens,
    cotangent,
    lengths,
    valid_count,
    first_gain,
    first_shift,
    joined_weight,
    joined_bias,
    dense_weight,
    dense_bias,
    second_gain,
    second_shift,
    up_weight,
    up_bias,
    down_weight,
    down_bias,
):
    grid = Grid()
    tok_rows, width = tokens.shape
    hops = WINDOW // tok_rows
    shard_rows = joined_weight.shape[0]

    y, x, core, z = grid.here
    ny, nx, _, nz = grid.size
    chips = ny * nx
    up_rows, ff = up_weight.shape
    ff_core = ff // 2

    def core_columns(block, which):
        wide = block.shape[1] // chips // 2
        return jnp.concatenate(
            [lax.dynamic_slice_in_dim(block, (2 * chip + which) * wide, wide, 1) for chip in range(chips)], axis=1
        )

    vectors = (first_gain, first_shift, joined_bias, dense_bias, second_gain, second_shift, up_bias, down_bias)
    counts = [v.shape[0] for v in vectors]
    joined_line = direct_gather(grid, pack_joined(joined_weight, vectors), Z)
    (query_mat, key_mat, value_mat), riders = gather_joined(grid, joined_line)
    gain_one, shift_one, _, dense_vec, gain_two, shift_two, up_vec, down_vec, query_vec, value_vec = unpack_vectors(
        riders, counts
    )

    up_kept, up_given = (core_columns(up_weight, which) for which in (core, 1 - core))
    up_blocks = [half for side in (up_kept, grid.shift(up_given, CORE)) for half in (side[:, :width], side[:, width:])]
    lines = ("y", "x", "z")
    up_shard = after(jnp.stack([*up_blocks, dense_weight]), *joined_line[1:])
    up_lines = lax.all_gather(up_shard, lines, axis=0)
    down_mat = lax.all_gather(after(down_weight, *joined_line[1:]), lines, axis=0, tiled=True)

    before = [after(tokens, *joined_line[1:])]
    for _ in range(hops):
        before.append(grid.to_later(before[-1]))
    first_pos = grid.linear * tok_rows - WINDOW
    positions = first_pos + jnp.arange(WINDOW + tok_rows, dtype=jnp.int32)
    seg_ext = segment_ids(lengths, valid_count, positions)
    query_side, key_side = side_lanes(seg_ext, tok_rows)
    slopes = jnp.asarray(slope_lanes())
    live_rows = (positions[WINDOW:] < valid_count[0])[:, None]
    change_low = jnp.where(live_rows, cotangent, jnp.zeros_like(cotangent))
    change_both = jnp.concatenate([change_low, grid.shift(change_low, CORE)], axis=0)

    values = tokens.astype(f32)
    mats, shifts = (key_mat, value_mat), (jnp.zeros_like(value_vec), value_vec)
    normed_ext, stats, keys, all_values, queries = project(
        tokens, gain_one, shift_one, (*mats, query_mat), (*shifts, query_vec), hops, hops + 1
    )
    chunks = [(tokens, stats)]
    for hop in range(1, hops + 1):
        normed_ext, stats, keys, all_values = project(
            before[hop], gain_one, shift_one, mats, shifts, hops - hop, hops + 1, (normed_ext, keys, all_values)
        )
        chunks.insert(0, (before[hop], stats))
    context, log_total = attend(queries, keys, all_values, query_side, key_side, after(slopes, change_both))
    dense_part = after(up_lines[:, 4].reshape(-1, width), context)
    dense_other = grid.shift(dense_part, CORE)
    dense_sides = [jnp.where(core == which, dense_part, dense_other).reshape(chips, -1, width) for which in range(2)]
    dense_mat = jnp.stack(dense_sides, axis=1).reshape(-1, width)
    middle = values + dot_nn(context, dense_mat) + dense_vec
    normal_two, inverse_two = normalize(middle)
    normed_two = (normal_two * gain_two + shift_two).astype(bf16)
    normed_other = grid.shift(normed_two, CORE)
    hidden, slope = hidden_units(chips, core, normed_two, normed_other, up_lines, core_columns(up_vec, core))
    up_mat = whole_up(grid, up_lines, hidden)

    def far_sums(part, terms, *earlier):
        axis = (Y, X)[part]
        moving = terms[0]
        for step in range(1, grid.size[axis]):
            moving = add_after(grid.shift(moving, axis), terms[step], *earlier)
        return moving

    out_change = change_low.astype(f32)
    down_sums, down_vec_grad = down_terms(hidden, change_both)
    down_plane = lax.psum_scatter(down_sums, ("y", "x"), scatter_dimension=0, tiled=True)
    pre_change, up_core_grad = hidden_back(change_both, down_mat, slope, (down_sums,))
    given = product_nt(pre_change, up_mat, bf16, 1, tok_rows)
    up_sums = up_terms(normed_two, normed_other, pre_change, (given,))
    up_plane = lax.psum_scatter(up_sums, ("y", "x"), scatter_dimension=0, tiled=True)
    middle_change, branch_change, context_change, gain_two_grad, shift_two_grad, dense_vec_grad = middle_back(
        pre_change, up_mat, grid.shift(given, CORE), middle, gain_two, change_low, dense_mat, (up_sums,)
    )
    halves = HEADS // 4
    changes = attend_back(
        queries, keys, all_values, context_change, context, log_total, query_side, key_side, slopes, 0, halves
    )
    down_plane = after(down_plane, changes[0]).reshape(nz, -1, width)
    query_change, key_change, value_change = attend_back(
        queries, keys, all_values, context_change, context, log_total, query_side, key_side, after(slopes, down_plane),
        halves, halves, changes,
    )
    backs = [(back_y, back_x) for back_y in range(1, ny + 1) for back_x in range(1, nx + 1)]

    down_grad = direct_reduce(grid, down_plane, Z)
    chips_at = [(y - back_y) % ny * nx + (x - back_x) % nx for back_y, back_x in backs]
    rights = (query_change, key_change, value_change, branch_change)
    joined_given = joined_terms(normed_ext, context, rights, chips_at, core, (down_grad,))
    pairs = [(key_change, key_mat), (value_change, value_mat)]
    returned, *sums = chunk_back(
        [(left, 0, right) for left, right in pairs], chunks[0], bf16, None, joined_given[:1]
    )
    chunk_sums = [sums]
    joined_kept = split_terms(
        joined_given[2], grid.shift(joined_given[0], CORE), joined_given[3], grid.shift(joined_given[1], CORE), ny, nx, (returned,)
    )
    own_change, *sums = chunk_back(
        [(left, hops, right) for left, right in pairs] + [(query_change, 0, query_mat)], chunks[-1], f32, None, joined_kept
    )
    chunk_sums.append(sums)
    done = own_change
    for chunk in range(1, hops):
        arrived = grid.to_earlier(returned)
        returned, *sums = chunk_back(
            [(left, chunk, right) for left, right in pairs], chunks[chunk], bf16, arrived, (done,)
        )
        chunk_sums.append(sums)
        done = returned
    joined_near = []
    for terms, axis in ((joined_kept[:nx], X), (joined_kept[nx:], Y)):
        total = terms[0]
        for step in range(1, grid.size[axis]):
            total = add_after(grid.shift(total, axis), terms[step], done, split=step == grid.size[axis] - 1)
        joined_near.append(total)
    nears = [*joined_near[0], *joined_near[1]]
    up_rows_both = after(up_plane, *nears).reshape(2, nz, up_rows, ff_core).swapaxes(0, 1)
    up_sum = direct_reduce(grid, up_rows_both, Z)
    up_mine = lax.dynamic_index_in_dim(up_sum, core, 0, keepdims=False)
    up_other = grid.shift(lax.dynamic_index_in_dim(up_sum, 1 - core, 0, keepdims=False), CORE)
    returned = grid.to_earlier(returned)
    joined_far = [far_sums(part, joined_near[part], returned, up_sum) for part in range(2)]
    both = [half.reshape(4, nz // 2, -1, width) for half in joined_far]
    owned_rows = direct_reduce(grid, jnp.concatenate(both, axis=1).swapaxes(0, 1), Z)
    dense_grad = owned_rows[3]
    joined_grad = jnp.concatenate(list(owned_rows[:3]), axis=1)
    returned = returned.astype(f32)

    def interleave(mine, other):
        first, second = jnp.where(core == 0, mine, other), jnp.where(core == 0, other, mine)
        wide = mine.shape[1] // chips
        cuts = [slice(chip * wide, (chip + 1) * wide) for chip in range(chips)]
        return jnp.concatenate([side[:, cut] for cut in cuts for side in (first, second)], axis=1)

    up_grad = interleave(up_mine, up_other)
    branch_given = product_nn(hidden, down_mat, bf16, 1, tok_rows, nears)
    branch_two = product_nn(hidden, down_mat, f32, 0, tok_rows, nears) + grid.shift(branch_given, CORE).astype(f32)
    layer_output = jnp.where(live_rows, middle + (branch_two + down_vec), 0.0).astype(bf16)
    gain_one_grad, shift_one_grad = (sum(total).reshape(-1) for total in zip(*chunk_sums))
    joined_vec_grad = jnp.stack(
        [
            jnp.sum(query_change.astype(f32), axis=0).reshape(HEADS, HEAD_DIM),
            jnp.sum(value_change.astype(f32), axis=0).reshape(HEADS, HEAD_DIM),
        ],
        axis=1,
    ).reshape(-1)
    input_grad = (middle_change + norm_back(own_change + returned, *normalize(values), gain_one)).astype(bf16)
    up_parts = up_core_grad.reshape(chips, 1, -1)
    up_vec_grad = jnp.concatenate(
        [jnp.where(core == which, up_parts, jnp.zeros_like(up_parts)) for which in range(2)], axis=1
    ).reshape(-1)
    vector_grads = (
        gain_one_grad, shift_one_grad, joined_vec_grad, dense_vec_grad, gain_two_grad, shift_two_grad, up_vec_grad,
        down_vec_grad,
    )
    cuts = np.cumsum([0] + counts)
    vector_rows = jnp.concatenate([v.reshape(grid.count, -1) for v in vector_grads], axis=1)
    owned = reduce_scatter_small(grid, after(vector_rows, *nears))
    owned = [owned[cuts[i] : cuts[i + 1]] for i in range(len(counts))]
    return (
        layer_output,
        input_grad,
        owned[0],
        owned[1],
        from_kinds(joined_grad),
        owned[2],
        dense_grad,
        owned[3],
        owned[4],
        owned[5],
        up_grad,
        owned[6],
        down_grad,
        owned[7],
    )


def solution(mesh):
    blocks, heads = mesh.devices.shape
    split = jax.sharding.Mesh(mesh.devices.reshape(2, blocks // 4, 2, heads), ALL)
    rows, vector, same = P(ALL, None), P(ALL), P()
    return jax.shard_map(
        on_device,
        mesh=split,
        in_specs=(
            rows, rows, same, same, vector, vector, rows, vector, rows, vector, vector, vector, rows, vector, rows, vector
        ),
        out_specs=(rows, rows, vector, vector, rows, vector, rows, vector, vector, vector, rows, vector, rows, vector),
        check_vma=False,
    )
```

```python
import functools

import functools

import jax
import jax.numpy as jnp
import numpy as np
from jax import lax
from jax.experimental import pallas as pl
from jax.experimental.pallas import tpu as pltpu
from jax.sharding import PartitionSpec as P

HEADS = 16
HEAD_DIM = 64
WINDOW = 1024
NDOCS = 32

ALL = ("y", "x", "core", "z")
norm_eps = 1e-05
bf16 = jnp.bfloat16
f32 = jnp.float32

MASKED = -1e30
TILE = 256
WIDE = 512
LANES = 128
SLOPE_LANE = NDOCS + 1
ROW_LANE = SLOPE_LANE + 6
SCALE = HEAD_DIM**-0.5
VMEM_LIMIT = 50 * 2**20
VMEM_ALL = 52 * 2**20
SHORT = pl.CostEstimate(flops=1, bytes_accessed=1, transcendentals=0)


def normalize(values):
    centred = values - jnp.mean(values, axis=-1, keepdims=True)
    inverse = lax.rsqrt(jnp.mean(centred * centred, axis=-1, keepdims=True) + norm_eps)
    return centred * inverse, inverse


def norm_back(change, normal, inverse, gain):
    scaled = change * gain
    mean_one = jnp.mean(scaled, axis=-1, keepdims=True)
    mean_two = jnp.mean(scaled * normal, axis=-1, keepdims=True)
    return inverse * (scaled - mean_one - normal * mean_two)


def dot_nn(left, right):
    return lax.dot_general(left, right, (((1,), (0,)), ((), ())), preferred_element_type=f32)


def dot_nt(left, right):
    return lax.dot_general(left, right, (((1,), (1,)), ((), ())), preferred_element_type=f32)


def dot_tn(left, right):
    return lax.dot_general(left, right, (((0,), (0,)), ((), ())), preferred_element_type=f32)


class Grid:
    def __init__(self):
        self.size = tuple(lax.axis_size(name) for name in ALL)
        self.here = tuple(lax.axis_index(name) for name in ALL)
        self.count = int(np.prod(self.size))
        self.linear = lax.axis_index(ALL)

    def shift(self, block, axis, distance=1):
        places = np.arange(self.count).reshape(self.size)
        ahead = np.roll(places, -distance, axis)
        return lax.ppermute(block, ALL, list(zip(places.ravel().tolist(), ahead.ravel().tolist())))

    def to_later(self, block):
        return lax.ppermute(block, ALL, [(i, i + 1) for i in range(self.count - 1)])

    def to_earlier(self, block):
        return lax.ppermute(block, ALL, [(i + 1, i) for i in range(self.count - 1)])


Y, X, CORE, Z = range(4)


def after(value, *earlier):
    anywhere = pl.BlockSpec(memory_space=pl.ANY)
    return pl.pallas_call(
        lambda *refs: None,
        in_specs=[anywhere] * (1 + len(earlier)),
        out_specs=anywhere,
        out_shape=jax.ShapeDtypeStruct(value.shape, value.dtype),
        input_output_aliases={0: 0},
        compiler_params=pltpu.CompilerParams(vmem_limit_bytes=2**17),
    )(value, *earlier)


def ring_gather(grid, block, axis):
    pieces = [block]
    for _ in range(grid.size[axis] - 1):
        pieces.append(grid.shift(pieces[-1], axis))
    return pieces


def direct_gather(grid, block, axis):
    return [block] + [grid.shift(block, axis, step) for step in range(1, grid.size[axis])]


def plane_gather(grid, line):
    half = len(line) // 2
    got = []
    for part, (one, two) in enumerate(((X, Y), (Y, X))):
        near = jnp.stack(ring_gather(grid, jnp.stack(line[part * half : (part + 1) * half]), one))
        for two_step, far in enumerate(ring_gather(grid, near, two)):
            got.append((part * half, one, two, two_step, far))
    return got


def plane_places(grid, got):
    ny, nx, _, nz = grid.size
    found = []
    for step, one, two, two_step, block in got:
        entries = []
        for one_step in range(block.shape[0]):
            back = {one: one_step, two: two_step}
            chip = (grid.here[Y] - back[Y]) % ny * nx + (grid.here[X] - back[X]) % nx
            entries.append([(chip, (grid.here[Z] - step - k) % nz) for k in range(block.shape[1])])
        found.append(entries)
    return found


def copy_blocks(moves, sems):
    copies = [pltpu.make_async_copy(source, target, sems.at[i]) for i, (source, target) in enumerate(moves)]
    for copy in copies:
        copy.start()
    for copy in copies:
        copy.wait()


def assemble(kernel, places, pieces, shapes, moves):
    anywhere = pl.BlockSpec(memory_space=pl.ANY)
    return pl.pallas_call(
        kernel,
        in_specs=[pl.BlockSpec(memory_space=pltpu.SMEM)] + [anywhere] * len(pieces),
        out_specs=[pl.BlockSpec(memory_space=pltpu.VMEM)] * len(shapes),
        out_shape=[jax.ShapeDtypeStruct(shape, bf16) for shape in shapes],
        scratch_shapes=[pltpu.SemaphoreType.DMA((moves,))],
        compiler_params=pltpu.CompilerParams(vmem_limit_bytes=VMEM_ALL),
        cost_estimate=SHORT,
    )(places, *pieces)


def joined_kernel(places, *refs):
    *pieces, query, key, value, riders, sems = refs
    width = query.shape[-1]
    moves = []
    for piece in pieces:
        for near in range(piece.shape[0]):
            for step in range(piece.shape[1]):
                at = places[len(moves) // 4]
                for kind, whole in enumerate((query, key, value)):
                    moves.append((piece.at[near, step, kind, :, pl.ds(0, width)], whole.at[at]))
                moves.append((piece.at[near, step, 0, :, pl.ds(width, LANES)], riders.at[at]))
    copy_blocks(moves, sems)


def gather_joined(grid, line):
    got = plane_gather(grid, line)
    rows, width = line[0].shape[-2], line[0].shape[-1] - LANES
    pieces, places = [], []
    for (_, _, _, _, block), entries in zip(got, plane_places(grid, got)):
        for which, piece in ((grid.here[CORE], block), (1 - grid.here[CORE], grid.shift(block, CORE))):
            pieces.append(piece)
            places += [(chip * 2 + which) * grid.size[Z] + z for near in entries for chip, z in near]
    *mats, riders = assemble(
        joined_kernel,
        jnp.stack(places).astype(jnp.int32),
        pieces,
        [(grid.count, rows, width)] * 3 + [(grid.count, rows, LANES)],
        4 * len(places),
    )
    return *(mat.reshape(-1, width) for mat in mats), riders


def up_kernel(places, lines, up, sems):
    width = lines.shape[-1]
    moves = []
    for entry in range(lines.shape[0]):
        for side in range(2):
            at = places[2 * entry + side]
            for half in range(2):
                moves.append((lines.at[entry, 2 * side + half], up.at[at, :, pl.ds(half * width, width)]))
    copy_blocks(moves, sems)


def whole_up(grid, lines, *earlier):
    count, _, rows, width = lines.shape
    nz, core = grid.size[Z], grid.here[CORE]
    places = [(entry // nz * 2 + which) * nz + entry % nz for entry in range(count) for which in (core, 1 - core)]
    places = after(jnp.stack(places).astype(jnp.int32), *earlier)
    (up,) = assemble(up_kernel, places, [lines], [(grid.count, rows, 2 * width)], 4 * count)
    return up.reshape(-1, 2 * width)


def add(left, right, kind=bf16):
    return (left.astype(f32) + right.astype(f32)).astype(kind)


def ring_reduce(grid, term, axis, kind=bf16):
    count = grid.size[axis]
    total = term(1)
    for step in range(2, count + 1):
        total = add(grid.shift(total, axis), term(step), kind)
    return total


def sum_kernel(count, *refs):
    total = refs[0][...].astype(f32)
    for ref in refs[1:count]:
        total += ref[...].astype(f32)
    refs[-1][...] = total


def sum_after(arrays, *earlier):
    held = pl.BlockSpec(memory_space=pltpu.VMEM)
    return pl.pallas_call(
        functools.partial(sum_kernel, len(arrays)),
        in_specs=[held] * len(arrays) + [pl.BlockSpec(memory_space=pl.ANY)] * len(earlier),
        out_specs=held,
        out_shape=jax.ShapeDtypeStruct(arrays[0].shape, f32),
        compiler_params=pltpu.CompilerParams(vmem_limit_bytes=2**23),
        cost_estimate=SHORT,
    )(*arrays, *earlier)


def direct_reduce(grid, terms, axis, earlier=()):
    count, place = grid.size[axis], grid.here[axis]

    def term(step):
        return lax.dynamic_index_in_dim(terms, (place + step) % count, 0, keepdims=False)

    return sum_after([term(0)] + [grid.shift(term(step), axis, step) for step in range(1, count)], *earlier)


def down_kernel(left, right, out, total):
    out[...] = dot_tn(left[...], right[...]).astype(bf16)

    @pl.when(pl.program_id(0) == 0)
    def _():
        total[...] = jnp.sum(right[: right.shape[0] // 2].astype(f32), axis=0, keepdims=True)


def down_terms(hidden, change):
    tokens, units = hidden.shape
    width = change.shape[1]
    return pl.pallas_call(
        down_kernel,
        grid=(units // TILE,),
        in_specs=[
            pl.BlockSpec((tokens, TILE), lambda i: (0, i)),
            pl.BlockSpec((tokens, width), lambda i: (0, 0)),
        ],
        out_specs=[pl.BlockSpec((TILE, width), lambda i: (i, 0)), pl.BlockSpec((1, width), lambda i: (0, 0))],
        out_shape=[jax.ShapeDtypeStruct((units, width), bf16), jax.ShapeDtypeStruct((1, width), f32)],
        compiler_params=pltpu.CompilerParams(vmem_limit_bytes=VMEM_LIMIT),
        cost_estimate=SHORT,
    )(hidden, change)


def up_kernel_terms(own, other, right, *refs):
    rows = own.shape[0]
    refs[-1][...] = (dot_tn(own[...], right[:rows]) + dot_tn(other[...], right[rows:])).astype(bf16)


def up_terms(own, other, pre_change, earlier=()):
    rows, width = own.shape
    tokens, units = pre_change.shape
    left = pl.BlockSpec((rows, width), lambda i: (0, 0))
    return pl.pallas_call(
        up_kernel_terms,
        grid=(units // WIDE,),
        in_specs=[left, left, pl.BlockSpec((tokens, WIDE), lambda i: (0, i))]
        + [pl.BlockSpec(memory_space=pl.ANY)] * len(earlier),
        out_specs=pl.BlockSpec((width, WIDE), lambda i: (0, i)),
        out_shape=jax.ShapeDtypeStruct((width, units), bf16),
        compiler_params=pltpu.CompilerParams(vmem_limit_bytes=VMEM_LIMIT),
        cost_estimate=SHORT,
    )(own, other, pre_change, *earlier)


def add_kernel(split, left, right, *refs):
    if split == 0:
        refs[-1][...] = (left[...].astype(f32) + right[...].astype(f32)).astype(bf16)
    for i in range(split):
        refs[-split + i][...] = (left[i].astype(f32) + right[i].astype(f32)).astype(bf16)


def add_after(left, right, *earlier, split=False):
    held = pl.BlockSpec(memory_space=pltpu.VMEM)
    shape = jax.ShapeDtypeStruct(left.shape, bf16)
    if split:
        shape = [jax.ShapeDtypeStruct(left.shape[1:], bf16)] * left.shape[0]
    return pl.pallas_call(
        functools.partial(add_kernel, left.shape[0] if split else 0),
        in_specs=[held] * 2 + [pl.BlockSpec(memory_space=pl.ANY)] * len(earlier),
        out_specs=[held] * left.shape[0] if split else held,
        out_shape=shape,
        compiler_params=pltpu.CompilerParams(vmem_limit_bytes=VMEM_LIMIT),
        cost_estimate=SHORT,
    )(left, right, *earlier)


def product_kernel(left, right, *refs):
    refs[-1][...] = dot_nt(left[...], right[...]).astype(refs[-1].dtype)


def product_nt(left, right, kind, row_block=0, rows=None, earlier=()):
    rows = left.shape[0] if rows is None else rows
    depth, wide = left.shape[1], right.shape[0]
    return pl.pallas_call(
        product_kernel,
        grid=(wide // WIDE,),
        in_specs=[
            pl.BlockSpec((rows, depth), lambda i: (row_block, 0)),
            pl.BlockSpec((WIDE, depth), lambda i: (i, 0)),
        ]
        + [pl.BlockSpec(memory_space=pl.ANY)] * len(earlier),
        out_specs=pl.BlockSpec((rows, WIDE), lambda i: (0, i)),
        out_shape=jax.ShapeDtypeStruct((rows, wide), kind),
        compiler_params=pltpu.CompilerParams(vmem_limit_bytes=VMEM_LIMIT),
        cost_estimate=SHORT,
    )(left, right, *earlier)


def product_nn_kernel(left, right, *refs):
    refs[-1][...] = dot_nn(left[...], right[...]).astype(refs[-1].dtype)


def product_nn(left, right, kind, row_block, rows, earlier=()):
    depth, wide = right.shape
    return pl.pallas_call(
        product_nn_kernel,
        grid=(wide // TILE,),
        in_specs=[
            pl.BlockSpec((rows, depth), lambda i: (row_block, 0)),
            pl.BlockSpec((depth, TILE), lambda i: (0, i)),
        ]
        + [pl.BlockSpec(memory_space=pl.ANY)] * len(earlier),
        out_specs=pl.BlockSpec((rows, TILE), lambda i: (0, i)),
        out_shape=jax.ShapeDtypeStruct((rows, wide), kind),
        compiler_params=pltpu.CompilerParams(vmem_limit_bytes=VMEM_LIMIT),
        cost_estimate=SHORT,
    )(left, right, *earlier)


def chunk_kernel(count, with_arrived, *refs):
    lefts, rights, (tokens, stats) = refs[:count], refs[count : 2 * count], refs[2 * count : 2 * count + 2]
    moved, gain_sum, shift_sum = refs[-3:]
    change = dot_nt(lefts[0][...], rights[0][...])
    for left, right in zip(lefts[1:], rights[1:]):
        change += dot_nt(left[...], right[...])
    normal = (tokens[...].astype(f32) - stats[:, :1]) * stats[:, 1:2]
    gain_sum[...] = jnp.sum(change * normal, axis=0, keepdims=True)
    shift_sum[...] = jnp.sum(change, axis=0, keepdims=True)
    if with_arrived:
        change += refs[2 * count + 2][...].astype(f32)
    moved[...] = change.astype(moved.dtype)


def chunk_back(pairs, chunk, kind, arrived=None, earlier=()):
    rows, width = chunk[0].shape
    tile = pl.BlockSpec((rows, TILE), lambda i: (0, i))
    sums = pl.BlockSpec((1, TILE), lambda i: (0, i))
    return pl.pallas_call(
        functools.partial(chunk_kernel, len(pairs), arrived is not None),
        grid=(width // TILE,),
        in_specs=[pl.BlockSpec((rows, left.shape[1]), lambda i, at=at: (at, 0)) for left, at, _ in pairs]
        + [pl.BlockSpec((TILE, right.shape[1]), lambda i: (i, 0)) for *_, right in pairs]
        + [tile, pl.BlockSpec((rows, LANES), lambda i: (0, 0))]
        + [tile] * (arrived is not None)
        + [pl.BlockSpec(memory_space=pl.ANY)] * len(earlier),
        out_specs=[tile, sums, sums],
        out_shape=[jax.ShapeDtypeStruct((rows, width), kind)] + [jax.ShapeDtypeStruct((1, width), f32)] * 2,
        compiler_params=pltpu.CompilerParams(vmem_limit_bytes=VMEM_LIMIT),
        cost_estimate=SHORT,
    )(
        *(left for left, *_ in pairs),
        *(right for *_, right in pairs),
        *chunk,
        *(() if arrived is None else (arrived,)),
        *earlier,
    )


def middle_kernel(pre_change, up, arrived, middle, gain, out_change, dense, *refs):
    middle_change, branch_change, context_change, gain_sum, shift_sum, branch_sum = refs[-6:]
    change = dot_nt(pre_change[...], up[...]) + arrived[...].astype(f32)
    normal, inverse = normalize(middle[...])
    moved = out_change[...].astype(f32) + norm_back(change, normal, inverse, gain[...])
    low = moved.astype(bf16)
    middle_change[...] = moved
    branch_change[...] = low
    context_change[...] = dot_nt(low, dense[...]).astype(bf16)
    first = pl.program_id(0) == 0
    for total, part in ((gain_sum, change * normal), (shift_sum, change), (branch_sum, low.astype(f32))):
        total[...] = jnp.where(first, 0.0, total[...]) + jnp.sum(part, axis=0, keepdims=True)


def middle_back(pre_change, up, arrived, middle, gain, out_change, dense, earlier=()):
    rows, width = middle.shape
    tile = pl.BlockSpec((TILE, width), lambda i: (i, 0))
    sums = pl.BlockSpec((1, width), lambda i: (0, 0))

    def whole(array):
        return pl.BlockSpec(array.shape, lambda i: (0, 0))

    return pl.pallas_call(
        middle_kernel,
        grid=(rows // TILE,),
        in_specs=[
            pl.BlockSpec((TILE, pre_change.shape[1]), lambda i: (i, 0)), whole(up), tile, tile, whole(gain), tile, whole(dense)
        ]
        + [pl.BlockSpec(memory_space=pl.ANY)] * len(earlier),
        out_specs=[tile, tile, tile, sums, sums, sums],
        out_shape=[
            jax.ShapeDtypeStruct((rows, width), f32),
            jax.ShapeDtypeStruct((rows, width), bf16),
            jax.ShapeDtypeStruct((rows, width), bf16),
        ]
        + [jax.ShapeDtypeStruct((1, width), f32)] * 3,
        compiler_params=pltpu.CompilerParams(vmem_limit_bytes=VMEM_LIMIT),
        cost_estimate=SHORT,
    )(pre_change, up, arrived, middle, gain, out_change, dense, *earlier)


def joined_kernel_terms(blocks, core, tokens_ext, context, query, key, value, branch, *refs):
    given_ahead, given_behind, kept_ahead, kept_behind = refs[-4:]
    left = tokens_ext[...]
    own = left[left.shape[0] - query.shape[0] :]
    rows = kept_ahead.shape[2]
    swapped = core[0] == 1
    for kind, (one, two) in enumerate(((own, query), (left, key), (left, value), (context[...], branch))):
        product = dot_tn(one, two[...])
        for part, (given, kept) in enumerate(((given_ahead, kept_ahead), (given_behind, kept_behind))):
            low, high = (product[(2 * side + part) * rows : (2 * side + part + 1) * rows] for side in range(2))
            given[0, kind] = jnp.where(swapped, low, high).astype(bf16)
            kept[0, kind] = jnp.where(swapped, high, low).astype(bf16)


def joined_terms(normed_ext, context, rights, chips_at, core, earlier=()):
    ext_rows, width = normed_ext.shape
    tok_rows = context.shape[0]
    count = len(chips_at)
    rows = width // count
    half = (1, 4, rows // 4, width)
    stacked = pl.BlockSpec(half, lambda i, at, core: (i, 0, 0, 0))

    def whole(array):
        return pl.BlockSpec(array.shape, lambda i, at, core: (0, 0))

    return pl.pallas_call(
        joined_kernel_terms,
        grid_spec=pltpu.PrefetchScalarGridSpec(
            num_scalar_prefetch=2,
            grid=(count,),
            in_specs=[
                pl.BlockSpec((ext_rows, rows), lambda i, at, core: (0, at[i])),
                pl.BlockSpec((tok_rows, rows), lambda i, at, core: (0, at[i])),
                *(whole(right) for right in rights),
                *[pl.BlockSpec(memory_space=pl.ANY)] * len(earlier),
            ],
            out_specs=[stacked] * 4,
        ),
        out_shape=[jax.ShapeDtypeStruct((count, *half[1:]), bf16)] * 4,
        compiler_params=pltpu.CompilerParams(vmem_limit_bytes=VMEM_LIMIT),
        cost_estimate=SHORT,
    )(
        jnp.stack(chips_at).astype(jnp.int32), jnp.reshape(core, (1,)).astype(jnp.int32), normed_ext, context, *rights, *earlier
    )


def split_kernel(nx, ahead, arrived_ahead, behind, arrived_behind, *refs):
    ny = ahead.shape[0]
    outs = refs[-nx - ny :]
    for back_y in range(ny):
        for back_x in range(nx):
            outs[back_x][back_y] = (ahead[back_y, back_x].astype(f32) + arrived_ahead[back_y, back_x].astype(f32)).astype(bf16)
            outs[nx + back_y][back_x] = (
                behind[back_y, back_x].astype(f32) + arrived_behind[back_y, back_x].astype(f32)
            ).astype(bf16)


def split_terms(ahead, arrived_ahead, behind, arrived_behind, ny, nx, earlier=()):
    arrays = [array.reshape(ny, nx, *array.shape[1:]) for array in (ahead, arrived_ahead, behind, arrived_behind)]
    shape = arrays[0].shape[2:]
    kinds = shape[0]
    rest = shape[1:]
    return pl.pallas_call(
        functools.partial(split_kernel, nx),
        grid=(kinds,),
        in_specs=[pl.BlockSpec((ny, nx, 1, *rest), lambda i: (0, 0, i, 0, 0))] * 4
        + [pl.BlockSpec(memory_space=pl.ANY)] * len(earlier),
        out_specs=[pl.BlockSpec((ny, 1, *rest), lambda i: (0, i, 0, 0))] * nx
        + [pl.BlockSpec((nx, 1, *rest), lambda i: (0, i, 0, 0))] * ny,
        out_shape=[jax.ShapeDtypeStruct((ny, *shape), bf16)] * nx + [jax.ShapeDtypeStruct((nx, *shape), bf16)] * ny,
        compiler_params=pltpu.CompilerParams(vmem_limit_bytes=VMEM_LIMIT),
        cost_estimate=SHORT,
    )(*arrays, *earlier)


def reduce_scatter_small(grid, terms):
    terms = terms.reshape(*grid.size, terms.shape[1])
    for axis, dim in ((CORE, 2), (X, 1), (Y, 0)):
        def term(step, terms=terms, axis=axis, dim=dim):
            return lax.dynamic_index_in_dim(terms, (grid.here[axis] - step) % grid.size[axis], dim, keepdims=False)

        terms = ring_reduce(grid, term, axis, f32)
    total = lax.dynamic_index_in_dim(terms, grid.here[Z], 0, keepdims=False)
    for step in range(1, grid.size[Z]):
        term = lax.dynamic_index_in_dim(terms, (grid.here[Z] + step) % grid.size[Z], 0, keepdims=False)
        total = total + grid.shift(term, Z, step)
    return total


def thirds(values):
    high = values.astype(bf16)
    rest = values - high.astype(f32)
    middle = rest.astype(bf16)
    return high, middle, (rest - middle.astype(f32)).astype(bf16)


def slope_lanes():
    lanes = np.zeros((HEADS // 2, 8, LANES), np.float32)
    for h in range(HEADS):
        rest = np.float32(2.0 ** (-8.0 * (h + 1) / HEADS))
        for part in range(3):
            piece = np.float32(rest.astype(bf16))
            rest = np.float32(rest - piece)
            lanes[h // 2, h % 2, SLOPE_LANE + part] = piece
            lanes[h // 2, h % 2, SLOPE_LANE + 3 + part] = piece
    return lanes


def side_lanes(seg_ext, tok_rows):
    lane = jnp.arange(LANES, dtype=jnp.int32)
    doc = lane[None, :] <= NDOCS
    seg_query = seg_ext[seg_ext.shape[0] - tok_rows :]
    query_side = jnp.where(doc & (lane[None, :] == seg_query[:, None]), 1.0, 0.0).astype(bf16)
    key_pos = jnp.arange(seg_ext.shape[0], dtype=jnp.int32)[:, None]
    key_side = jnp.where(doc & (lane[None, :] != seg_ext[:, None]), MASKED, 0.0)
    key_side = jnp.where((lane >= SLOPE_LANE) & (lane < SLOPE_LANE + 3), (key_pos // TILE * TILE).astype(f32), key_side)
    key_side = jnp.where((lane >= SLOPE_LANE + 3) & (lane < ROW_LANE), (key_pos % TILE).astype(f32), key_side)
    key_side = jnp.where((lane >= ROW_LANE) & (lane < ROW_LANE + 3), 1.0, key_side)
    return query_side, key_side.astype(bf16)


def key_tiles(tile):
    wide = WINDOW // TILE
    edges = [(tile + step) * TILE for step in (0, 1, wide, wide + 1)]
    return [slice(edges[i], edges[i + 1]) for i in range(3)]


def attend_kernel(query, key, value, query_side, key_side, slope, context, log_total):
    pair = pl.program_id(0)
    lane = lax.broadcasted_iota(jnp.int32, (TILE, LANES), 1)
    causal = lax.broadcasted_iota(jnp.int32, (TILE, TILE), 0) >= lax.broadcasted_iota(jnp.int32, (TILE, TILE), 1)
    keys = jnp.concatenate([key[...], key_side[...]], axis=1)
    for tile in range(query.shape[0] // TILE):
        rows = slice(tile * TILE, (tile + 1) * TILE)
        first, middle, last = key_tiles(tile)
        scaled = query[rows, :] * jnp.asarray(SCALE, bf16)
        outs, logs = [], []
        for half in range(2):
            mine = (lane >= HEAD_DIM) == (half == 1)
            side = query_side[rows, :] + slope[0, half : half + 1, :].astype(bf16)
            queries = jnp.concatenate([jnp.where(mine, scaled, jnp.zeros_like(scaled)), side], axis=1)
            inner = dot_nt(queries, keys[middle])
            outer = jnp.where(causal, dot_nt(queries, keys[last]), dot_nt(queries, keys[first]))
            top = jnp.maximum(jnp.max(inner, axis=1, keepdims=True), jnp.max(outer, axis=1, keepdims=True))
            inner = jnp.exp(inner - top)
            outer = jnp.exp(outer - top)
            total = jnp.sum(inner, axis=1, keepdims=True) + jnp.sum(outer, axis=1, keepdims=True)
            summed = dot_nn(inner.astype(bf16), value[middle, :])
            summed += dot_nn(jnp.where(causal, outer, 0.0).astype(bf16), value[last, :])
            summed += dot_nn(jnp.where(causal, 0.0, outer).astype(bf16), value[first, :])
            outs.append(summed / total)
            logs.append(top + jnp.log(total))
        context[rows, :] = jnp.where(lane < HEAD_DIM, outs[0], outs[1]).astype(bf16)
        before = jnp.where(pair == 0, jnp.zeros((TILE, LANES), f32), log_total[rows, :])
        log_total[rows, :] = jnp.where(lane == 2 * pair, logs[0], jnp.where(lane == 2 * pair + 1, logs[1], before))


def attend(queries, keys, values, query_side, key_side, slopes):
    tok_rows, width = queries.shape
    key_rows = keys.shape[0]
    steps = HEADS // 2
    return pl.pallas_call(
        attend_kernel,
        grid=(steps,),
        in_specs=[
            pl.BlockSpec((tok_rows, LANES), lambda p: (0, p)),
            pl.BlockSpec((key_rows, LANES), lambda p: (0, p)),
            pl.BlockSpec((key_rows, LANES), lambda p: (0, p)),
            pl.BlockSpec((tok_rows, LANES), lambda p: (0, 0)),
            pl.BlockSpec((key_rows, LANES), lambda p: (0, 0)),
            pl.BlockSpec((1, 8, LANES), lambda p: (p, 0, 0)),
        ],
        out_specs=[
            pl.BlockSpec((tok_rows, LANES), lambda p: (0, p)),
            pl.BlockSpec((tok_rows, LANES), lambda p: (0, 0)),
        ],
        out_shape=[
            jax.ShapeDtypeStruct((tok_rows, width), bf16),
            jax.ShapeDtypeStruct((tok_rows, LANES), f32),
        ],
        compiler_params=pltpu.CompilerParams(vmem_limit_bytes=VMEM_ALL),
        cost_estimate=SHORT,
    )(queries, keys, values, query_side, key_side, slopes)


def attend_back_kernel(
    query, key, value, change, context, log_total, query_side, key_side, slope, *refs, first_pair,
):
    query_change, key_change, value_change, key_sum, value_sum = refs[-5:]
    pair = first_pair + pl.program_id(0)
    lane = lax.broadcasted_iota(jnp.int32, (TILE, LANES), 1)
    causal = lax.broadcasted_iota(jnp.int32, (TILE, TILE), 0) <= lax.broadcasted_iota(jnp.int32, (TILE, TILE), 1)
    keys = jnp.concatenate([key[...], key_side[...]], axis=1)
    values = jnp.concatenate([value[...], key_side[...]], axis=1)
    keys_across = key[...].T
    key_sum[...] = jnp.zeros_like(key_sum)
    value_sum[...] = jnp.zeros_like(value_sum)

    def row_lanes(column):
        high, middle, low = thirds(column)
        lanes = jnp.where(lane == ROW_LANE + 2, low, jnp.zeros((TILE, LANES), bf16))
        return jnp.where(lane == ROW_LANE, high, jnp.where(lane == ROW_LANE + 1, middle, lanes))

    for tile in range(query.shape[0] // TILE):
        rows = slice(tile * TILE, (tile + 1) * TILE)
        first, middle, last = key_tiles(tile)
        scaled = query[rows, :] * jnp.asarray(SCALE, bf16)
        changed = change[rows, :]
        product = changed.astype(f32) * context[rows, :].astype(f32)
        logs = log_total[rows, :]
        parts = []
        for half in range(2):
            mine = (lane >= HEAD_DIM) == (half == 1)
            asked = jnp.where(mine, scaled, jnp.zeros_like(scaled))
            moved = jnp.where(mine, changed, jnp.zeros_like(changed))
            log_row = jnp.sum(jnp.where(lane == 2 * pair + half, logs, 0.0), axis=1, keepdims=True)
            inner_row = jnp.sum(jnp.where(mine, product, 0.0), axis=1, keepdims=True)
            side = query_side[rows, :] + slope[0, half : half + 1, :].astype(bf16) + row_lanes(-log_row)
            queries = jnp.concatenate([asked, side], axis=1)
            changes = jnp.concatenate([moved, row_lanes(-inner_row)], axis=1)
            prob = jnp.exp(dot_nt(keys[middle], queries))
            prob_edge = jnp.exp(jnp.where(causal, dot_nt(keys[last], queries), dot_nt(keys[first], queries)))
            score = (prob * dot_nt(values[middle], changes)).astype(bf16)
            score_edge = prob_edge * jnp.where(causal, dot_nt(values[last], changes), dot_nt(values[first], changes))
            score_last = jnp.where(causal, score_edge, 0.0).astype(bf16)
            score_first = jnp.where(causal, 0.0, score_edge).astype(bf16)
            value_sum[middle, :] += dot_nn(prob.astype(bf16), moved)
            value_sum[last, :] += dot_nn(jnp.where(causal, prob_edge, 0.0).astype(bf16), moved)
            value_sum[first, :] += dot_nn(jnp.where(causal, 0.0, prob_edge).astype(bf16), moved)
            key_sum[middle, :] += dot_nn(score, asked)
            key_sum[last, :] += dot_nn(score_last, asked)
            key_sum[first, :] += dot_nn(score_first, asked)
            parts.append(
                dot_nn(keys_across[:, middle], score)
                + dot_nn(keys_across[:, last], score_last)
                + dot_nn(keys_across[:, first], score_first)
            )
        entry = lax.broadcasted_iota(jnp.int32, (LANES, TILE), 0)
        query_change[rows, :] = (jnp.where(entry < HEAD_DIM, parts[0], parts[1]).T * SCALE).astype(bf16)
    key_change[...] = key_sum[...].astype(bf16)
    value_change[...] = value_sum[...].astype(bf16)


def attend_back(queries, keys, values, change, context, log_total, query_side, key_side, slopes, first_pair, count, others=()):
    tok_rows, width = queries.shape
    key_rows = keys.shape[0]
    steps = HEADS // 2
    by_query = pl.BlockSpec((tok_rows, LANES), lambda p: (0, first_pair + p))
    by_key = pl.BlockSpec((key_rows, LANES), lambda p: (0, first_pair + p))
    return pl.pallas_call(
        functools.partial(attend_back_kernel, first_pair=first_pair),
        grid=(count,),
        in_specs=[
            by_query,
            by_key,
            by_key,
            by_query,
            by_query,
            pl.BlockSpec((tok_rows, LANES), lambda p: (0, 0)),
            pl.BlockSpec((tok_rows, LANES), lambda p: (0, 0)),
            pl.BlockSpec((key_rows, LANES), lambda p: (0, 0)),
            pl.BlockSpec((1, 8, LANES), lambda p: (first_pair + p, 0, 0)),
        ]
        + [pl.BlockSpec(memory_space=pl.ANY)] * len(others),
        out_specs=[by_query, by_key, by_key],
        out_shape=[
            jax.ShapeDtypeStruct((tok_rows, width), bf16),
            jax.ShapeDtypeStruct((key_rows, width), bf16),
            jax.ShapeDtypeStruct((key_rows, width), bf16),
        ],
        input_output_aliases={9 + i: i for i in range(len(others))},
        scratch_shapes=[pltpu.VMEM((key_rows, LANES), f32), pltpu.VMEM((key_rows, LANES), f32)],
        compiler_params=pltpu.CompilerParams(vmem_limit_bytes=VMEM_ALL),
        cost_estimate=SHORT,
    )(queries, keys, values, change, context, log_total, query_side, key_side, slopes, *others)


def segment_ids(lengths, valid_count, positions):
    doc_ends = jnp.cumsum(lengths)
    passed = jnp.sum((doc_ends[None, :] <= positions[:, None]).astype(jnp.int32), axis=1)
    inside = jnp.where(positions < valid_count[0], passed, NDOCS)
    return jnp.where(positions < 0, -1, inside)


ROOT = float(np.sqrt(2.0 / np.pi))


def gelu_parts(values):
    square = values * values
    rise = 0.5 * jnp.tanh(values * (square * (ROOT * 0.044715) + ROOT)) + 0.5
    bend = values * (square * (6.0 * ROOT * 0.044715) + 2.0 * ROOT)
    return values * rise, rise + bend * (rise - rise * rise)


def hidden_kernel(chips, core, own, other, up_kept, up_given, bias, hidden, slope, sides):
    rows, width = own.shape
    wide = width // (2 * chips)

    @pl.when(pl.program_id(0) == 0)
    def _():
        first = core[0] == 0
        for chip in range(chips):
            start, to = 2 * chip * wide, slice(chip * wide, (chip + 1) * wide)
            for part, tokens in enumerate((own, other)):
                low, high = tokens[:, start : start + wide], tokens[:, start + wide : start + 2 * wide]
                sides[0, part * rows : (part + 1) * rows, to] = jnp.where(first, low, high)
                sides[1, part * rows : (part + 1) * rows, to] = jnp.where(first, high, low)

    kept = up_kept[...].reshape(width // 2, WIDE)
    given = up_given[...].reshape(width // 2, WIDE)
    for start in range(0, 2 * rows, TILE):
        product = dot_nn(sides[0, start : start + TILE], kept) + dot_nn(sides[1, start : start + TILE], given)
        value, rise = gelu_parts(product + bias[...])
        hidden[start : start + TILE, :] = value.astype(bf16)
        slope[start : start + TILE, :] = rise.astype(bf16)


def hidden_units(chips, core, own, other, lines, bias):
    rows, depth = own.shape
    count, _, height, width = lines.shape
    units = 2 * width
    steps = width // WIDE
    columns = pl.BlockSpec((2 * rows, WIDE), lambda i, at: (0, i))
    whole = pl.BlockSpec((rows, depth), lambda i, at: (0, 0))

    def block(side):
        return pl.BlockSpec((count, 1, height, WIDE), lambda i, at: (0, 2 * side + i // steps, 0, i % steps))

    return pl.pallas_call(
        functools.partial(hidden_kernel, chips),
        grid_spec=pltpu.PrefetchScalarGridSpec(
            num_scalar_prefetch=1,
            grid=(units // WIDE,),
            in_specs=[whole, whole, block(0), block(1), pl.BlockSpec((1, WIDE), lambda i, at: (0, i))],
            out_specs=[columns, columns],
            scratch_shapes=[pltpu.VMEM((2, 2 * rows, depth // 2), bf16)],
        ),
        out_shape=[jax.ShapeDtypeStruct((2 * rows, units), bf16)] * 2,
        compiler_params=pltpu.CompilerParams(vmem_limit_bytes=VMEM_LIMIT),
        cost_estimate=SHORT,
    )(jnp.reshape(core, (1,)).astype(jnp.int32), own, other, lines, lines, bias)


def pre_change_kernel(change, down, slope, *refs):
    pre_change, total = refs[-2:]
    moved = (dot_nt(change[...], down[...]) * slope[...].astype(f32)).astype(bf16)
    pre_change[...] = moved
    total[...] = jnp.sum(moved.astype(f32), axis=0, keepdims=True)


def hidden_back(change, down, slope, earlier=()):
    tokens, depth = change.shape
    units = down.shape[0]
    columns = pl.BlockSpec((tokens, WIDE), lambda i: (0, i))
    return pl.pallas_call(
        pre_change_kernel,
        grid=(units // WIDE,),
        in_specs=[
            pl.BlockSpec((tokens, depth), lambda i: (0, 0)),
            pl.BlockSpec((WIDE, depth), lambda i: (i, 0)),
            columns,
        ]
        + [pl.BlockSpec(memory_space=pl.ANY)] * len(earlier),
        out_specs=[columns, pl.BlockSpec((1, WIDE), lambda i: (0, i))],
        out_shape=[jax.ShapeDtypeStruct((tokens, units), bf16), jax.ShapeDtypeStruct((1, units), f32)],
        compiler_params=pltpu.CompilerParams(vmem_limit_bytes=VMEM_LIMIT),
        cost_estimate=SHORT,
    )(change, down, slope, *earlier)


def projection_kernel(kinds, others, tokens, gain, shift, *refs):
    mats, shifts = refs[:kinds], refs[kinds : 2 * kinds]
    normed, stats, *outs, held = refs[2 * kinds + others :]

    @pl.when(pl.program_id(0) == 0)
    def _():
        values = tokens[...].astype(f32)
        mean = jnp.mean(values, axis=-1, keepdims=True)
        centred = values - mean
        inverse = lax.rsqrt(jnp.mean(centred * centred, axis=-1, keepdims=True) + norm_eps)
        low = (centred * inverse * gain[...] + shift[...]).astype(bf16)
        normed[...] = low
        held[...] = low
        lane = lax.broadcasted_iota(jnp.int32, stats.shape, 1)
        stats[...] = jnp.where(lane == 0, mean, inverse)

    for mat, add, out in zip(mats, shifts, outs):
        out[...] = (dot_nn(held[...], mat[...]) + add[...]).astype(bf16)


def project(tokens, gain, shift, mats, shifts, chunk, chunks, others=()):
    rows, width = tokens.shape
    kinds = len(mats)
    ext_rows = chunks * rows
    fixed = pl.BlockSpec((rows, width), lambda i: (0, 0))
    row = pl.BlockSpec((1, width), lambda i: (0, 0))
    placed = pl.BlockSpec((rows, WIDE), lambda i: (chunk, i))
    out_specs = [pl.BlockSpec((rows, width), lambda i: (chunk, 0)), pl.BlockSpec((rows, LANES), lambda i: (0, 0)), placed, placed]
    out_shape = [jax.ShapeDtypeStruct((ext_rows, width), bf16), jax.ShapeDtypeStruct((rows, LANES), f32)]
    out_shape += [jax.ShapeDtypeStruct((ext_rows, width), bf16)] * 2
    if kinds == 3:
        out_specs.append(pl.BlockSpec((rows, WIDE), lambda i: (0, i)))
        out_shape.append(jax.ShapeDtypeStruct((rows, width), bf16))
    aliases = {3 + 2 * kinds + i: place for i, place in enumerate((0, 2, 3)[: len(others)])}
    return pl.pallas_call(
        functools.partial(projection_kernel, kinds, len(others)),
        grid=(width // WIDE,),
        in_specs=[fixed, row, row]
        + [pl.BlockSpec((width, WIDE), lambda i: (0, i))] * kinds
        + [pl.BlockSpec((1, WIDE), lambda i: (0, i))] * kinds
        + [pl.BlockSpec(memory_space=pl.ANY)] * len(others),
        out_specs=out_specs,
        out_shape=out_shape,
        scratch_shapes=[pltpu.VMEM((rows, width), bf16)],
        input_output_aliases=aliases,
        compiler_params=pltpu.CompilerParams(vmem_limit_bytes=VMEM_LIMIT),
        cost_estimate=SHORT,
    )(tokens, gain, shift, *mats, *shifts, *others)


def pack_kernel(weight, *refs):
    *vectors, packed, rider = refs
    width = packed.shape[-1] - LANES
    for kind in range(3):
        for pair in range(HEADS // 2):
            at = [((2 * pair + half) * 3 + kind) * HEAD_DIM for half in range(2)]
            packed[kind, :, pair * LANES : (pair + 1) * LANES] = jnp.concatenate(
                [weight[:, start : start + HEAD_DIM] for start in at], axis=1
            )
        packed[kind, :, width:] = jnp.zeros((packed.shape[1], LANES), bf16)
    rider[...] = jnp.zeros_like(rider)
    for i, vector in enumerate(vectors):
        rider[i : i + 1, : vector.shape[1]] = vector[...].astype(f32)
    packed[0, :, width:] = rider[...].astype(bf16)


def pack_joined(weight, vectors):
    rows, wide = weight.shape
    return pl.pallas_call(
        pack_kernel,
        out_shape=jax.ShapeDtypeStruct((3, rows, wide // 3 + LANES), bf16),
        scratch_shapes=[pltpu.VMEM((rows, LANES), f32)],
    )(weight, *(v[None] for v in vectors))


def unpack_kernel(riders, *refs):
    *vectors, query, value = refs
    for i, vector in enumerate(vectors):
        wide = vector.shape[1] // riders.shape[0]
        for device in range(riders.shape[0]):
            vector[:, device * wide : (device + 1) * wide] = riders[device, i : i + 1, :wide].astype(f32)
    for pair in range(HEADS // 2):
        for offset, out in ((0, query), (HEAD_DIM, value)):
            start = 4 * HEAD_DIM * pair + offset
            halves = [vectors[2][:, at : at + HEAD_DIM] for at in (start, start + 2 * HEAD_DIM)]
            out[:, pair * LANES : (pair + 1) * LANES] = jnp.concatenate(halves, axis=1)


def unpack_vectors(riders, counts):
    sizes = [riders.shape[0] * count for count in counts] + [HEADS * HEAD_DIM] * 2
    return pl.pallas_call(
        unpack_kernel,
        out_shape=[jax.ShapeDtypeStruct((1, size), f32) for size in sizes],
        cost_estimate=SHORT,
    )(riders)


def finish_kernel(count, *refs):
    terms, (joined, dense) = refs[:count], refs[-2:]
    total = terms[0][...].astype(f32)
    for term in terms[1:]:
        total += term[...].astype(f32)
    dense[...] = total[3]
    for first in range(0, 3 * HEADS, 2):
        halves = []
        for at in (first, first + 1):
            start = at // 3 * HEAD_DIM
            halves.append(total[at % 3, :, start : start + HEAD_DIM])
        joined[:, first * HEAD_DIM : (first + 2) * HEAD_DIM] = jnp.concatenate(halves, axis=1)


def finish_joined(own, arrived, earlier=()):
    _, rows, width = own.shape
    held = pl.BlockSpec(memory_space=pltpu.VMEM)
    return pl.pallas_call(
        functools.partial(finish_kernel, 1 + len(arrived)),
        in_specs=[held] * (1 + len(arrived)) + [pl.BlockSpec(memory_space=pl.ANY)] * len(earlier),
        out_specs=[held, held],
        out_shape=[jax.ShapeDtypeStruct((rows, 3 * width), f32), jax.ShapeDtypeStruct((rows, width), f32)],
        compiler_params=pltpu.CompilerParams(vmem_limit_bytes=2**23),
        cost_estimate=SHORT,
    )(own, *arrived, *earlier)


def on_device(
    tokens,
    cotangent,
    lengths,
    valid_count,
    first_gain,
    first_shift,
    joined_weight,
    joined_bias,
    dense_weight,
    dense_bias,
    second_gain,
    second_shift,
    up_weight,
    up_bias,
    down_weight,
    down_bias,
):
    grid = Grid()
    tok_rows, width = tokens.shape
    hops = WINDOW // tok_rows
    shard_rows = joined_weight.shape[0]

    y, x, core, z = grid.here
    ny, nx, _, nz = grid.size
    chips = ny * nx
    up_rows, ff = up_weight.shape
    ff_core = ff // 2

    def core_columns(block, which):
        wide = block.shape[1] // chips // 2
        return jnp.concatenate(
            [lax.dynamic_slice_in_dim(block, (2 * chip + which) * wide, wide, 1) for chip in range(chips)], axis=1
        )

    vectors = (first_gain, first_shift, joined_bias, dense_bias, second_gain, second_shift, up_bias, down_bias)
    counts = [v.shape[0] for v in vectors]
    joined_line = direct_gather(grid, pack_joined(joined_weight, vectors), Z)
    query_mat, key_mat, value_mat, riders = gather_joined(grid, joined_line)
    gain_one, shift_one, _, dense_vec, gain_two, shift_two, up_vec, down_vec, query_vec, value_vec = unpack_vectors(
        riders, counts
    )

    up_kept, up_given = (core_columns(up_weight, which) for which in (core, 1 - core))
    up_blocks = [half for side in (up_kept, grid.shift(up_given, CORE)) for half in (side[:, :width], side[:, width:])]
    lines = ("y", "x", "z")
    up_shard = after(jnp.stack([*up_blocks, dense_weight]), *joined_line[1:])
    up_lines = lax.all_gather(up_shard, lines, axis=0)
    down_mat = lax.all_gather(after(down_weight, *joined_line[1:]), lines, axis=0, tiled=True)

    before = [after(tokens, *joined_line[1:])]
    for _ in range(hops):
        before.append(grid.to_later(before[-1]))
    first_pos = grid.linear * tok_rows - WINDOW
    positions = first_pos + jnp.arange(WINDOW + tok_rows, dtype=jnp.int32)
    seg_ext = segment_ids(lengths, valid_count, positions)
    query_side, key_side = side_lanes(seg_ext, tok_rows)
    slopes = jnp.asarray(slope_lanes())
    live_rows = (positions[WINDOW:] < valid_count[0])[:, None]
    change_low = jnp.where(live_rows, cotangent, jnp.zeros_like(cotangent))
    change_both = jnp.concatenate([change_low, grid.shift(change_low, CORE)], axis=0)

    values = tokens.astype(f32)
    mats, shifts = (key_mat, value_mat), (jnp.zeros_like(value_vec), value_vec)
    normed_ext, stats, keys, all_values, queries = project(
        tokens, gain_one, shift_one, (*mats, query_mat), (*shifts, query_vec), hops, hops + 1
    )
    chunks = [(tokens, stats)]
    for hop in range(1, hops + 1):
        normed_ext, stats, keys, all_values = project(
            before[hop], gain_one, shift_one, mats, shifts, hops - hop, hops + 1, (normed_ext, keys, all_values)
        )
        chunks.insert(0, (before[hop], stats))
    context, log_total = attend(queries, keys, all_values, query_side, key_side, after(slopes, change_both))
    dense_part = after(up_lines[:, 4].reshape(-1, width), context)
    dense_other = grid.shift(dense_part, CORE)
    dense_sides = [jnp.where(core == which, dense_part, dense_other).reshape(chips, -1, width) for which in range(2)]
    dense_mat = jnp.stack(dense_sides, axis=1).reshape(-1, width)
    middle = values + dot_nn(context, dense_mat) + dense_vec
    normal_two, inverse_two = normalize(middle)
    normed_two = (normal_two * gain_two + shift_two).astype(bf16)
    normed_other = grid.shift(normed_two, CORE)
    hidden, slope = hidden_units(chips, core, normed_two, normed_other, up_lines, core_columns(up_vec, core))
    up_mat = whole_up(grid, up_lines, hidden)

    def far_sums(part, terms, *earlier):
        axis = (Y, X)[part]
        moving = terms[0]
        for step in range(1, grid.size[axis]):
            moving = add_after(grid.shift(moving, axis), terms[step], *earlier)
        return moving

    out_change = change_low.astype(f32)
    down_sums, down_vec_grad = down_terms(hidden, change_both)
    down_plane = lax.psum_scatter(down_sums, ("y", "x"), scatter_dimension=0, tiled=True)
    pre_change, up_core_grad = hidden_back(change_both, down_mat, slope, (down_sums,))
    given = product_nt(pre_change, up_mat, bf16, 1, tok_rows)
    up_sums = up_terms(normed_two, normed_other, pre_change, (given,))
    up_plane = lax.psum_scatter(up_sums, ("y", "x"), scatter_dimension=0, tiled=True)
    middle_change, branch_change, context_change, gain_two_grad, shift_two_grad, dense_vec_grad = middle_back(
        pre_change, up_mat, grid.shift(given, CORE), middle, gain_two, change_low, dense_mat, (up_sums,)
    )
    halves = HEADS // 4
    changes = attend_back(
        queries, keys, all_values, context_change, context, log_total, query_side, key_side, slopes, 0, halves
    )
    down_plane = after(down_plane, changes[0]).reshape(nz, -1, width)
    query_change, key_change, value_change = attend_back(
        queries, keys, all_values, context_change, context, log_total, query_side, key_side, after(slopes, down_plane),
        halves, halves, changes,
    )
    backs = [(back_y, back_x) for back_y in range(1, ny + 1) for back_x in range(1, nx + 1)]

    down_grad = direct_reduce(grid, down_plane, Z)
    chips_at = [(y - back_y) % ny * nx + (x - back_x) % nx for back_y, back_x in backs]
    rights = (query_change, key_change, value_change, branch_change)
    joined_given = joined_terms(normed_ext, context, rights, chips_at, core, (down_grad,))
    pairs = [(key_change, key_mat), (value_change, value_mat)]
    returned, *sums = chunk_back(
        [(left, 0, right) for left, right in pairs], chunks[0], bf16, None, joined_given[:1]
    )
    chunk_sums = [sums]
    joined_kept = split_terms(
        joined_given[2], grid.shift(joined_given[0], CORE), joined_given[3], grid.shift(joined_given[1], CORE), ny, nx, (returned,)
    )
    own_change, *sums = chunk_back(
        [(left, hops, right) for left, right in pairs] + [(query_change, 0, query_mat)], chunks[-1], f32, None, joined_kept
    )
    chunk_sums.append(sums)
    done = own_change
    for chunk in range(1, hops):
        arrived = grid.to_earlier(returned)
        returned, *sums = chunk_back(
            [(left, chunk, right) for left, right in pairs], chunks[chunk], bf16, arrived, (done,)
        )
        chunk_sums.append(sums)
        done = returned
    joined_near = []
    for terms, axis in ((joined_kept[:nx], X), (joined_kept[nx:], Y)):
        total = terms[0]
        for step in range(1, grid.size[axis]):
            total = add_after(grid.shift(total, axis), terms[step], done, split=step == grid.size[axis] - 1)
        joined_near.append(total)
    nears = [*joined_near[0], *joined_near[1]]
    up_rows_both = after(up_plane, *nears).reshape(2, nz, up_rows, ff_core).swapaxes(0, 1)
    returned = grid.to_earlier(returned)
    branch_given = product_nn(hidden, down_mat, bf16, 1, tok_rows, nears)
    branch_kept = product_nn(hidden, down_mat, f32, 0, tok_rows, (branch_given,))
    joined_far = [far_sums(part, joined_near[part], returned, branch_kept) for part in range(2)]
    both = [half.reshape(4, nz // 2, -1, width) for half in joined_far]
    both = jnp.concatenate(both, axis=1)

    def line_term(step):
        return lax.dynamic_index_in_dim(both, (z + step) % nz, 1, keepdims=False)

    arrived = [grid.shift(line_term(step), Z, step) for step in range(1, nz)]
    joined_grad, dense_grad = finish_joined(line_term(0), arrived)
    up_sum = direct_reduce(grid, up_rows_both, Z, arrived)
    up_mine = lax.dynamic_index_in_dim(up_sum, core, 0, keepdims=False)
    up_other = grid.shift(lax.dynamic_index_in_dim(up_sum, 1 - core, 0, keepdims=False), CORE)
    returned = returned.astype(f32)

    def interleave(mine, other):
        first, second = jnp.where(core == 0, mine, other), jnp.where(core == 0, other, mine)
        wide = mine.shape[1] // chips
        cuts = [slice(chip * wide, (chip + 1) * wide) for chip in range(chips)]
        return jnp.concatenate([side[:, cut] for cut in cuts for side in (first, second)], axis=1)

    up_grad = interleave(up_mine, up_other)
    branch_two = branch_kept + grid.shift(branch_given, CORE).astype(f32)
    layer_output = jnp.where(live_rows, middle + (branch_two + down_vec), 0.0).astype(bf16)
    gain_one_grad, shift_one_grad = (sum(total).reshape(-1) for total in zip(*chunk_sums))
    joined_vec_grad = jnp.stack(
        [
            jnp.sum(query_change.astype(f32), axis=0).reshape(HEADS, HEAD_DIM),
            jnp.sum(value_change.astype(f32), axis=0).reshape(HEADS, HEAD_DIM),
        ],
        axis=1,
    ).reshape(-1)
    input_grad = (middle_change + norm_back(own_change + returned, *normalize(values), gain_one)).astype(bf16)
    up_parts = up_core_grad.reshape(chips, 1, -1)
    up_vec_grad = jnp.concatenate(
        [jnp.where(core == which, up_parts, jnp.zeros_like(up_parts)) for which in range(2)], axis=1
    ).reshape(-1)
    vector_grads = (
        gain_one_grad, shift_one_grad, joined_vec_grad, dense_vec_grad, gain_two_grad, shift_two_grad, up_vec_grad,
        down_vec_grad,
    )
    cuts = np.cumsum([0] + counts)
    vector_rows = jnp.concatenate([v.reshape(grid.count, -1) for v in vector_grads], axis=1)
    owned = reduce_scatter_small(grid, after(vector_rows, *nears))
    owned = [owned[cuts[i] : cuts[i + 1]] for i in range(len(counts))]
    return (
        layer_output,
        input_grad,
        owned[0],
        owned[1],
        joined_grad,
        owned[2],
        dense_grad,
        owned[3],
        owned[4],
        owned[5],
        up_grad,
        owned[6],
        down_grad,
        owned[7],
    )


def solution(mesh):
    blocks, heads = mesh.devices.shape
    split = jax.sharding.Mesh(mesh.devices.reshape(2, blocks // 4, 2, heads), ALL)
    rows, vector, same = P(ALL, None), P(ALL), P()
    return jax.shard_map(
        on_device,
        mesh=split,
        in_specs=(
            rows, rows, same, same, vector, vector, rows, vector, rows, vector, vector, vector, rows, vector, rows, vector
        ),
        out_specs=(rows, rows, vector, vector, rows, vector, rows, vector, vector, vector, rows, vector, rows, vector),
        check_vma=False,
    )
```

```python
import functools

import functools

import jax
import jax.numpy as jnp
import numpy as np
from jax import lax
from jax.experimental import pallas as pl
from jax.experimental.pallas import tpu as pltpu
from jax.sharding import PartitionSpec as P

HEADS = 16
HEAD_DIM = 64
WINDOW = 1024
NDOCS = 32

ALL = ("y", "x", "core", "z")
norm_eps = 1e-05
bf16 = jnp.bfloat16
f32 = jnp.float32

MASKED = -1e30
TILE = 256
WIDE = 512
LANES = 128
SLOPE_LANE = NDOCS + 1
ROW_LANE = SLOPE_LANE + 6
SCALE = HEAD_DIM**-0.5
VMEM_LIMIT = 50 * 2**20
VMEM_ALL = 52 * 2**20
SHORT = pl.CostEstimate(flops=1, bytes_accessed=1, transcendentals=0)


def normalize(values):
    centred = values - jnp.mean(values, axis=-1, keepdims=True)
    inverse = lax.rsqrt(jnp.mean(centred * centred, axis=-1, keepdims=True) + norm_eps)
    return centred * inverse, inverse


def norm_back(change, normal, inverse, gain):
    scaled = change * gain
    mean_one = jnp.mean(scaled, axis=-1, keepdims=True)
    mean_two = jnp.mean(scaled * normal, axis=-1, keepdims=True)
    return inverse * (scaled - mean_one - normal * mean_two)


def dot_nn(left, right):
    return lax.dot_general(left, right, (((1,), (0,)), ((), ())), preferred_element_type=f32)


def dot_nt(left, right):
    return lax.dot_general(left, right, (((1,), (1,)), ((), ())), preferred_element_type=f32)


def dot_tn(left, right):
    return lax.dot_general(left, right, (((0,), (0,)), ((), ())), preferred_element_type=f32)


class Grid:
    def __init__(self):
        self.size = tuple(lax.axis_size(name) for name in ALL)
        self.here = tuple(lax.axis_index(name) for name in ALL)
        self.count = int(np.prod(self.size))
        self.linear = lax.axis_index(ALL)

    def shift(self, block, axis, distance=1):
        places = np.arange(self.count).reshape(self.size)
        ahead = np.roll(places, -distance, axis)
        return lax.ppermute(block, ALL, list(zip(places.ravel().tolist(), ahead.ravel().tolist())))

    def to_later(self, block):
        return lax.ppermute(block, ALL, [(i, i + 1) for i in range(self.count - 1)])

    def to_earlier(self, block):
        return lax.ppermute(block, ALL, [(i + 1, i) for i in range(self.count - 1)])


Y, X, CORE, Z = range(4)


def after(value, *earlier):
    anywhere = pl.BlockSpec(memory_space=pl.ANY)
    return pl.pallas_call(
        lambda *refs: None,
        in_specs=[anywhere] * (1 + len(earlier)),
        out_specs=anywhere,
        out_shape=jax.ShapeDtypeStruct(value.shape, value.dtype),
        input_output_aliases={0: 0},
        compiler_params=pltpu.CompilerParams(vmem_limit_bytes=2**17),
    )(value, *earlier)


def ring_gather(grid, block, axis):
    pieces = [block]
    for _ in range(grid.size[axis] - 1):
        pieces.append(grid.shift(pieces[-1], axis))
    return pieces


def direct_gather(grid, block, axis):
    return [block] + [grid.shift(block, axis, step) for step in range(1, grid.size[axis])]


def plane_gather(grid, line):
    half = len(line) // 2
    got = []
    for part, (one, two) in enumerate(((X, Y), (Y, X))):
        near = jnp.stack(ring_gather(grid, jnp.stack(line[part * half : (part + 1) * half]), one))
        for two_step, far in enumerate(ring_gather(grid, near, two)):
            got.append((part * half, one, two, two_step, far))
    return got


def plane_places(grid, got):
    ny, nx, _, nz = grid.size
    found = []
    for step, one, two, two_step, block in got:
        entries = []
        for one_step in range(block.shape[0]):
            back = {one: one_step, two: two_step}
            chip = (grid.here[Y] - back[Y]) % ny * nx + (grid.here[X] - back[X]) % nx
            entries.append([(chip, (grid.here[Z] - step - k) % nz) for k in range(block.shape[1])])
        found.append(entries)
    return found


def copy_blocks(moves, sems):
    copies = [pltpu.make_async_copy(source, target, sems.at[i]) for i, (source, target) in enumerate(moves)]
    for copy in copies:
        copy.start()
    for copy in copies:
        copy.wait()


def assemble(kernel, places, pieces, shapes, moves):
    anywhere = pl.BlockSpec(memory_space=pl.ANY)
    return pl.pallas_call(
        kernel,
        in_specs=[pl.BlockSpec(memory_space=pltpu.SMEM)] + [anywhere] * len(pieces),
        out_specs=[pl.BlockSpec(memory_space=pltpu.VMEM)] * len(shapes),
        out_shape=[jax.ShapeDtypeStruct(shape, bf16) for shape in shapes],
        scratch_shapes=[pltpu.SemaphoreType.DMA((moves,))],
        compiler_params=pltpu.CompilerParams(vmem_limit_bytes=VMEM_ALL),
        cost_estimate=SHORT,
    )(places, *pieces)


def joined_kernel(places, *refs):
    *pieces, query, key, value, riders, sems = refs
    width = query.shape[-1]
    moves = []
    for piece in pieces:
        for near in range(piece.shape[0]):
            for step in range(piece.shape[1]):
                at = places[len(moves) // 4]
                for kind, whole in enumerate((query, key, value)):
                    moves.append((piece.at[near, step, kind, :, pl.ds(0, width)], whole.at[at]))
                moves.append((piece.at[near, step, 0, :, pl.ds(width, LANES)], riders.at[at]))
    copy_blocks(moves, sems)


def gather_joined(grid, line):
    got = plane_gather(grid, line)
    rows, width = line[0].shape[-2], line[0].shape[-1] - LANES
    pieces, places = [], []
    for (_, _, _, _, block), entries in zip(got, plane_places(grid, got)):
        for which, piece in ((grid.here[CORE], block), (1 - grid.here[CORE], grid.shift(block, CORE))):
            pieces.append(piece)
            places += [(chip * 2 + which) * grid.size[Z] + z for near in entries for chip, z in near]
    *mats, riders = assemble(
        joined_kernel,
        jnp.stack(places).astype(jnp.int32),
        pieces,
        [(grid.count, rows, width)] * 3 + [(grid.count, rows, LANES)],
        4 * len(places),
    )
    return *(mat.reshape(-1, width) for mat in mats), riders


def up_kernel(places, lines, up, sems):
    width = lines.shape[-1]
    moves = []
    for entry in range(lines.shape[0]):
        for side in range(2):
            at = places[2 * entry + side]
            for half in range(2):
                moves.append((lines.at[entry, 2 * side + half], up.at[at, :, pl.ds(half * width, width)]))
    copy_blocks(moves, sems)


def whole_up(grid, lines, *earlier):
    count, _, rows, width = lines.shape
    nz, core = grid.size[Z], grid.here[CORE]
    places = [(entry // nz * 2 + which) * nz + entry % nz for entry in range(count) for which in (core, 1 - core)]
    places = after(jnp.stack(places).astype(jnp.int32), *earlier)
    (up,) = assemble(up_kernel, places, [lines], [(grid.count, rows, 2 * width)], 4 * count)
    return up.reshape(-1, 2 * width)


def add(left, right, kind=bf16):
    return (left.astype(f32) + right.astype(f32)).astype(kind)


def ring_reduce(grid, term, axis, kind=bf16):
    count = grid.size[axis]
    total = term(1)
    for step in range(2, count + 1):
        total = add(grid.shift(total, axis), term(step), kind)
    return total


def sum_kernel(count, *refs):
    total = refs[0][...].astype(f32)
    for ref in refs[1:count]:
        total += ref[...].astype(f32)
    refs[-1][...] = total


def sum_after(arrays, *earlier):
    held = pl.BlockSpec(memory_space=pltpu.VMEM)
    return pl.pallas_call(
        functools.partial(sum_kernel, len(arrays)),
        in_specs=[held] * len(arrays) + [pl.BlockSpec(memory_space=pl.ANY)] * len(earlier),
        out_specs=held,
        out_shape=jax.ShapeDtypeStruct(arrays[0].shape, f32),
        compiler_params=pltpu.CompilerParams(vmem_limit_bytes=2**23),
        cost_estimate=SHORT,
    )(*arrays, *earlier)


def direct_reduce(grid, terms, axis, earlier=()):
    count, place = grid.size[axis], grid.here[axis]

    def term(step):
        return lax.dynamic_index_in_dim(terms, (place + step) % count, 0, keepdims=False)

    return sum_after([term(0)] + [grid.shift(term(step), axis, step) for step in range(1, count)], *earlier)


def down_kernel(left, right, out, total):
    out[...] = dot_tn(left[...], right[...]).astype(bf16)

    @pl.when(pl.program_id(0) == 0)
    def _():
        total[...] = jnp.sum(right[: right.shape[0] // 2].astype(f32), axis=0, keepdims=True)


def down_terms(hidden, change):
    tokens, units = hidden.shape
    width = change.shape[1]
    return pl.pallas_call(
        down_kernel,
        grid=(units // TILE,),
        in_specs=[
            pl.BlockSpec((tokens, TILE), lambda i: (0, i)),
            pl.BlockSpec((tokens, width), lambda i: (0, 0)),
        ],
        out_specs=[pl.BlockSpec((TILE, width), lambda i: (i, 0)), pl.BlockSpec((1, width), lambda i: (0, 0))],
        out_shape=[jax.ShapeDtypeStruct((units, width), bf16), jax.ShapeDtypeStruct((1, width), f32)],
        compiler_params=pltpu.CompilerParams(vmem_limit_bytes=VMEM_LIMIT),
        cost_estimate=SHORT,
    )(hidden, change)


def up_kernel_terms(own, other, right, *refs):
    rows = own.shape[0]
    refs[-1][...] = (dot_tn(own[...], right[:rows]) + dot_tn(other[...], right[rows:])).astype(bf16)


def up_terms(own, other, pre_change, earlier=()):
    rows, width = own.shape
    tokens, units = pre_change.shape
    left = pl.BlockSpec((rows, width), lambda i: (0, 0))
    return pl.pallas_call(
        up_kernel_terms,
        grid=(units // WIDE,),
        in_specs=[left, left, pl.BlockSpec((tokens, WIDE), lambda i: (0, i))]
        + [pl.BlockSpec(memory_space=pl.ANY)] * len(earlier),
        out_specs=pl.BlockSpec((width, WIDE), lambda i: (0, i)),
        out_shape=jax.ShapeDtypeStruct((width, units), bf16),
        compiler_params=pltpu.CompilerParams(vmem_limit_bytes=VMEM_LIMIT),
        cost_estimate=SHORT,
    )(own, other, pre_change, *earlier)


def add_kernel(split, left, right, *refs):
    if split == 0:
        refs[-1][...] = (left[...].astype(f32) + right[...].astype(f32)).astype(bf16)
    for i in range(split):
        refs[-split + i][...] = (left[i].astype(f32) + right[i].astype(f32)).astype(bf16)


def add_after(left, right, *earlier, split=False):
    held = pl.BlockSpec(memory_space=pltpu.VMEM)
    shape = jax.ShapeDtypeStruct(left.shape, bf16)
    if split:
        shape = [jax.ShapeDtypeStruct(left.shape[1:], bf16)] * left.shape[0]
    return pl.pallas_call(
        functools.partial(add_kernel, left.shape[0] if split else 0),
        in_specs=[held] * 2 + [pl.BlockSpec(memory_space=pl.ANY)] * len(earlier),
        out_specs=[held] * left.shape[0] if split else held,
        out_shape=shape,
        compiler_params=pltpu.CompilerParams(vmem_limit_bytes=VMEM_LIMIT),
        cost_estimate=SHORT,
    )(left, right, *earlier)


def product_kernel(left, right, *refs):
    refs[-1][...] = dot_nt(left[...], right[...]).astype(refs[-1].dtype)


def product_nt(left, right, kind, row_block=0, rows=None, earlier=()):
    rows = left.shape[0] if rows is None else rows
    depth, wide = left.shape[1], right.shape[0]
    return pl.pallas_call(
        product_kernel,
        grid=(wide // WIDE,),
        in_specs=[
            pl.BlockSpec((rows, depth), lambda i: (row_block, 0)),
            pl.BlockSpec((WIDE, depth), lambda i: (i, 0)),
        ]
        + [pl.BlockSpec(memory_space=pl.ANY)] * len(earlier),
        out_specs=pl.BlockSpec((rows, WIDE), lambda i: (0, i)),
        out_shape=jax.ShapeDtypeStruct((rows, wide), kind),
        compiler_params=pltpu.CompilerParams(vmem_limit_bytes=VMEM_LIMIT),
        cost_estimate=SHORT,
    )(left, right, *earlier)


def branch_kernel(hidden, down, *refs):
    kept, given = refs[-2:]
    product = dot_nn(hidden[...], down[...])
    rows = kept.shape[0]
    kept[...] = product[:rows]
    given[...] = product[rows:].astype(bf16)


def branch_terms(hidden, down, earlier=()):
    tokens, units = hidden.shape
    width = down.shape[1]
    rows = tokens // 2
    tile = pl.BlockSpec((rows, TILE), lambda i: (0, i))
    return pl.pallas_call(
        branch_kernel,
        grid=(width // TILE,),
        in_specs=[pl.BlockSpec((tokens, units), lambda i: (0, 0)), pl.BlockSpec((units, TILE), lambda i: (0, i))]
        + [pl.BlockSpec(memory_space=pl.ANY)] * len(earlier),
        out_specs=[tile, tile],
        out_shape=[jax.ShapeDtypeStruct((rows, width), f32), jax.ShapeDtypeStruct((rows, width), bf16)],
        compiler_params=pltpu.CompilerParams(vmem_limit_bytes=VMEM_LIMIT),
        cost_estimate=SHORT,
    )(hidden, down, *earlier)


def chunk_kernel(count, with_arrived, *refs):
    lefts, rights, (tokens, stats) = refs[:count], refs[count : 2 * count], refs[2 * count : 2 * count + 2]
    moved, gain_sum, shift_sum = refs[-3:]
    change = dot_nt(lefts[0][...], rights[0][...])
    for left, right in zip(lefts[1:], rights[1:]):
        change += dot_nt(left[...], right[...])
    normal = (tokens[...].astype(f32) - stats[:, :1]) * stats[:, 1:2]
    gain_sum[...] = jnp.sum(change * normal, axis=0, keepdims=True)
    shift_sum[...] = jnp.sum(change, axis=0, keepdims=True)
    if with_arrived:
        change += refs[2 * count + 2][...].astype(f32)
    moved[...] = change.astype(moved.dtype)


def chunk_back(pairs, chunk, kind, arrived=None, earlier=()):
    rows, width = chunk[0].shape
    tile = pl.BlockSpec((rows, WIDE), lambda i: (0, i))
    sums = pl.BlockSpec((1, WIDE), lambda i: (0, i))
    return pl.pallas_call(
        functools.partial(chunk_kernel, len(pairs), arrived is not None),
        grid=(width // WIDE,),
        in_specs=[pl.BlockSpec((rows, left.shape[1]), lambda i, at=at: (at, 0)) for left, at, _ in pairs]
        + [pl.BlockSpec((WIDE, right.shape[1]), lambda i: (i, 0)) for *_, right in pairs]
        + [tile, pl.BlockSpec((rows, LANES), lambda i: (0, 0))]
        + [tile] * (arrived is not None)
        + [pl.BlockSpec(memory_space=pl.ANY)] * len(earlier),
        out_specs=[tile, sums, sums],
        out_shape=[jax.ShapeDtypeStruct((rows, width), kind)] + [jax.ShapeDtypeStruct((1, width), f32)] * 2,
        compiler_params=pltpu.CompilerParams(vmem_limit_bytes=VMEM_LIMIT),
        cost_estimate=SHORT,
    )(
        *(left for left, *_ in pairs),
        *(right for *_, right in pairs),
        *chunk,
        *(() if arrived is None else (arrived,)),
        *earlier,
    )


def middle_kernel(pre_change, up, arrived, middle, gain, out_change, dense, *refs):
    middle_change, branch_change, context_change, gain_sum, shift_sum, branch_sum = refs[-6:]
    change = dot_nt(pre_change[...], up[...]) + arrived[...].astype(f32)
    normal, inverse = normalize(middle[...])
    moved = out_change[...].astype(f32) + norm_back(change, normal, inverse, gain[...])
    low = moved.astype(bf16)
    middle_change[...] = moved
    branch_change[...] = low
    context_change[...] = dot_nt(low, dense[...]).astype(bf16)
    first = pl.program_id(0) == 0
    for total, part in ((gain_sum, change * normal), (shift_sum, change), (branch_sum, low.astype(f32))):
        total[...] = jnp.where(first, 0.0, total[...]) + jnp.sum(part, axis=0, keepdims=True)


def middle_back(pre_change, up, arrived, middle, gain, out_change, dense, earlier=()):
    rows, width = middle.shape
    tile = pl.BlockSpec((TILE, width), lambda i: (i, 0))
    sums = pl.BlockSpec((1, width), lambda i: (0, 0))

    def whole(array):
        return pl.BlockSpec(array.shape, lambda i: (0, 0))

    return pl.pallas_call(
        middle_kernel,
        grid=(rows // TILE,),
        in_specs=[
            pl.BlockSpec((TILE, pre_change.shape[1]), lambda i: (i, 0)), whole(up), tile, tile, whole(gain), tile, whole(dense)
        ]
        + [pl.BlockSpec(memory_space=pl.ANY)] * len(earlier),
        out_specs=[tile, tile, tile, sums, sums, sums],
        out_shape=[
            jax.ShapeDtypeStruct((rows, width), f32),
            jax.ShapeDtypeStruct((rows, width), bf16),
            jax.ShapeDtypeStruct((rows, width), bf16),
        ]
        + [jax.ShapeDtypeStruct((1, width), f32)] * 3,
        compiler_params=pltpu.CompilerParams(vmem_limit_bytes=VMEM_LIMIT),
        cost_estimate=SHORT,
    )(pre_change, up, arrived, middle, gain, out_change, dense, *earlier)


def joined_kernel_terms(blocks, core, tokens_ext, context, query, key, value, branch, *refs):
    given_ahead, given_behind, kept_ahead, kept_behind, query_sum, value_sum = refs[-6:]

    @pl.when(pl.program_id(0) == 0)
    def _():
        query_sum[...] = jnp.sum(query[...].astype(f32), axis=0, keepdims=True)
        value_sum[...] = jnp.sum(value[...].astype(f32), axis=0, keepdims=True)

    left = tokens_ext[...]
    own = left[left.shape[0] - query.shape[0] :]
    rows = kept_ahead.shape[2]
    swapped = core[0] == 1
    for kind, (one, two) in enumerate(((own, query), (left, key), (left, value), (context[...], branch))):
        product = dot_tn(one, two[...])
        for part, (given, kept) in enumerate(((given_ahead, kept_ahead), (given_behind, kept_behind))):
            low, high = (product[(2 * side + part) * rows : (2 * side + part + 1) * rows] for side in range(2))
            given[0, kind] = jnp.where(swapped, low, high).astype(bf16)
            kept[0, kind] = jnp.where(swapped, high, low).astype(bf16)


def joined_terms(normed_ext, context, rights, chips_at, core, earlier=()):
    ext_rows, width = normed_ext.shape
    tok_rows = context.shape[0]
    count = len(chips_at)
    rows = width // count
    half = (1, 4, rows // 4, width)
    stacked = pl.BlockSpec(half, lambda i, at, core: (i, 0, 0, 0))
    sums = pl.BlockSpec((1, width), lambda i, at, core: (0, 0))

    def whole(array):
        return pl.BlockSpec(array.shape, lambda i, at, core: (0, 0))

    return pl.pallas_call(
        joined_kernel_terms,
        grid_spec=pltpu.PrefetchScalarGridSpec(
            num_scalar_prefetch=2,
            grid=(count,),
            in_specs=[
                pl.BlockSpec((ext_rows, rows), lambda i, at, core: (0, at[i])),
                pl.BlockSpec((tok_rows, rows), lambda i, at, core: (0, at[i])),
                *(whole(right) for right in rights),
                *[pl.BlockSpec(memory_space=pl.ANY)] * len(earlier),
            ],
            out_specs=[stacked] * 4 + [sums] * 2,
        ),
        out_shape=[jax.ShapeDtypeStruct((count, *half[1:]), bf16)] * 4 + [jax.ShapeDtypeStruct((1, width), f32)] * 2,
        compiler_params=pltpu.CompilerParams(vmem_limit_bytes=VMEM_LIMIT),
        cost_estimate=SHORT,
    )(
        jnp.stack(chips_at).astype(jnp.int32), jnp.reshape(core, (1,)).astype(jnp.int32), normed_ext, context, *rights, *earlier
    )


def split_kernel(nx, ahead, arrived_ahead, behind, arrived_behind, *refs):
    ny = ahead.shape[0]
    outs = refs[-nx - ny :]
    for back_y in range(ny):
        for back_x in range(nx):
            outs[back_x][back_y] = (ahead[back_y, back_x].astype(f32) + arrived_ahead[back_y, back_x].astype(f32)).astype(bf16)
            outs[nx + back_y][back_x] = (
                behind[back_y, back_x].astype(f32) + arrived_behind[back_y, back_x].astype(f32)
            ).astype(bf16)


def split_terms(ahead, arrived_ahead, behind, arrived_behind, ny, nx, earlier=()):
    arrays = [array.reshape(ny, nx, *array.shape[1:]) for array in (ahead, arrived_ahead, behind, arrived_behind)]
    shape = arrays[0].shape[2:]
    kinds = shape[0]
    rest = shape[1:]
    return pl.pallas_call(
        functools.partial(split_kernel, nx),
        grid=(kinds,),
        in_specs=[pl.BlockSpec((ny, nx, 1, *rest), lambda i: (0, 0, i, 0, 0))] * 4
        + [pl.BlockSpec(memory_space=pl.ANY)] * len(earlier),
        out_specs=[pl.BlockSpec((ny, 1, *rest), lambda i: (0, i, 0, 0))] * nx
        + [pl.BlockSpec((nx, 1, *rest), lambda i: (0, i, 0, 0))] * ny,
        out_shape=[jax.ShapeDtypeStruct((ny, *shape), bf16)] * nx + [jax.ShapeDtypeStruct((nx, *shape), bf16)] * ny,
        compiler_params=pltpu.CompilerParams(vmem_limit_bytes=VMEM_LIMIT),
        cost_estimate=SHORT,
    )(*arrays, *earlier)


def reduce_scatter_small(grid, terms):
    terms = terms.reshape(*grid.size, terms.shape[1])
    for axis, dim in ((CORE, 2), (X, 1), (Y, 0)):
        def term(step, terms=terms, axis=axis, dim=dim):
            return lax.dynamic_index_in_dim(terms, (grid.here[axis] - step) % grid.size[axis], dim, keepdims=False)

        terms = ring_reduce(grid, term, axis, f32)
    total = lax.dynamic_index_in_dim(terms, grid.here[Z], 0, keepdims=False)
    for step in range(1, grid.size[Z]):
        term = lax.dynamic_index_in_dim(terms, (grid.here[Z] + step) % grid.size[Z], 0, keepdims=False)
        total = total + grid.shift(term, Z, step)
    return total


def thirds(values):
    high = values.astype(bf16)
    rest = values - high.astype(f32)
    middle = rest.astype(bf16)
    return high, middle, (rest - middle.astype(f32)).astype(bf16)


def slope_lanes():
    lanes = np.zeros((HEADS // 2, 8, LANES), np.float32)
    for h in range(HEADS):
        rest = np.float32(2.0 ** (-8.0 * (h + 1) / HEADS))
        for part in range(3):
            piece = np.float32(rest.astype(bf16))
            rest = np.float32(rest - piece)
            lanes[h // 2, h % 2, SLOPE_LANE + part] = piece
            lanes[h // 2, h % 2, SLOPE_LANE + 3 + part] = piece
    return lanes


def side_lanes(seg_ext, tok_rows):
    lane = jnp.arange(LANES, dtype=jnp.int32)
    doc = lane[None, :] <= NDOCS
    seg_query = seg_ext[seg_ext.shape[0] - tok_rows :]
    query_side = jnp.where(doc & (lane[None, :] == seg_query[:, None]), 1.0, 0.0).astype(bf16)
    key_pos = jnp.arange(seg_ext.shape[0], dtype=jnp.int32)[:, None]
    key_side = jnp.where(doc & (lane[None, :] != seg_ext[:, None]), MASKED, 0.0)
    key_side = jnp.where((lane >= SLOPE_LANE) & (lane < SLOPE_LANE + 3), (key_pos // TILE * TILE).astype(f32), key_side)
    key_side = jnp.where((lane >= SLOPE_LANE + 3) & (lane < ROW_LANE), (key_pos % TILE).astype(f32), key_side)
    key_side = jnp.where((lane >= ROW_LANE) & (lane < ROW_LANE + 3), 1.0, key_side)
    return query_side, key_side.astype(bf16)


def key_tiles(tile):
    wide = WINDOW // TILE
    edges = [(tile + step) * TILE for step in (0, 1, wide, wide + 1)]
    return [slice(edges[i], edges[i + 1]) for i in range(3)]


def attend_kernel(query, key, value, query_side, key_side, slope, context, log_total):
    pair = pl.program_id(0)
    lane = lax.broadcasted_iota(jnp.int32, (TILE, LANES), 1)
    causal = lax.broadcasted_iota(jnp.int32, (TILE, TILE), 0) >= lax.broadcasted_iota(jnp.int32, (TILE, TILE), 1)
    keys = jnp.concatenate([key[...], key_side[...]], axis=1)
    for tile in range(query.shape[0] // TILE):
        rows = slice(tile * TILE, (tile + 1) * TILE)
        first, middle, last = key_tiles(tile)
        scaled = query[rows, :] * jnp.asarray(SCALE, bf16)
        outs, logs = [], []
        for half in range(2):
            mine = (lane >= HEAD_DIM) == (half == 1)
            side = query_side[rows, :] + slope[0, half : half + 1, :].astype(bf16)
            queries = jnp.concatenate([jnp.where(mine, scaled, jnp.zeros_like(scaled)), side], axis=1)
            inner = dot_nt(queries, keys[middle])
            outer = jnp.where(causal, dot_nt(queries, keys[last]), dot_nt(queries, keys[first]))
            top = jnp.maximum(jnp.max(inner, axis=1, keepdims=True), jnp.max(outer, axis=1, keepdims=True))
            inner = jnp.exp(inner - top)
            outer = jnp.exp(outer - top)
            total = jnp.sum(inner, axis=1, keepdims=True) + jnp.sum(outer, axis=1, keepdims=True)
            summed = dot_nn(inner.astype(bf16), value[middle, :])
            summed += dot_nn(jnp.where(causal, outer, 0.0).astype(bf16), value[last, :])
            summed += dot_nn(jnp.where(causal, 0.0, outer).astype(bf16), value[first, :])
            outs.append(summed / total)
            logs.append(top + jnp.log(total))
        context[rows, :] = jnp.where(lane < HEAD_DIM, outs[0], outs[1]).astype(bf16)
        before = jnp.where(pair == 0, jnp.zeros((TILE, LANES), f32), log_total[rows, :])
        log_total[rows, :] = jnp.where(lane == 2 * pair, logs[0], jnp.where(lane == 2 * pair + 1, logs[1], before))


def attend(queries, keys, values, query_side, key_side, slopes):
    tok_rows, width = queries.shape
    key_rows = keys.shape[0]
    steps = HEADS // 2
    return pl.pallas_call(
        attend_kernel,
        grid=(steps,),
        in_specs=[
            pl.BlockSpec((tok_rows, LANES), lambda p: (0, p)),
            pl.BlockSpec((key_rows, LANES), lambda p: (0, p)),
            pl.BlockSpec((key_rows, LANES), lambda p: (0, p)),
            pl.BlockSpec((tok_rows, LANES), lambda p: (0, 0)),
            pl.BlockSpec((key_rows, LANES), lambda p: (0, 0)),
            pl.BlockSpec((1, 8, LANES), lambda p: (p, 0, 0)),
        ],
        out_specs=[
            pl.BlockSpec((tok_rows, LANES), lambda p: (0, p)),
            pl.BlockSpec((tok_rows, LANES), lambda p: (0, 0)),
        ],
        out_shape=[
            jax.ShapeDtypeStruct((tok_rows, width), bf16),
            jax.ShapeDtypeStruct((tok_rows, LANES), f32),
        ],
        compiler_params=pltpu.CompilerParams(vmem_limit_bytes=VMEM_ALL),
        cost_estimate=SHORT,
    )(queries, keys, values, query_side, key_side, slopes)


def attend_back_kernel(
    query, key, value, change, context, log_total, query_side, key_side, slope, *refs, first_pair,
):
    query_change, key_change, value_change, key_sum, value_sum = refs[-5:]
    pair = first_pair + pl.program_id(0)
    lane = lax.broadcasted_iota(jnp.int32, (TILE, LANES), 1)
    causal = lax.broadcasted_iota(jnp.int32, (TILE, TILE), 0) <= lax.broadcasted_iota(jnp.int32, (TILE, TILE), 1)
    keys = jnp.concatenate([key[...], key_side[...]], axis=1)
    values = jnp.concatenate([value[...], key_side[...]], axis=1)
    keys_across = key[...].T
    key_sum[...] = jnp.zeros_like(key_sum)
    value_sum[...] = jnp.zeros_like(value_sum)

    def row_lanes(column):
        high, middle, low = thirds(column)
        lanes = jnp.where(lane == ROW_LANE + 2, low, jnp.zeros((TILE, LANES), bf16))
        return jnp.where(lane == ROW_LANE, high, jnp.where(lane == ROW_LANE + 1, middle, lanes))

    for tile in range(query.shape[0] // TILE):
        rows = slice(tile * TILE, (tile + 1) * TILE)
        first, middle, last = key_tiles(tile)
        scaled = query[rows, :] * jnp.asarray(SCALE, bf16)
        changed = change[rows, :]
        product = changed.astype(f32) * context[rows, :].astype(f32)
        logs = log_total[rows, :]
        parts = []
        for half in range(2):
            mine = (lane >= HEAD_DIM) == (half == 1)
            asked = jnp.where(mine, scaled, jnp.zeros_like(scaled))
            moved = jnp.where(mine, changed, jnp.zeros_like(changed))
            log_row = jnp.sum(jnp.where(lane == 2 * pair + half, logs, 0.0), axis=1, keepdims=True)
            inner_row = jnp.sum(jnp.where(mine, product, 0.0), axis=1, keepdims=True)
            side = query_side[rows, :] + slope[0, half : half + 1, :].astype(bf16) + row_lanes(-log_row)
            queries = jnp.concatenate([asked, side], axis=1)
            changes = jnp.concatenate([moved, row_lanes(-inner_row)], axis=1)
            prob = jnp.exp(dot_nt(keys[middle], queries))
            prob_edge = jnp.exp(jnp.where(causal, dot_nt(keys[last], queries), dot_nt(keys[first], queries)))
            score = (prob * dot_nt(values[middle], changes)).astype(bf16)
            score_edge = prob_edge * jnp.where(causal, dot_nt(values[last], changes), dot_nt(values[first], changes))
            score_last = jnp.where(causal, score_edge, 0.0).astype(bf16)
            score_first = jnp.where(causal, 0.0, score_edge).astype(bf16)
            value_sum[middle, :] += dot_nn(prob.astype(bf16), moved)
            value_sum[last, :] += dot_nn(jnp.where(causal, prob_edge, 0.0).astype(bf16), moved)
            value_sum[first, :] += dot_nn(jnp.where(causal, 0.0, prob_edge).astype(bf16), moved)
            key_sum[middle, :] += dot_nn(score, asked)
            key_sum[last, :] += dot_nn(score_last, asked)
            key_sum[first, :] += dot_nn(score_first, asked)
            parts.append(
                dot_nn(keys_across[:, middle], score)
                + dot_nn(keys_across[:, last], score_last)
                + dot_nn(keys_across[:, first], score_first)
            )
        entry = lax.broadcasted_iota(jnp.int32, (LANES, TILE), 0)
        query_change[rows, :] = (jnp.where(entry < HEAD_DIM, parts[0], parts[1]).T * SCALE).astype(bf16)
    key_change[...] = key_sum[...].astype(bf16)
    value_change[...] = value_sum[...].astype(bf16)


def attend_back(queries, keys, values, change, context, log_total, query_side, key_side, slopes, first_pair, count, others=()):
    tok_rows, width = queries.shape
    key_rows = keys.shape[0]
    steps = HEADS // 2
    by_query = pl.BlockSpec((tok_rows, LANES), lambda p: (0, first_pair + p))
    by_key = pl.BlockSpec((key_rows, LANES), lambda p: (0, first_pair + p))
    return pl.pallas_call(
        functools.partial(attend_back_kernel, first_pair=first_pair),
        grid=(count,),
        in_specs=[
            by_query,
            by_key,
            by_key,
            by_query,
            by_query,
            pl.BlockSpec((tok_rows, LANES), lambda p: (0, 0)),
            pl.BlockSpec((tok_rows, LANES), lambda p: (0, 0)),
            pl.BlockSpec((key_rows, LANES), lambda p: (0, 0)),
            pl.BlockSpec((1, 8, LANES), lambda p: (first_pair + p, 0, 0)),
        ]
        + [pl.BlockSpec(memory_space=pl.ANY)] * len(others),
        out_specs=[by_query, by_key, by_key],
        out_shape=[
            jax.ShapeDtypeStruct((tok_rows, width), bf16),
            jax.ShapeDtypeStruct((key_rows, width), bf16),
            jax.ShapeDtypeStruct((key_rows, width), bf16),
        ],
        input_output_aliases={9 + i: i for i in range(len(others))},
        scratch_shapes=[pltpu.VMEM((key_rows, LANES), f32), pltpu.VMEM((key_rows, LANES), f32)],
        compiler_params=pltpu.CompilerParams(vmem_limit_bytes=VMEM_ALL),
        cost_estimate=SHORT,
    )(queries, keys, values, change, context, log_total, query_side, key_side, slopes, *others)


def segment_ids(lengths, valid_count, positions):
    doc_ends = jnp.cumsum(lengths)
    passed = jnp.sum((doc_ends[None, :] <= positions[:, None]).astype(jnp.int32), axis=1)
    inside = jnp.where(positions < valid_count[0], passed, NDOCS)
    return jnp.where(positions < 0, -1, inside)


ROOT = float(np.sqrt(2.0 / np.pi))


def gelu_parts(values):
    square = values * values
    rise = 0.5 * jnp.tanh(values * (square * (ROOT * 0.044715) + ROOT)) + 0.5
    bend = values * (square * (6.0 * ROOT * 0.044715) + 2.0 * ROOT)
    return values * rise, rise + bend * (rise - rise * rise)


def hidden_kernel(chips, core, own, other, up_kept, up_given, bias, hidden, slope, sides):
    rows, width = own.shape
    wide = width // (2 * chips)

    @pl.when(pl.program_id(0) == 0)
    def _():
        first = core[0] == 0
        for chip in range(chips):
            start, to = 2 * chip * wide, slice(chip * wide, (chip + 1) * wide)
            for part, tokens in enumerate((own, other)):
                low, high = tokens[:, start : start + wide], tokens[:, start + wide : start + 2 * wide]
                sides[0, part * rows : (part + 1) * rows, to] = jnp.where(first, low, high)
                sides[1, part * rows : (part + 1) * rows, to] = jnp.where(first, high, low)

    kept = up_kept[...].reshape(width // 2, WIDE)
    given = up_given[...].reshape(width // 2, WIDE)
    for start in range(0, 2 * rows, TILE):
        product = dot_nn(sides[0, start : start + TILE], kept) + dot_nn(sides[1, start : start + TILE], given)
        value, rise = gelu_parts(product + bias[...])
        hidden[start : start + TILE, :] = value.astype(bf16)
        slope[start : start + TILE, :] = rise.astype(bf16)


def hidden_units(chips, core, own, other, lines, bias):
    rows, depth = own.shape
    count, _, height, width = lines.shape
    units = 2 * width
    steps = width // WIDE
    columns = pl.BlockSpec((2 * rows, WIDE), lambda i, at: (0, i))
    whole = pl.BlockSpec((rows, depth), lambda i, at: (0, 0))

    def block(side):
        return pl.BlockSpec((count, 1, height, WIDE), lambda i, at: (0, 2 * side + i // steps, 0, i % steps))

    return pl.pallas_call(
        functools.partial(hidden_kernel, chips),
        grid_spec=pltpu.PrefetchScalarGridSpec(
            num_scalar_prefetch=1,
            grid=(units // WIDE,),
            in_specs=[whole, whole, block(0), block(1), pl.BlockSpec((1, WIDE), lambda i, at: (0, i))],
            out_specs=[columns, columns],
            scratch_shapes=[pltpu.VMEM((2, 2 * rows, depth // 2), bf16)],
        ),
        out_shape=[jax.ShapeDtypeStruct((2 * rows, units), bf16)] * 2,
        compiler_params=pltpu.CompilerParams(vmem_limit_bytes=VMEM_LIMIT),
        cost_estimate=SHORT,
    )(jnp.reshape(core, (1,)).astype(jnp.int32), own, other, lines, lines, bias)


def pre_change_kernel(change, down, slope, *refs):
    pre_change, total = refs[-2:]
    moved = (dot_nt(change[...], down[...]) * slope[...].astype(f32)).astype(bf16)
    pre_change[...] = moved
    total[...] = jnp.sum(moved.astype(f32), axis=0, keepdims=True)


def hidden_back(change, down, slope, earlier=()):
    tokens, depth = change.shape
    units = down.shape[0]
    columns = pl.BlockSpec((tokens, WIDE), lambda i: (0, i))
    return pl.pallas_call(
        pre_change_kernel,
        grid=(units // WIDE,),
        in_specs=[
            pl.BlockSpec((tokens, depth), lambda i: (0, 0)),
            pl.BlockSpec((WIDE, depth), lambda i: (i, 0)),
            columns,
        ]
        + [pl.BlockSpec(memory_space=pl.ANY)] * len(earlier),
        out_specs=[columns, pl.BlockSpec((1, WIDE), lambda i: (0, i))],
        out_shape=[jax.ShapeDtypeStruct((tokens, units), bf16), jax.ShapeDtypeStruct((1, units), f32)],
        compiler_params=pltpu.CompilerParams(vmem_limit_bytes=VMEM_LIMIT),
        cost_estimate=SHORT,
    )(change, down, slope, *earlier)


def projection_kernel(kinds, others, tokens, gain, shift, *refs):
    mats, shifts = refs[:kinds], refs[kinds : 2 * kinds]
    normed, stats, *outs, held = refs[2 * kinds + others :]

    @pl.when(pl.program_id(0) == 0)
    def _():
        values = tokens[...].astype(f32)
        mean = jnp.mean(values, axis=-1, keepdims=True)
        centred = values - mean
        inverse = lax.rsqrt(jnp.mean(centred * centred, axis=-1, keepdims=True) + norm_eps)
        low = (centred * inverse * gain[...] + shift[...]).astype(bf16)
        normed[...] = low
        held[...] = low
        lane = lax.broadcasted_iota(jnp.int32, stats.shape, 1)
        stats[...] = jnp.where(lane == 0, mean, inverse)

    for mat, add, out in zip(mats, shifts, outs):
        out[...] = (dot_nn(held[...], mat[...]) + add[...]).astype(bf16)


def project(tokens, gain, shift, mats, shifts, chunk, chunks, others=()):
    rows, width = tokens.shape
    kinds = len(mats)
    ext_rows = chunks * rows
    fixed = pl.BlockSpec((rows, width), lambda i: (0, 0))
    row = pl.BlockSpec((1, width), lambda i: (0, 0))
    placed = pl.BlockSpec((rows, WIDE), lambda i: (chunk, i))
    out_specs = [pl.BlockSpec((rows, width), lambda i: (chunk, 0)), pl.BlockSpec((rows, LANES), lambda i: (0, 0)), placed, placed]
    out_shape = [jax.ShapeDtypeStruct((ext_rows, width), bf16), jax.ShapeDtypeStruct((rows, LANES), f32)]
    out_shape += [jax.ShapeDtypeStruct((ext_rows, width), bf16)] * 2
    if kinds == 3:
        out_specs.append(pl.BlockSpec((rows, WIDE), lambda i: (0, i)))
        out_shape.append(jax.ShapeDtypeStruct((rows, width), bf16))
    aliases = {3 + 2 * kinds + i: place for i, place in enumerate((0, 2, 3)[: len(others)])}
    return pl.pallas_call(
        functools.partial(projection_kernel, kinds, len(others)),
        grid=(width // WIDE,),
        in_specs=[fixed, row, row]
        + [pl.BlockSpec((width, WIDE), lambda i: (0, i))] * kinds
        + [pl.BlockSpec((1, WIDE), lambda i: (0, i))] * kinds
        + [pl.BlockSpec(memory_space=pl.ANY)] * len(others),
        out_specs=out_specs,
        out_shape=out_shape,
        scratch_shapes=[pltpu.VMEM((rows, width), bf16)],
        input_output_aliases=aliases,
        compiler_params=pltpu.CompilerParams(vmem_limit_bytes=VMEM_LIMIT),
        cost_estimate=SHORT,
    )(tokens, gain, shift, *mats, *shifts, *others)


def pack_kernel(weight, *refs):
    *vectors, packed, rider = refs
    width = packed.shape[-1] - LANES
    for kind in range(3):
        for pair in range(HEADS // 2):
            at = [((2 * pair + half) * 3 + kind) * HEAD_DIM for half in range(2)]
            packed[kind, :, pair * LANES : (pair + 1) * LANES] = jnp.concatenate(
                [weight[:, start : start + HEAD_DIM] for start in at], axis=1
            )
        packed[kind, :, width:] = jnp.zeros((packed.shape[1], LANES), bf16)
    rider[...] = jnp.zeros_like(rider)
    for i, vector in enumerate(vectors):
        rider[i : i + 1, : vector.shape[1]] = vector[...].astype(f32)
    packed[0, :, width:] = rider[...].astype(bf16)


def pack_joined(weight, vectors):
    rows, wide = weight.shape
    return pl.pallas_call(
        pack_kernel,
        out_shape=jax.ShapeDtypeStruct((3, rows, wide // 3 + LANES), bf16),
        scratch_shapes=[pltpu.VMEM((rows, LANES), f32)],
    )(weight, *(v[None] for v in vectors))


def unpack_kernel(riders, *refs):
    *vectors, query, value = refs
    for i, vector in enumerate(vectors):
        wide = vector.shape[1] // riders.shape[0]
        for device in range(riders.shape[0]):
            vector[:, device * wide : (device + 1) * wide] = riders[device, i : i + 1, :wide].astype(f32)
    for pair in range(HEADS // 2):
        for offset, out in ((0, query), (HEAD_DIM, value)):
            start = 4 * HEAD_DIM * pair + offset
            halves = [vectors[2][:, at : at + HEAD_DIM] for at in (start, start + 2 * HEAD_DIM)]
            out[:, pair * LANES : (pair + 1) * LANES] = jnp.concatenate(halves, axis=1)


def unpack_vectors(riders, counts):
    sizes = [riders.shape[0] * count for count in counts] + [HEADS * HEAD_DIM] * 2
    return pl.pallas_call(
        unpack_kernel,
        out_shape=[jax.ShapeDtypeStruct((1, size), f32) for size in sizes],
        cost_estimate=SHORT,
    )(riders)


def finish_kernel(count, *refs):
    terms, (joined, dense) = refs[:count], refs[-2:]
    total = terms[0][...].astype(f32)
    for term in terms[1:]:
        total += term[...].astype(f32)
    dense[...] = total[3]
    for first in range(0, 3 * HEADS, 2):
        halves = []
        for at in (first, first + 1):
            start = at // 3 * HEAD_DIM
            halves.append(total[at % 3, :, start : start + HEAD_DIM])
        joined[:, first * HEAD_DIM : (first + 2) * HEAD_DIM] = jnp.concatenate(halves, axis=1)


def finish_joined(own, arrived, earlier=()):
    _, rows, width = own.shape
    held = pl.BlockSpec(memory_space=pltpu.VMEM)
    return pl.pallas_call(
        functools.partial(finish_kernel, 1 + len(arrived)),
        in_specs=[held] * (1 + len(arrived)) + [pl.BlockSpec(memory_space=pl.ANY)] * len(earlier),
        out_specs=[held, held],
        out_shape=[jax.ShapeDtypeStruct((rows, 3 * width), f32), jax.ShapeDtypeStruct((rows, width), f32)],
        compiler_params=pltpu.CompilerParams(vmem_limit_bytes=2**23),
        cost_estimate=SHORT,
    )(own, *arrived, *earlier)


def on_device(
    tokens,
    cotangent,
    lengths,
    valid_count,
    first_gain,
    first_shift,
    joined_weight,
    joined_bias,
    dense_weight,
    dense_bias,
    second_gain,
    second_shift,
    up_weight,
    up_bias,
    down_weight,
    down_bias,
):
    grid = Grid()
    tok_rows, width = tokens.shape
    hops = WINDOW // tok_rows
    shard_rows = joined_weight.shape[0]

    y, x, core, z = grid.here
    ny, nx, _, nz = grid.size
    chips = ny * nx
    up_rows, ff = up_weight.shape
    ff_core = ff // 2

    def core_columns(block, which):
        wide = block.shape[1] // chips // 2
        return jnp.concatenate(
            [lax.dynamic_slice_in_dim(block, (2 * chip + which) * wide, wide, 1) for chip in range(chips)], axis=1
        )

    vectors = (first_gain, first_shift, joined_bias, dense_bias, second_gain, second_shift, up_bias, down_bias)
    counts = [v.shape[0] for v in vectors]
    joined_line = direct_gather(grid, pack_joined(joined_weight, vectors), Z)
    query_mat, key_mat, value_mat, riders = gather_joined(grid, joined_line)
    gain_one, shift_one, _, dense_vec, gain_two, shift_two, up_vec, down_vec, query_vec, value_vec = unpack_vectors(
        riders, counts
    )

    up_kept, up_given = (core_columns(up_weight, which) for which in (core, 1 - core))
    up_blocks = [half for side in (up_kept, grid.shift(up_given, CORE)) for half in (side[:, :width], side[:, width:])]
    lines = ("y", "x", "z")
    up_shard = after(jnp.stack([*up_blocks, dense_weight]), *joined_line[1:])
    up_lines = lax.all_gather(up_shard, lines, axis=0)
    down_mat = lax.all_gather(after(down_weight, *joined_line[1:]), lines, axis=0, tiled=True)

    before = [after(tokens, *joined_line[1:])]
    for _ in range(hops):
        before.append(grid.to_later(before[-1]))
    first_pos = grid.linear * tok_rows - WINDOW
    positions = first_pos + jnp.arange(WINDOW + tok_rows, dtype=jnp.int32)
    seg_ext = segment_ids(lengths, valid_count, positions)
    query_side, key_side = side_lanes(seg_ext, tok_rows)
    slopes = jnp.asarray(slope_lanes())
    live_rows = (positions[WINDOW:] < valid_count[0])[:, None]
    change_low = jnp.where(live_rows, cotangent, jnp.zeros_like(cotangent))
    change_both = jnp.concatenate([change_low, grid.shift(change_low, CORE)], axis=0)

    values = tokens.astype(f32)
    mats, shifts = (key_mat, value_mat), (jnp.zeros_like(value_vec), value_vec)
    normed_ext, stats, keys, all_values, queries = project(
        tokens, gain_one, shift_one, (*mats, query_mat), (*shifts, query_vec), hops, hops + 1
    )
    chunks = [(tokens, stats)]
    for hop in range(1, hops + 1):
        normed_ext, stats, keys, all_values = project(
            before[hop], gain_one, shift_one, mats, shifts, hops - hop, hops + 1, (normed_ext, keys, all_values)
        )
        chunks.insert(0, (before[hop], stats))
    context, log_total = attend(queries, keys, all_values, query_side, key_side, after(slopes, change_both))
    dense_part = after(up_lines[:, 4].reshape(-1, width), context)
    dense_other = grid.shift(dense_part, CORE)
    dense_sides = [jnp.where(core == which, dense_part, dense_other).reshape(chips, -1, width) for which in range(2)]
    dense_mat = jnp.stack(dense_sides, axis=1).reshape(-1, width)
    middle = values + dot_nn(context, dense_mat) + dense_vec
    normal_two, inverse_two = normalize(middle)
    normed_two = (normal_two * gain_two + shift_two).astype(bf16)
    normed_other = grid.shift(normed_two, CORE)
    hidden, slope = hidden_units(chips, core, normed_two, normed_other, up_lines, core_columns(up_vec, core))
    up_mat = whole_up(grid, up_lines, hidden)

    def far_sums(part, terms, *earlier):
        axis = (Y, X)[part]
        moving = terms[0]
        for step in range(1, grid.size[axis]):
            moving = add_after(grid.shift(moving, axis), terms[step], *earlier)
        return moving

    out_change = change_low.astype(f32)
    down_sums, down_vec_grad = down_terms(hidden, change_both)
    down_plane = lax.psum_scatter(down_sums, ("y", "x"), scatter_dimension=0, tiled=True)
    pre_change, up_core_grad = hidden_back(change_both, down_mat, slope, (down_sums,))
    given = product_nt(pre_change, up_mat, bf16, 1, tok_rows)
    up_sums = up_terms(normed_two, normed_other, pre_change, (given,))
    up_plane = lax.psum_scatter(up_sums, ("y", "x"), scatter_dimension=0, tiled=True)
    middle_change, branch_change, context_change, gain_two_grad, shift_two_grad, dense_vec_grad = middle_back(
        pre_change, up_mat, grid.shift(given, CORE), middle, gain_two, change_low, dense_mat, (up_sums,)
    )
    halves = HEADS // 4
    changes = attend_back(
        queries, keys, all_values, context_change, context, log_total, query_side, key_side, slopes, 0, halves
    )
    down_plane = after(down_plane, changes[0]).reshape(nz, -1, width)
    query_change, key_change, value_change = attend_back(
        queries, keys, all_values, context_change, context, log_total, query_side, key_side, after(slopes, down_plane),
        halves, halves, changes,
    )
    backs = [(back_y, back_x) for back_y in range(1, ny + 1) for back_x in range(1, nx + 1)]

    down_grad = direct_reduce(grid, down_plane, Z)
    chips_at = [(y - back_y) % ny * nx + (x - back_x) % nx for back_y, back_x in backs]
    rights = (query_change, key_change, value_change, branch_change)
    joined_given = joined_terms(normed_ext, context, rights, chips_at, core, (down_grad,))
    pairs = [(key_change, key_mat), (value_change, value_mat)]
    returned, *sums = chunk_back(
        [(left, 0, right) for left, right in pairs], chunks[0], bf16, None, joined_given[:1]
    )
    chunk_sums = [sums]
    joined_kept = split_terms(
        joined_given[2], grid.shift(joined_given[0], CORE), joined_given[3], grid.shift(joined_given[1], CORE), ny, nx, (returned,)
    )
    own_change, *sums = chunk_back(
        [(left, hops, right) for left, right in pairs] + [(query_change, 0, query_mat)], chunks[-1], f32, None, joined_kept
    )
    chunk_sums.append(sums)
    done = own_change
    for chunk in range(1, hops):
        arrived = grid.to_earlier(returned)
        returned, *sums = chunk_back(
            [(left, chunk, right) for left, right in pairs], chunks[chunk], bf16, arrived, (done,)
        )
        chunk_sums.append(sums)
        done = returned
    joined_near = []
    for terms, axis in ((joined_kept[:nx], X), (joined_kept[nx:], Y)):
        total = terms[0]
        for step in range(1, grid.size[axis]):
            total = add_after(grid.shift(total, axis), terms[step], done, split=step == grid.size[axis] - 1)
        joined_near.append(total)
    nears = [*joined_near[0], *joined_near[1]]
    up_rows_both = after(up_plane, *nears).reshape(2, nz, up_rows, ff_core).swapaxes(0, 1)
    returned = grid.to_earlier(returned)
    branch_kept, branch_given = branch_terms(hidden, down_mat, nears)
    joined_far = [far_sums(part, joined_near[part], returned, branch_kept) for part in range(2)]
    both = [half.reshape(4, nz // 2, -1, width) for half in joined_far]
    both = jnp.concatenate(both, axis=1)

    def line_term(step):
        return lax.dynamic_index_in_dim(both, (z + step) % nz, 1, keepdims=False)

    arrived = [grid.shift(line_term(step), Z, step) for step in range(1, nz)]
    joined_grad, dense_grad = finish_joined(line_term(0), arrived)
    up_sum = direct_reduce(grid, up_rows_both, Z, arrived)
    up_mine = lax.dynamic_index_in_dim(up_sum, core, 0, keepdims=False)
    up_other = grid.shift(lax.dynamic_index_in_dim(up_sum, 1 - core, 0, keepdims=False), CORE)
    returned = returned.astype(f32)

    def interleave(mine, other):
        first, second = jnp.where(core == 0, mine, other), jnp.where(core == 0, other, mine)
        wide = mine.shape[1] // chips
        cuts = [slice(chip * wide, (chip + 1) * wide) for chip in range(chips)]
        return jnp.concatenate([side[:, cut] for cut in cuts for side in (first, second)], axis=1)

    up_grad = interleave(up_mine, up_other)
    branch_two = branch_kept + grid.shift(branch_given, CORE).astype(f32)
    layer_output = jnp.where(live_rows, middle + (branch_two + down_vec), 0.0).astype(bf16)
    gain_one_grad, shift_one_grad = (sum(total).reshape(-1) for total in zip(*chunk_sums))
    joined_vec_grad = jnp.stack(
        [
            joined_given[4].reshape(HEADS, HEAD_DIM),
            joined_given[5].reshape(HEADS, HEAD_DIM),
        ],
        axis=1,
    ).reshape(-1)
    input_grad = (middle_change + norm_back(own_change + returned, *normalize(values), gain_one)).astype(bf16)
    up_parts = up_core_grad.reshape(chips, 1, -1)
    up_vec_grad = jnp.concatenate(
        [jnp.where(core == which, up_parts, jnp.zeros_like(up_parts)) for which in range(2)], axis=1
    ).reshape(-1)
    vector_grads = (
        gain_one_grad, shift_one_grad, joined_vec_grad, dense_vec_grad, gain_two_grad, shift_two_grad, up_vec_grad,
        down_vec_grad,
    )
    cuts = np.cumsum([0] + counts)
    vector_rows = jnp.concatenate([v.reshape(grid.count, -1) for v in vector_grads], axis=1)
    owned = reduce_scatter_small(grid, after(vector_rows, *nears))
    owned = [owned[cuts[i] : cuts[i + 1]] for i in range(len(counts))]
    return (
        layer_output,
        input_grad,
        owned[0],
        owned[1],
        joined_grad,
        owned[2],
        dense_grad,
        owned[3],
        owned[4],
        owned[5],
        up_grad,
        owned[6],
        down_grad,
        owned[7],
    )


def solution(mesh):
    blocks, heads = mesh.devices.shape
    split = jax.sharding.Mesh(mesh.devices.reshape(2, blocks // 4, 2, heads), ALL)
    rows, vector, same = P(ALL, None), P(ALL), P()
    return jax.shard_map(
        on_device,
        mesh=split,
        in_specs=(
            rows, rows, same, same, vector, vector, rows, vector, rows, vector, vector, vector, rows, vector, rows, vector
        ),
        out_specs=(rows, rows, vector, vector, rows, vector, rows, vector, vector, vector, rows, vector, rows, vector),
        check_vma=False,
    )
```

```python
import functools

import functools

import jax
import jax.numpy as jnp
import numpy as np
from jax import lax
from jax.experimental import pallas as pl
from jax.experimental.pallas import tpu as pltpu
from jax.sharding import PartitionSpec as P

HEADS = 16
HEAD_DIM = 64
WINDOW = 1024
NDOCS = 32

ALL = ("y", "x", "core", "z")
norm_eps = 1e-05
bf16 = jnp.bfloat16
f32 = jnp.float32

MASKED = -1e30
TILE = 256
WIDE = 512
LANES = 128
SLOPE_LANE = NDOCS + 1
ROW_LANE = SLOPE_LANE + 6
SCALE = HEAD_DIM**-0.5
VMEM_LIMIT = 50 * 2**20
VMEM_ALL = 52 * 2**20
SHORT = pl.CostEstimate(flops=1, bytes_accessed=1, transcendentals=0)


def normalize(values):
    centred = values - jnp.mean(values, axis=-1, keepdims=True)
    inverse = lax.rsqrt(jnp.mean(centred * centred, axis=-1, keepdims=True) + norm_eps)
    return centred * inverse, inverse


def norm_back(change, normal, inverse, gain):
    scaled = change * gain
    mean_one = jnp.mean(scaled, axis=-1, keepdims=True)
    mean_two = jnp.mean(scaled * normal, axis=-1, keepdims=True)
    return inverse * (scaled - mean_one - normal * mean_two)


def dot_nn(left, right):
    return lax.dot_general(left, right, (((1,), (0,)), ((), ())), preferred_element_type=f32)


def dot_nt(left, right):
    return lax.dot_general(left, right, (((1,), (1,)), ((), ())), preferred_element_type=f32)


def dot_tn(left, right):
    return lax.dot_general(left, right, (((0,), (0,)), ((), ())), preferred_element_type=f32)


class Grid:
    def __init__(self):
        self.size = tuple(lax.axis_size(name) for name in ALL)
        self.here = tuple(lax.axis_index(name) for name in ALL)
        self.count = int(np.prod(self.size))
        self.linear = lax.axis_index(ALL)

    def shift(self, block, axis, distance=1):
        places = np.arange(self.count).reshape(self.size)
        ahead = np.roll(places, -distance, axis)
        return lax.ppermute(block, ALL, list(zip(places.ravel().tolist(), ahead.ravel().tolist())))

    def to_later(self, block):
        return lax.ppermute(block, ALL, [(i, i + 1) for i in range(self.count - 1)])

    def to_earlier(self, block):
        return lax.ppermute(block, ALL, [(i + 1, i) for i in range(self.count - 1)])


Y, X, CORE, Z = range(4)


def after(value, *earlier):
    anywhere = pl.BlockSpec(memory_space=pl.ANY)
    return pl.pallas_call(
        lambda *refs: None,
        in_specs=[anywhere] * (1 + len(earlier)),
        out_specs=anywhere,
        out_shape=jax.ShapeDtypeStruct(value.shape, value.dtype),
        input_output_aliases={0: 0},
        compiler_params=pltpu.CompilerParams(vmem_limit_bytes=2**17),
    )(value, *earlier)


def ring_gather(grid, block, axis):
    pieces = [block]
    for _ in range(grid.size[axis] - 1):
        pieces.append(grid.shift(pieces[-1], axis))
    return pieces


def direct_gather(grid, block, axis):
    return [block] + [grid.shift(block, axis, step) for step in range(1, grid.size[axis])]


def plane_gather(grid, line):
    half = len(line) // 2
    got = []
    for part, (one, two) in enumerate(((X, Y), (Y, X))):
        near = jnp.stack(ring_gather(grid, jnp.stack(line[part * half : (part + 1) * half]), one))
        for two_step, far in enumerate(ring_gather(grid, near, two)):
            got.append((part * half, one, two, two_step, far))
    return got


def plane_places(grid, got):
    ny, nx, _, nz = grid.size
    found = []
    for step, one, two, two_step, block in got:
        entries = []
        for one_step in range(block.shape[0]):
            back = {one: one_step, two: two_step}
            chip = (grid.here[Y] - back[Y]) % ny * nx + (grid.here[X] - back[X]) % nx
            entries.append([(chip, (grid.here[Z] - step - k) % nz) for k in range(block.shape[1])])
        found.append(entries)
    return found


def copy_blocks(moves, sems):
    copies = [pltpu.make_async_copy(source, target, sems.at[i]) for i, (source, target) in enumerate(moves)]
    for copy in copies:
        copy.start()
    for copy in copies:
        copy.wait()


def assemble(kernel, places, pieces, shapes, moves):
    anywhere = pl.BlockSpec(memory_space=pl.ANY)
    return pl.pallas_call(
        kernel,
        in_specs=[pl.BlockSpec(memory_space=pltpu.SMEM)] + [anywhere] * len(pieces),
        out_specs=[pl.BlockSpec(memory_space=pltpu.VMEM)] * len(shapes),
        out_shape=[jax.ShapeDtypeStruct(shape, bf16) for shape in shapes],
        scratch_shapes=[pltpu.SemaphoreType.DMA((moves,))],
        compiler_params=pltpu.CompilerParams(vmem_limit_bytes=VMEM_ALL),
        cost_estimate=SHORT,
    )(places, *pieces)


def joined_kernel(places, *refs):
    *pieces, query, key, value, riders, sems = refs
    width = query.shape[-1]
    moves = []
    for piece in pieces:
        for near in range(piece.shape[0]):
            for step in range(piece.shape[1]):
                at = places[len(moves) // 4]
                for kind, whole in enumerate((query, key, value)):
                    moves.append((piece.at[near, step, kind, :, pl.ds(0, width)], whole.at[at]))
                moves.append((piece.at[near, step, 0, :, pl.ds(width, LANES)], riders.at[at]))
    copy_blocks(moves, sems)


def gather_joined(grid, line):
    got = plane_gather(grid, line)
    rows, width = line[0].shape[-2], line[0].shape[-1] - LANES
    pieces, places = [], []
    for (_, _, _, _, block), entries in zip(got, plane_places(grid, got)):
        for which, piece in ((grid.here[CORE], block), (1 - grid.here[CORE], grid.shift(block, CORE))):
            pieces.append(piece)
            places += [(chip * 2 + which) * grid.size[Z] + z for near in entries for chip, z in near]
    *mats, riders = assemble(
        joined_kernel,
        jnp.stack(places).astype(jnp.int32),
        pieces,
        [(grid.count, rows, width)] * 3 + [(grid.count, rows, LANES)],
        4 * len(places),
    )
    return *(mat.reshape(-1, width) for mat in mats), riders


def up_kernel(places, lines, up, sems):
    width = lines.shape[-1]
    moves = []
    for entry in range(lines.shape[0]):
        for side in range(2):
            at = places[2 * entry + side]
            for half in range(2):
                moves.append((lines.at[entry, 2 * side + half], up.at[at, :, pl.ds(half * width, width)]))
    copy_blocks(moves, sems)


def whole_up(grid, lines, *earlier):
    count, _, rows, width = lines.shape
    nz, core = grid.size[Z], grid.here[CORE]
    places = [(entry // nz * 2 + which) * nz + entry % nz for entry in range(count) for which in (core, 1 - core)]
    places = after(jnp.stack(places).astype(jnp.int32), *earlier)
    (up,) = assemble(up_kernel, places, [lines], [(grid.count, rows, 2 * width)], 4 * count)
    return up.reshape(-1, 2 * width)


def add(left, right, kind=bf16):
    return (left.astype(f32) + right.astype(f32)).astype(kind)


def ring_reduce(grid, term, axis, kind=bf16):
    count = grid.size[axis]
    total = term(1)
    for step in range(2, count + 1):
        total = add(grid.shift(total, axis), term(step), kind)
    return total


def sum_kernel(count, *refs):
    total = refs[0][...].astype(f32)
    for ref in refs[1:count]:
        total += ref[...].astype(f32)
    refs[-1][...] = total


def sum_after(arrays, *earlier):
    held = pl.BlockSpec(memory_space=pltpu.VMEM)
    return pl.pallas_call(
        functools.partial(sum_kernel, len(arrays)),
        in_specs=[held] * len(arrays) + [pl.BlockSpec(memory_space=pl.ANY)] * len(earlier),
        out_specs=held,
        out_shape=jax.ShapeDtypeStruct(arrays[0].shape, f32),
        compiler_params=pltpu.CompilerParams(vmem_limit_bytes=2**23),
        cost_estimate=SHORT,
    )(*arrays, *earlier)


def direct_reduce(grid, terms, axis, earlier=()):
    count, place = grid.size[axis], grid.here[axis]

    def term(step):
        return lax.dynamic_index_in_dim(terms, (place + step) % count, 0, keepdims=False)

    return sum_after([term(0)] + [grid.shift(term(step), axis, step) for step in range(1, count)], *earlier)


def down_kernel(left, right, out, total):
    out[...] = dot_tn(left[...], right[...]).astype(bf16)

    @pl.when(pl.program_id(0) == 0)
    def _():
        total[...] = jnp.sum(right[: right.shape[0] // 2].astype(f32), axis=0, keepdims=True)


def down_terms(hidden, change):
    tokens, units = hidden.shape
    width = change.shape[1]
    return pl.pallas_call(
        down_kernel,
        grid=(units // TILE,),
        in_specs=[
            pl.BlockSpec((tokens, TILE), lambda i: (0, i)),
            pl.BlockSpec((tokens, width), lambda i: (0, 0)),
        ],
        out_specs=[pl.BlockSpec((TILE, width), lambda i: (i, 0)), pl.BlockSpec((1, width), lambda i: (0, 0))],
        out_shape=[jax.ShapeDtypeStruct((units, width), bf16), jax.ShapeDtypeStruct((1, width), f32)],
        compiler_params=pltpu.CompilerParams(vmem_limit_bytes=VMEM_LIMIT),
        cost_estimate=SHORT,
    )(hidden, change)


def up_kernel_terms(own, other, right, *refs):
    rows = own.shape[0]
    refs[-1][...] = (dot_tn(own[...], right[:rows]) + dot_tn(other[...], right[rows:])).astype(bf16)


def up_terms(own, other, pre_change, earlier=()):
    rows, width = own.shape
    tokens, units = pre_change.shape
    left = pl.BlockSpec((rows, width), lambda i: (0, 0))
    return pl.pallas_call(
        up_kernel_terms,
        grid=(units // WIDE,),
        in_specs=[left, left, pl.BlockSpec((tokens, WIDE), lambda i: (0, i))]
        + [pl.BlockSpec(memory_space=pl.ANY)] * len(earlier),
        out_specs=pl.BlockSpec((width, WIDE), lambda i: (0, i)),
        out_shape=jax.ShapeDtypeStruct((width, units), bf16),
        compiler_params=pltpu.CompilerParams(vmem_limit_bytes=VMEM_LIMIT),
        cost_estimate=SHORT,
    )(own, other, pre_change, *earlier)


def add_kernel(split, left, right, *refs):
    if split == 0:
        refs[-1][...] = (left[...].astype(f32) + right[...].astype(f32)).astype(bf16)
    for i in range(split):
        refs[-split + i][...] = (left[i].astype(f32) + right[i].astype(f32)).astype(bf16)


def add_after(left, right, *earlier, split=False):
    held = pl.BlockSpec(memory_space=pltpu.VMEM)
    shape = jax.ShapeDtypeStruct(left.shape, bf16)
    if split:
        shape = [jax.ShapeDtypeStruct(left.shape[1:], bf16)] * left.shape[0]
    return pl.pallas_call(
        functools.partial(add_kernel, left.shape[0] if split else 0),
        in_specs=[held] * 2 + [pl.BlockSpec(memory_space=pl.ANY)] * len(earlier),
        out_specs=[held] * left.shape[0] if split else held,
        out_shape=shape,
        compiler_params=pltpu.CompilerParams(vmem_limit_bytes=VMEM_LIMIT),
        cost_estimate=SHORT,
    )(left, right, *earlier)


def product_kernel(left, right, *refs):
    refs[-1][...] = dot_nt(left[...], right[...]).astype(refs[-1].dtype)


def product_nt(left, right, kind, row_block=0, rows=None, earlier=()):
    rows = left.shape[0] if rows is None else rows
    depth, wide = left.shape[1], right.shape[0]
    return pl.pallas_call(
        product_kernel,
        grid=(wide // WIDE,),
        in_specs=[
            pl.BlockSpec((rows, depth), lambda i: (row_block, 0)),
            pl.BlockSpec((WIDE, depth), lambda i: (i, 0)),
        ]
        + [pl.BlockSpec(memory_space=pl.ANY)] * len(earlier),
        out_specs=pl.BlockSpec((rows, WIDE), lambda i: (0, i)),
        out_shape=jax.ShapeDtypeStruct((rows, wide), kind),
        compiler_params=pltpu.CompilerParams(vmem_limit_bytes=VMEM_LIMIT),
        cost_estimate=SHORT,
    )(left, right, *earlier)


def branch_kernel(hidden, down, *refs):
    kept, given = refs[-2:]
    product = dot_nn(hidden[...], down[...])
    rows = kept.shape[0]
    kept[...] = product[:rows]
    given[...] = product[rows:].astype(bf16)


def branch_terms(hidden, down, earlier=()):
    tokens, units = hidden.shape
    width = down.shape[1]
    rows = tokens // 2
    tile = pl.BlockSpec((rows, TILE), lambda i: (0, i))
    return pl.pallas_call(
        branch_kernel,
        grid=(width // TILE,),
        in_specs=[pl.BlockSpec((tokens, units), lambda i: (0, 0)), pl.BlockSpec((units, TILE), lambda i: (0, i))]
        + [pl.BlockSpec(memory_space=pl.ANY)] * len(earlier),
        out_specs=[tile, tile],
        out_shape=[jax.ShapeDtypeStruct((rows, width), f32), jax.ShapeDtypeStruct((rows, width), bf16)],
        compiler_params=pltpu.CompilerParams(vmem_limit_bytes=VMEM_LIMIT),
        cost_estimate=SHORT,
    )(hidden, down, *earlier)


def chunk_kernel(count, with_arrived, *refs):
    lefts, rights, (tokens, stats) = refs[:count], refs[count : 2 * count], refs[2 * count : 2 * count + 2]
    moved, gain_sum, shift_sum = refs[-3:]
    change = dot_nt(lefts[0][...], rights[0][...])
    for left, right in zip(lefts[1:], rights[1:]):
        change += dot_nt(left[...], right[...])
    normal = (tokens[...].astype(f32) - stats[:, :1]) * stats[:, 1:2]
    gain_sum[...] = jnp.sum(change * normal, axis=0, keepdims=True)
    shift_sum[...] = jnp.sum(change, axis=0, keepdims=True)
    if with_arrived:
        change += refs[2 * count + 2][...].astype(f32)
    moved[...] = change.astype(moved.dtype)


def chunk_back(pairs, chunk, kind, arrived=None, earlier=()):
    rows, width = chunk[0].shape
    tile = pl.BlockSpec((rows, WIDE), lambda i: (0, i))
    sums = pl.BlockSpec((1, WIDE), lambda i: (0, i))
    return pl.pallas_call(
        functools.partial(chunk_kernel, len(pairs), arrived is not None),
        grid=(width // WIDE,),
        in_specs=[pl.BlockSpec((rows, left.shape[1]), lambda i, at=at: (at, 0)) for left, at, _ in pairs]
        + [pl.BlockSpec((WIDE, right.shape[1]), lambda i: (i, 0)) for *_, right in pairs]
        + [tile, pl.BlockSpec((rows, LANES), lambda i: (0, 0))]
        + [tile] * (arrived is not None)
        + [pl.BlockSpec(memory_space=pl.ANY)] * len(earlier),
        out_specs=[tile, sums, sums],
        out_shape=[jax.ShapeDtypeStruct((rows, width), kind)] + [jax.ShapeDtypeStruct((1, width), f32)] * 2,
        compiler_params=pltpu.CompilerParams(vmem_limit_bytes=VMEM_LIMIT),
        cost_estimate=SHORT,
    )(
        *(left for left, *_ in pairs),
        *(right for *_, right in pairs),
        *chunk,
        *(() if arrived is None else (arrived,)),
        *earlier,
    )


def middle_kernel(pre_change, up, arrived, middle, gain, out_change, dense, *refs):
    middle_change, branch_change, context_change, gain_sum, shift_sum, branch_sum = refs[-6:]
    change = dot_nt(pre_change[...], up[...]) + arrived[...].astype(f32)
    normal, inverse = normalize(middle[...])
    moved = out_change[...].astype(f32) + norm_back(change, normal, inverse, gain[...])
    low = moved.astype(bf16)
    middle_change[...] = moved
    branch_change[...] = low
    context_change[...] = dot_nt(low, dense[...]).astype(bf16)
    first = pl.program_id(0) == 0
    for total, part in ((gain_sum, change * normal), (shift_sum, change), (branch_sum, low.astype(f32))):
        total[...] = jnp.where(first, 0.0, total[...]) + jnp.sum(part, axis=0, keepdims=True)


def middle_back(pre_change, up, arrived, middle, gain, out_change, dense, earlier=()):
    rows, width = middle.shape
    tile = pl.BlockSpec((TILE, width), lambda i: (i, 0))
    sums = pl.BlockSpec((1, width), lambda i: (0, 0))

    def whole(array):
        return pl.BlockSpec(array.shape, lambda i: (0, 0))

    return pl.pallas_call(
        middle_kernel,
        grid=(rows // TILE,),
        in_specs=[
            pl.BlockSpec((TILE, pre_change.shape[1]), lambda i: (i, 0)), whole(up), tile, tile, whole(gain), tile, whole(dense)
        ]
        + [pl.BlockSpec(memory_space=pl.ANY)] * len(earlier),
        out_specs=[tile, tile, tile, sums, sums, sums],
        out_shape=[
            jax.ShapeDtypeStruct((rows, width), f32),
            jax.ShapeDtypeStruct((rows, width), bf16),
            jax.ShapeDtypeStruct((rows, width), bf16),
        ]
        + [jax.ShapeDtypeStruct((1, width), f32)] * 3,
        compiler_params=pltpu.CompilerParams(vmem_limit_bytes=VMEM_LIMIT),
        cost_estimate=SHORT,
    )(pre_change, up, arrived, middle, gain, out_change, dense, *earlier)


def joined_kernel_terms(blocks, core, tokens_ext, context, query, key, value, branch, *refs):
    given_ahead, given_behind, kept_ahead, kept_behind, query_sum, value_sum = refs[-6:]

    @pl.when(pl.program_id(0) == 0)
    def _():
        query_sum[...] = jnp.sum(query[...].astype(f32), axis=0, keepdims=True)
        value_sum[...] = jnp.sum(value[...].astype(f32), axis=0, keepdims=True)

    left = tokens_ext[...]
    own = left[left.shape[0] - query.shape[0] :]
    rows = kept_ahead.shape[2]
    swapped = core[0] == 1
    for kind, (one, two) in enumerate(((own, query), (left, key), (left, value), (context[...], branch))):
        product = dot_tn(one, two[...])
        for part, (given, kept) in enumerate(((given_ahead, kept_ahead), (given_behind, kept_behind))):
            low, high = (product[(2 * side + part) * rows : (2 * side + part + 1) * rows] for side in range(2))
            given[0, kind] = jnp.where(swapped, low, high).astype(bf16)
            kept[0, kind] = jnp.where(swapped, high, low).astype(bf16)


def joined_terms(normed_ext, context, rights, chips_at, core, earlier=()):
    ext_rows, width = normed_ext.shape
    tok_rows = context.shape[0]
    count = len(chips_at)
    rows = width // count
    half = (1, 4, rows // 4, width)
    stacked = pl.BlockSpec(half, lambda i, at, core: (i, 0, 0, 0))
    sums = pl.BlockSpec((1, width), lambda i, at, core: (0, 0))

    def whole(array):
        return pl.BlockSpec(array.shape, lambda i, at, core: (0, 0))

    return pl.pallas_call(
        joined_kernel_terms,
        grid_spec=pltpu.PrefetchScalarGridSpec(
            num_scalar_prefetch=2,
            grid=(count,),
            in_specs=[
                pl.BlockSpec((ext_rows, rows), lambda i, at, core: (0, at[i])),
                pl.BlockSpec((tok_rows, rows), lambda i, at, core: (0, at[i])),
                *(whole(right) for right in rights),
                *[pl.BlockSpec(memory_space=pl.ANY)] * len(earlier),
            ],
            out_specs=[stacked] * 4 + [sums] * 2,
        ),
        out_shape=[jax.ShapeDtypeStruct((count, *half[1:]), bf16)] * 4 + [jax.ShapeDtypeStruct((1, width), f32)] * 2,
        compiler_params=pltpu.CompilerParams(vmem_limit_bytes=VMEM_LIMIT),
        cost_estimate=SHORT,
    )(
        jnp.stack(chips_at).astype(jnp.int32), jnp.reshape(core, (1,)).astype(jnp.int32), normed_ext, context, *rights, *earlier
    )


def split_kernel(nx, ahead, arrived_ahead, behind, arrived_behind, *refs):
    ny = ahead.shape[0]
    outs = refs[-nx - ny :]
    for back_y in range(ny):
        for back_x in range(nx):
            outs[back_x][back_y] = (ahead[back_y, back_x].astype(f32) + arrived_ahead[back_y, back_x].astype(f32)).astype(bf16)
            outs[nx + back_y][back_x] = (
                behind[back_y, back_x].astype(f32) + arrived_behind[back_y, back_x].astype(f32)
            ).astype(bf16)


def split_terms(ahead, arrived_ahead, behind, arrived_behind, ny, nx, earlier=()):
    arrays = [array.reshape(ny, nx, *array.shape[1:]) for array in (ahead, arrived_ahead, behind, arrived_behind)]
    shape = arrays[0].shape[2:]
    kinds = shape[0]
    rest = shape[1:]
    return pl.pallas_call(
        functools.partial(split_kernel, nx),
        grid=(kinds,),
        in_specs=[pl.BlockSpec((ny, nx, 1, *rest), lambda i: (0, 0, i, 0, 0))] * 4
        + [pl.BlockSpec(memory_space=pl.ANY)] * len(earlier),
        out_specs=[pl.BlockSpec((ny, 1, *rest), lambda i: (0, i, 0, 0))] * nx
        + [pl.BlockSpec((nx, 1, *rest), lambda i: (0, i, 0, 0))] * ny,
        out_shape=[jax.ShapeDtypeStruct((ny, *shape), bf16)] * nx + [jax.ShapeDtypeStruct((nx, *shape), bf16)] * ny,
        compiler_params=pltpu.CompilerParams(vmem_limit_bytes=VMEM_LIMIT),
        cost_estimate=SHORT,
    )(*arrays, *earlier)


def reduce_scatter_small(grid, terms):
    terms = terms.reshape(*grid.size, terms.shape[1])
    for axis, dim in ((CORE, 2), (X, 1), (Y, 0)):
        def term(step, terms=terms, axis=axis, dim=dim):
            return lax.dynamic_index_in_dim(terms, (grid.here[axis] - step) % grid.size[axis], dim, keepdims=False)

        terms = ring_reduce(grid, term, axis, f32)
    total = lax.dynamic_index_in_dim(terms, grid.here[Z], 0, keepdims=False)
    for step in range(1, grid.size[Z]):
        term = lax.dynamic_index_in_dim(terms, (grid.here[Z] + step) % grid.size[Z], 0, keepdims=False)
        total = total + grid.shift(term, Z, step)
    return total


def thirds(values):
    high = values.astype(bf16)
    rest = values - high.astype(f32)
    middle = rest.astype(bf16)
    return high, middle, (rest - middle.astype(f32)).astype(bf16)


def slope_lanes():
    lanes = np.zeros((HEADS // 2, 8, LANES), np.float32)
    for h in range(HEADS):
        rest = np.float32(2.0 ** (-8.0 * (h + 1) / HEADS))
        for part in range(3):
            piece = np.float32(rest.astype(bf16))
            rest = np.float32(rest - piece)
            lanes[h // 2, h % 2, SLOPE_LANE + part] = piece
            lanes[h // 2, h % 2, SLOPE_LANE + 3 + part] = piece
    return lanes


def side_lanes(seg_ext, tok_rows):
    lane = jnp.arange(LANES, dtype=jnp.int32)
    doc = lane[None, :] <= NDOCS
    seg_query = seg_ext[seg_ext.shape[0] - tok_rows :]
    query_side = jnp.where(doc & (lane[None, :] == seg_query[:, None]), 1.0, 0.0).astype(bf16)
    key_pos = jnp.arange(seg_ext.shape[0], dtype=jnp.int32)[:, None]
    key_side = jnp.where(doc & (lane[None, :] != seg_ext[:, None]), MASKED, 0.0)
    key_side = jnp.where((lane >= SLOPE_LANE) & (lane < SLOPE_LANE + 3), (key_pos // TILE * TILE).astype(f32), key_side)
    key_side = jnp.where((lane >= SLOPE_LANE + 3) & (lane < ROW_LANE), (key_pos % TILE).astype(f32), key_side)
    key_side = jnp.where((lane >= ROW_LANE) & (lane < ROW_LANE + 3), 1.0, key_side)
    return query_side, key_side.astype(bf16)


def key_tiles(tile):
    wide = WINDOW // TILE
    edges = [(tile + step) * TILE for step in (0, 1, wide, wide + 1)]
    return [slice(edges[i], edges[i + 1]) for i in range(3)]


def attend_kernel(query, key, value, query_side, key_side, slope, context, log_total):
    pair = pl.program_id(0)
    lane = lax.broadcasted_iota(jnp.int32, (TILE, LANES), 1)
    causal = lax.broadcasted_iota(jnp.int32, (TILE, TILE), 0) >= lax.broadcasted_iota(jnp.int32, (TILE, TILE), 1)
    keys = jnp.concatenate([key[...], key_side[...]], axis=1)
    for tile in range(query.shape[0] // TILE):
        rows = slice(tile * TILE, (tile + 1) * TILE)
        first, middle, last = key_tiles(tile)
        scaled = query[rows, :] * jnp.asarray(SCALE, bf16)
        outs, logs = [], []
        for half in range(2):
            mine = (lane >= HEAD_DIM) == (half == 1)
            side = query_side[rows, :] + slope[0, half : half + 1, :].astype(bf16)
            queries = jnp.concatenate([jnp.where(mine, scaled, jnp.zeros_like(scaled)), side], axis=1)
            inner = dot_nt(queries, keys[middle])
            outer = jnp.where(causal, dot_nt(queries, keys[last]), dot_nt(queries, keys[first]))
            top = jnp.maximum(jnp.max(inner, axis=1, keepdims=True), jnp.max(outer, axis=1, keepdims=True))
            inner = jnp.exp(inner - top)
            outer = jnp.exp(outer - top)
            total = jnp.sum(inner, axis=1, keepdims=True) + jnp.sum(outer, axis=1, keepdims=True)
            summed = dot_nn(inner.astype(bf16), value[middle, :])
            summed += dot_nn(jnp.where(causal, outer, 0.0).astype(bf16), value[last, :])
            summed += dot_nn(jnp.where(causal, 0.0, outer).astype(bf16), value[first, :])
            outs.append(summed / total)
            logs.append(top + jnp.log(total))
        context[rows, :] = jnp.where(lane < HEAD_DIM, outs[0], outs[1]).astype(bf16)
        before = jnp.where(pair == 0, jnp.zeros((TILE, LANES), f32), log_total[rows, :])
        log_total[rows, :] = jnp.where(lane == 2 * pair, logs[0], jnp.where(lane == 2 * pair + 1, logs[1], before))


def attend(queries, keys, values, query_side, key_side, slopes):
    tok_rows, width = queries.shape
    key_rows = keys.shape[0]
    steps = HEADS // 2
    return pl.pallas_call(
        attend_kernel,
        grid=(steps,),
        in_specs=[
            pl.BlockSpec((tok_rows, LANES), lambda p: (0, p)),
            pl.BlockSpec((key_rows, LANES), lambda p: (0, p)),
            pl.BlockSpec((key_rows, LANES), lambda p: (0, p)),
            pl.BlockSpec((tok_rows, LANES), lambda p: (0, 0)),
            pl.BlockSpec((key_rows, LANES), lambda p: (0, 0)),
            pl.BlockSpec((1, 8, LANES), lambda p: (p, 0, 0)),
        ],
        out_specs=[
            pl.BlockSpec((tok_rows, LANES), lambda p: (0, p)),
            pl.BlockSpec((tok_rows, LANES), lambda p: (0, 0)),
        ],
        out_shape=[
            jax.ShapeDtypeStruct((tok_rows, width), bf16),
            jax.ShapeDtypeStruct((tok_rows, LANES), f32),
        ],
        compiler_params=pltpu.CompilerParams(vmem_limit_bytes=VMEM_ALL),
        cost_estimate=SHORT,
    )(queries, keys, values, query_side, key_side, slopes)


def attend_back_kernel(
    query, key, value, change, context, log_total, query_side, key_side, slope, *refs, first_pair,
):
    query_change, key_change, value_change, key_sum, value_sum = refs[-5:]
    pair = first_pair + pl.program_id(0)
    lane = lax.broadcasted_iota(jnp.int32, (TILE, LANES), 1)
    causal = lax.broadcasted_iota(jnp.int32, (TILE, TILE), 0) <= lax.broadcasted_iota(jnp.int32, (TILE, TILE), 1)
    keys = jnp.concatenate([key[...], key_side[...]], axis=1)
    values = jnp.concatenate([value[...], key_side[...]], axis=1)
    keys_across = key[...].T
    key_sum[...] = jnp.zeros_like(key_sum)
    value_sum[...] = jnp.zeros_like(value_sum)

    def row_lanes(column):
        high, middle, low = thirds(column)
        lanes = jnp.where(lane == ROW_LANE + 2, low, jnp.zeros((TILE, LANES), bf16))
        return jnp.where(lane == ROW_LANE, high, jnp.where(lane == ROW_LANE + 1, middle, lanes))

    for tile in range(query.shape[0] // TILE):
        rows = slice(tile * TILE, (tile + 1) * TILE)
        first, middle, last = key_tiles(tile)
        scaled = query[rows, :] * jnp.asarray(SCALE, bf16)
        changed = change[rows, :]
        product = changed.astype(f32) * context[rows, :].astype(f32)
        logs = log_total[rows, :]
        parts = []
        for half in range(2):
            mine = (lane >= HEAD_DIM) == (half == 1)
            asked = jnp.where(mine, scaled, jnp.zeros_like(scaled))
            moved = jnp.where(mine, changed, jnp.zeros_like(changed))
            log_row = jnp.sum(jnp.where(lane == 2 * pair + half, logs, 0.0), axis=1, keepdims=True)
            inner_row = jnp.sum(jnp.where(mine, product, 0.0), axis=1, keepdims=True)
            side = query_side[rows, :] + slope[0, half : half + 1, :].astype(bf16) + row_lanes(-log_row)
            queries = jnp.concatenate([asked, side], axis=1)
            changes = jnp.concatenate([moved, row_lanes(-inner_row)], axis=1)
            prob = jnp.exp(dot_nt(keys[middle], queries))
            prob_edge = jnp.exp(jnp.where(causal, dot_nt(keys[last], queries), dot_nt(keys[first], queries)))
            score = (prob * dot_nt(values[middle], changes)).astype(bf16)
            score_edge = prob_edge * jnp.where(causal, dot_nt(values[last], changes), dot_nt(values[first], changes))
            score_last = jnp.where(causal, score_edge, 0.0).astype(bf16)
            score_first = jnp.where(causal, 0.0, score_edge).astype(bf16)
            value_sum[middle, :] += dot_nn(prob.astype(bf16), moved)
            value_sum[last, :] += dot_nn(jnp.where(causal, prob_edge, 0.0).astype(bf16), moved)
            value_sum[first, :] += dot_nn(jnp.where(causal, 0.0, prob_edge).astype(bf16), moved)
            key_sum[middle, :] += dot_nn(score, asked)
            key_sum[last, :] += dot_nn(score_last, asked)
            key_sum[first, :] += dot_nn(score_first, asked)
            parts.append(
                dot_nn(keys_across[:, middle], score)
                + dot_nn(keys_across[:, last], score_last)
                + dot_nn(keys_across[:, first], score_first)
            )
        entry = lax.broadcasted_iota(jnp.int32, (LANES, TILE), 0)
        query_change[rows, :] = (jnp.where(entry < HEAD_DIM, parts[0], parts[1]).T * SCALE).astype(bf16)
    key_change[...] = key_sum[...].astype(bf16)
    value_change[...] = value_sum[...].astype(bf16)


def attend_back(queries, keys, values, change, context, log_total, query_side, key_side, slopes, first_pair, count, others=()):
    tok_rows, width = queries.shape
    key_rows = keys.shape[0]
    steps = HEADS // 2
    by_query = pl.BlockSpec((tok_rows, LANES), lambda p: (0, first_pair + p))
    by_key = pl.BlockSpec((key_rows, LANES), lambda p: (0, first_pair + p))
    return pl.pallas_call(
        functools.partial(attend_back_kernel, first_pair=first_pair),
        grid=(count,),
        in_specs=[
            by_query,
            by_key,
            by_key,
            by_query,
            by_query,
            pl.BlockSpec((tok_rows, LANES), lambda p: (0, 0)),
            pl.BlockSpec((tok_rows, LANES), lambda p: (0, 0)),
            pl.BlockSpec((key_rows, LANES), lambda p: (0, 0)),
            pl.BlockSpec((1, 8, LANES), lambda p: (first_pair + p, 0, 0)),
        ]
        + [pl.BlockSpec(memory_space=pl.ANY)] * len(others),
        out_specs=[by_query, by_key, by_key],
        out_shape=[
            jax.ShapeDtypeStruct((tok_rows, width), bf16),
            jax.ShapeDtypeStruct((key_rows, width), bf16),
            jax.ShapeDtypeStruct((key_rows, width), bf16),
        ],
        input_output_aliases={9 + i: i for i in range(len(others))},
        scratch_shapes=[pltpu.VMEM((key_rows, LANES), f32), pltpu.VMEM((key_rows, LANES), f32)],
        compiler_params=pltpu.CompilerParams(vmem_limit_bytes=VMEM_ALL),
        cost_estimate=SHORT,
    )(queries, keys, values, change, context, log_total, query_side, key_side, slopes, *others)


def segment_ids(lengths, valid_count, positions):
    doc_ends = jnp.cumsum(lengths)
    passed = jnp.sum((doc_ends[None, :] <= positions[:, None]).astype(jnp.int32), axis=1)
    inside = jnp.where(positions < valid_count[0], passed, NDOCS)
    return jnp.where(positions < 0, -1, inside)


ROOT = float(np.sqrt(2.0 / np.pi))


def gelu_parts(values):
    square = values * values
    rise = 0.5 * jnp.tanh(values * (square * (ROOT * 0.044715) + ROOT)) + 0.5
    bend = values * (square * (6.0 * ROOT * 0.044715) + 2.0 * ROOT)
    return values * rise, rise + bend * (rise - rise * rise)


def hidden_kernel(chips, core, own, other, up_kept, up_given, bias, hidden, slope, sides):
    rows, width = own.shape
    wide = width // (2 * chips)

    @pl.when(pl.program_id(0) == 0)
    def _():
        first = core[0] == 0
        for chip in range(chips):
            start, to = 2 * chip * wide, slice(chip * wide, (chip + 1) * wide)
            for part, tokens in enumerate((own, other)):
                low, high = tokens[:, start : start + wide], tokens[:, start + wide : start + 2 * wide]
                sides[0, part * rows : (part + 1) * rows, to] = jnp.where(first, low, high)
                sides[1, part * rows : (part + 1) * rows, to] = jnp.where(first, high, low)

    kept = up_kept[...].reshape(width // 2, WIDE)
    given = up_given[...].reshape(width // 2, WIDE)
    for start in range(0, 2 * rows, TILE):
        product = dot_nn(sides[0, start : start + TILE], kept) + dot_nn(sides[1, start : start + TILE], given)
        value, rise = gelu_parts(product + bias[...])
        hidden[start : start + TILE, :] = value.astype(bf16)
        slope[start : start + TILE, :] = rise.astype(bf16)


def hidden_units(chips, core, own, other, lines, bias):
    rows, depth = own.shape
    count, _, height, width = lines.shape
    units = 2 * width
    steps = width // WIDE
    columns = pl.BlockSpec((2 * rows, WIDE), lambda i, at: (0, i))
    whole = pl.BlockSpec((rows, depth), lambda i, at: (0, 0))

    def block(side):
        return pl.BlockSpec((count, 1, height, WIDE), lambda i, at: (0, 2 * side + i // steps, 0, i % steps))

    return pl.pallas_call(
        functools.partial(hidden_kernel, chips),
        grid_spec=pltpu.PrefetchScalarGridSpec(
            num_scalar_prefetch=1,
            grid=(units // WIDE,),
            in_specs=[whole, whole, block(0), block(1), pl.BlockSpec((1, WIDE), lambda i, at: (0, i))],
            out_specs=[columns, columns],
            scratch_shapes=[pltpu.VMEM((2, 2 * rows, depth // 2), bf16)],
        ),
        out_shape=[jax.ShapeDtypeStruct((2 * rows, units), bf16)] * 2,
        compiler_params=pltpu.CompilerParams(vmem_limit_bytes=VMEM_LIMIT),
        cost_estimate=SHORT,
    )(jnp.reshape(core, (1,)).astype(jnp.int32), own, other, lines, lines, bias)


def pre_change_kernel(change, down, slope, *refs):
    pre_change, total = refs[-2:]
    moved = (dot_nt(change[...], down[...]) * slope[...].astype(f32)).astype(bf16)
    pre_change[...] = moved
    total[...] = jnp.sum(moved.astype(f32), axis=0, keepdims=True)


def hidden_back(change, down, slope, earlier=()):
    tokens, depth = change.shape
    units = down.shape[0]
    columns = pl.BlockSpec((tokens, WIDE), lambda i: (0, i))
    return pl.pallas_call(
        pre_change_kernel,
        grid=(units // WIDE,),
        in_specs=[
            pl.BlockSpec((tokens, depth), lambda i: (0, 0)),
            pl.BlockSpec((WIDE, depth), lambda i: (i, 0)),
            columns,
        ]
        + [pl.BlockSpec(memory_space=pl.ANY)] * len(earlier),
        out_specs=[columns, pl.BlockSpec((1, WIDE), lambda i: (0, i))],
        out_shape=[jax.ShapeDtypeStruct((tokens, units), bf16), jax.ShapeDtypeStruct((1, units), f32)],
        compiler_params=pltpu.CompilerParams(vmem_limit_bytes=VMEM_LIMIT),
        cost_estimate=SHORT,
    )(change, down, slope, *earlier)


def projection_kernel(kinds, others, tokens, gain, shift, *refs):
    mats, shifts = refs[:kinds], refs[kinds : 2 * kinds]
    normed, stats, *outs, held = refs[2 * kinds + others :]

    @pl.when(pl.program_id(0) == 0)
    def _():
        values = tokens[...].astype(f32)
        mean = jnp.mean(values, axis=-1, keepdims=True)
        centred = values - mean
        inverse = lax.rsqrt(jnp.mean(centred * centred, axis=-1, keepdims=True) + norm_eps)
        low = (centred * inverse * gain[...] + shift[...]).astype(bf16)
        normed[...] = low
        held[...] = low
        lane = lax.broadcasted_iota(jnp.int32, stats.shape, 1)
        stats[...] = jnp.where(lane == 0, mean, inverse)

    for mat, add, out in zip(mats, shifts, outs):
        out[...] = (dot_nn(held[...], mat[...]) + add[...]).astype(bf16)


def project(tokens, gain, shift, mats, shifts, chunk, chunks, others=()):
    rows, width = tokens.shape
    kinds = len(mats)
    ext_rows = chunks * rows
    fixed = pl.BlockSpec((rows, width), lambda i: (0, 0))
    row = pl.BlockSpec((1, width), lambda i: (0, 0))
    placed = pl.BlockSpec((rows, WIDE), lambda i: (chunk, i))
    out_specs = [pl.BlockSpec((rows, width), lambda i: (chunk, 0)), pl.BlockSpec((rows, LANES), lambda i: (0, 0)), placed, placed]
    out_shape = [jax.ShapeDtypeStruct((ext_rows, width), bf16), jax.ShapeDtypeStruct((rows, LANES), f32)]
    out_shape += [jax.ShapeDtypeStruct((ext_rows, width), bf16)] * 2
    if kinds == 3:
        out_specs.append(pl.BlockSpec((rows, WIDE), lambda i: (0, i)))
        out_shape.append(jax.ShapeDtypeStruct((rows, width), bf16))
    aliases = {3 + 2 * kinds + i: place for i, place in enumerate((0, 2, 3)[: len(others)])}
    return pl.pallas_call(
        functools.partial(projection_kernel, kinds, len(others)),
        grid=(width // WIDE,),
        in_specs=[fixed, row, row]
        + [pl.BlockSpec((width, WIDE), lambda i: (0, i))] * kinds
        + [pl.BlockSpec((1, WIDE), lambda i: (0, i))] * kinds
        + [pl.BlockSpec(memory_space=pl.ANY)] * len(others),
        out_specs=out_specs,
        out_shape=out_shape,
        scratch_shapes=[pltpu.VMEM((rows, width), bf16)],
        input_output_aliases=aliases,
        compiler_params=pltpu.CompilerParams(vmem_limit_bytes=VMEM_LIMIT),
        cost_estimate=SHORT,
    )(tokens, gain, shift, *mats, *shifts, *others)


def pack_kernel(weight, *refs):
    *vectors, packed, rider = refs
    width = packed.shape[-1] - LANES
    for kind in range(3):
        for pair in range(HEADS // 2):
            at = [((2 * pair + half) * 3 + kind) * HEAD_DIM for half in range(2)]
            packed[kind, :, pair * LANES : (pair + 1) * LANES] = jnp.concatenate(
                [weight[:, start : start + HEAD_DIM] for start in at], axis=1
            )
        packed[kind, :, width:] = jnp.zeros((packed.shape[1], LANES), bf16)
    rider[...] = jnp.zeros_like(rider)
    for i, vector in enumerate(vectors):
        rider[i : i + 1, : vector.shape[1]] = vector[...].astype(f32)
    packed[0, :, width:] = rider[...].astype(bf16)


def pack_joined(weight, vectors):
    rows, wide = weight.shape
    return pl.pallas_call(
        pack_kernel,
        out_shape=jax.ShapeDtypeStruct((3, rows, wide // 3 + LANES), bf16),
        scratch_shapes=[pltpu.VMEM((rows, LANES), f32)],
    )(weight, *(v[None] for v in vectors))


def unpack_kernel(riders, *refs):
    *vectors, query, value = refs
    for i, vector in enumerate(vectors):
        wide = vector.shape[1] // riders.shape[0]
        for device in range(riders.shape[0]):
            vector[:, device * wide : (device + 1) * wide] = riders[device, i : i + 1, :wide].astype(f32)
    for pair in range(HEADS // 2):
        for offset, out in ((0, query), (HEAD_DIM, value)):
            start = 4 * HEAD_DIM * pair + offset
            halves = [vectors[2][:, at : at + HEAD_DIM] for at in (start, start + 2 * HEAD_DIM)]
            out[:, pair * LANES : (pair + 1) * LANES] = jnp.concatenate(halves, axis=1)


def unpack_vectors(riders, counts):
    sizes = [riders.shape[0] * count for count in counts] + [HEADS * HEAD_DIM] * 2
    return pl.pallas_call(
        unpack_kernel,
        out_shape=[jax.ShapeDtypeStruct((1, size), f32) for size in sizes],
        cost_estimate=SHORT,
    )(riders)


def finish_kernel(count, *refs):
    terms, (joined, dense) = refs[:count], refs[-2:]
    total = terms[0][...].astype(f32)
    for term in terms[1:]:
        total += term[...].astype(f32)
    dense[...] = total[3]
    for first in range(0, 3 * HEADS, 2):
        halves = []
        for at in (first, first + 1):
            start = at // 3 * HEAD_DIM
            halves.append(total[at % 3, :, start : start + HEAD_DIM])
        joined[:, first * HEAD_DIM : (first + 2) * HEAD_DIM] = jnp.concatenate(halves, axis=1)


def finish_joined(own, arrived, earlier=()):
    _, rows, width = own.shape
    held = pl.BlockSpec(memory_space=pltpu.VMEM)
    return pl.pallas_call(
        functools.partial(finish_kernel, 1 + len(arrived)),
        in_specs=[held] * (1 + len(arrived)) + [pl.BlockSpec(memory_space=pl.ANY)] * len(earlier),
        out_specs=[held, held],
        out_shape=[jax.ShapeDtypeStruct((rows, 3 * width), f32), jax.ShapeDtypeStruct((rows, width), f32)],
        compiler_params=pltpu.CompilerParams(vmem_limit_bytes=2**23),
        cost_estimate=SHORT,
    )(own, *arrived, *earlier)


def on_device(
    tokens,
    cotangent,
    lengths,
    valid_count,
    first_gain,
    first_shift,
    joined_weight,
    joined_bias,
    dense_weight,
    dense_bias,
    second_gain,
    second_shift,
    up_weight,
    up_bias,
    down_weight,
    down_bias,
):
    grid = Grid()
    tok_rows, width = tokens.shape
    hops = WINDOW // tok_rows
    shard_rows = joined_weight.shape[0]

    y, x, core, z = grid.here
    ny, nx, _, nz = grid.size
    chips = ny * nx
    up_rows, ff = up_weight.shape
    ff_core = ff // 2

    def core_columns(block, which):
        wide = block.shape[1] // chips // 2
        return jnp.concatenate(
            [lax.dynamic_slice_in_dim(block, (2 * chip + which) * wide, wide, 1) for chip in range(chips)], axis=1
        )

    vectors = (first_gain, first_shift, joined_bias, dense_bias, second_gain, second_shift, up_bias, down_bias)
    counts = [v.shape[0] for v in vectors]
    joined_line = direct_gather(grid, pack_joined(joined_weight, vectors), Z)
    query_mat, key_mat, value_mat, riders = gather_joined(grid, joined_line)
    gain_one, shift_one, _, dense_vec, gain_two, shift_two, up_vec, down_vec, query_vec, value_vec = unpack_vectors(
        riders, counts
    )

    up_kept, up_given = (core_columns(up_weight, which) for which in (core, 1 - core))
    up_blocks = [half for side in (up_kept, grid.shift(up_given, CORE)) for half in (side[:, :width], side[:, width:])]
    lines = ("y", "x", "z")
    up_shard = after(jnp.stack([*up_blocks, dense_weight]), *joined_line[1:])
    up_lines = lax.all_gather(up_shard, lines, axis=0)
    down_mat = lax.all_gather(after(down_weight, *joined_line[1:]), lines, axis=0, tiled=True)

    before = [after(tokens, *joined_line[1:])]
    for _ in range(hops):
        before.append(grid.to_later(before[-1]))
    first_pos = grid.linear * tok_rows - WINDOW
    positions = first_pos + jnp.arange(WINDOW + tok_rows, dtype=jnp.int32)
    seg_ext = segment_ids(lengths, valid_count, positions)
    query_side, key_side = side_lanes(seg_ext, tok_rows)
    slopes = jnp.asarray(slope_lanes())
    live_rows = (positions[WINDOW:] < valid_count[0])[:, None]
    change_low = jnp.where(live_rows, cotangent, jnp.zeros_like(cotangent))
    change_both = jnp.concatenate([change_low, grid.shift(change_low, CORE)], axis=0)

    values = tokens.astype(f32)
    mats, shifts = (key_mat, value_mat), (jnp.zeros_like(value_vec), value_vec)
    normed_ext, stats, keys, all_values, queries = project(
        tokens, gain_one, shift_one, (*mats, query_mat), (*shifts, query_vec), hops, hops + 1
    )
    chunks = [(tokens, stats)]
    for hop in range(1, hops + 1):
        normed_ext, stats, keys, all_values = project(
            before[hop], gain_one, shift_one, mats, shifts, hops - hop, hops + 1, (normed_ext, keys, all_values)
        )
        chunks.insert(0, (before[hop], stats))
    context, log_total = attend(queries, keys, all_values, query_side, key_side, after(slopes, change_both))
    dense_part = after(up_lines[:, 4].reshape(-1, width), context)
    dense_other = grid.shift(dense_part, CORE)
    dense_sides = [jnp.where(core == which, dense_part, dense_other).reshape(chips, -1, width) for which in range(2)]
    dense_mat = jnp.stack(dense_sides, axis=1).reshape(-1, width)
    middle = values + dot_nn(context, dense_mat) + dense_vec
    normal_two, inverse_two = normalize(middle)
    normed_two = (normal_two * gain_two + shift_two).astype(bf16)
    normed_other = grid.shift(normed_two, CORE)
    hidden, slope = hidden_units(chips, core, normed_two, normed_other, up_lines, core_columns(up_vec, core))
    up_mat = whole_up(grid, up_lines, hidden)

    def far_sums(part, terms, *earlier):
        axis = (Y, X)[part]
        moving = terms[0]
        for step in range(1, grid.size[axis]):
            moving = add_after(grid.shift(moving, axis), terms[step], *earlier)
        return moving

    out_change = change_low.astype(f32)
    down_sums, down_vec_grad = down_terms(hidden, change_both)
    down_plane = lax.psum_scatter(down_sums, ("y", "x"), scatter_dimension=0, tiled=True)
    pre_change, up_core_grad = hidden_back(change_both, down_mat, slope, (down_sums,))
    given = product_nt(pre_change, up_mat, bf16, 1, tok_rows)
    up_sums = up_terms(normed_two, normed_other, pre_change, (given,))
    up_plane = lax.psum_scatter(up_sums, ("y", "x"), scatter_dimension=0, tiled=True)
    middle_change, branch_change, context_change, gain_two_grad, shift_two_grad, dense_vec_grad = middle_back(
        pre_change, up_mat, grid.shift(given, CORE), middle, gain_two, change_low, dense_mat, (up_sums,)
    )
    halves = HEADS // 4
    changes = attend_back(
        queries, keys, all_values, context_change, context, log_total, query_side, key_side, slopes, 0, halves
    )
    down_plane = after(down_plane, changes[0]).reshape(nz, -1, width)
    query_change, key_change, value_change = attend_back(
        queries, keys, all_values, context_change, context, log_total, query_side, key_side, after(slopes, down_plane),
        halves, halves, changes,
    )
    backs = [(back_y, back_x) for back_y in range(1, ny + 1) for back_x in range(1, nx + 1)]

    down_grad = direct_reduce(grid, down_plane, Z)
    chips_at = [(y - back_y) % ny * nx + (x - back_x) % nx for back_y, back_x in backs]
    rights = (query_change, key_change, value_change, branch_change)
    joined_given = joined_terms(normed_ext, context, rights, chips_at, core, (down_grad,))
    pairs = [(key_change, key_mat), (value_change, value_mat)]
    returned, *sums = chunk_back(
        [(left, 0, right) for left, right in pairs], chunks[0], bf16, None, joined_given[:1]
    )
    chunk_sums = [sums]
    joined_kept = split_terms(
        joined_given[2], grid.shift(joined_given[0], CORE), joined_given[3], grid.shift(joined_given[1], CORE), ny, nx, (returned,)
    )
    own_change, *sums = chunk_back(
        [(left, hops, right) for left, right in pairs] + [(query_change, 0, query_mat)], chunks[-1], f32, None, joined_kept
    )
    chunk_sums.append(sums)
    done = own_change
    for chunk in range(1, hops):
        arrived = grid.to_earlier(returned)
        returned, *sums = chunk_back(
            [(left, chunk, right) for left, right in pairs], chunks[chunk], bf16, arrived, (done,)
        )
        chunk_sums.append(sums)
        done = returned
    joined_near = []
    for terms, axis in ((joined_kept[:nx], X), (joined_kept[nx:], Y)):
        total = terms[0]
        for step in range(1, grid.size[axis]):
            total = add_after(grid.shift(total, axis), terms[step], done, split=step == grid.size[axis] - 1)
        joined_near.append(total)
    nears = [*joined_near[0], *joined_near[1]]
    up_rows_both = after(up_plane, *nears).reshape(2, nz, up_rows, ff_core).swapaxes(0, 1)
    returned = grid.to_earlier(returned)
    branch_kept, branch_given = branch_terms(hidden, down_mat, nears)
    joined_far = [far_sums(part, joined_near[part], returned) for part in range(2)]
    both = [half.reshape(4, nz // 2, -1, width) for half in joined_far]
    both = jnp.concatenate(both, axis=1)

    def line_term(step):
        return lax.dynamic_index_in_dim(both, (z + step) % nz, 1, keepdims=False)

    arrived = [grid.shift(line_term(step), Z, step) for step in range(1, nz)]
    joined_grad, dense_grad = finish_joined(line_term(0), arrived)
    up_sum = direct_reduce(grid, up_rows_both, Z, arrived)
    up_mine = lax.dynamic_index_in_dim(up_sum, core, 0, keepdims=False)
    up_other = grid.shift(lax.dynamic_index_in_dim(up_sum, 1 - core, 0, keepdims=False), CORE)
    returned = returned.astype(f32)

    def interleave(mine, other):
        first, second = jnp.where(core == 0, mine, other), jnp.where(core == 0, other, mine)
        wide = mine.shape[1] // chips
        cuts = [slice(chip * wide, (chip + 1) * wide) for chip in range(chips)]
        return jnp.concatenate([side[:, cut] for cut in cuts for side in (first, second)], axis=1)

    up_grad = interleave(up_mine, up_other)
    branch_two = branch_kept + grid.shift(branch_given, CORE).astype(f32)
    layer_output = jnp.where(live_rows, middle + (branch_two + down_vec), 0.0).astype(bf16)
    gain_one_grad, shift_one_grad = (sum(total).reshape(-1) for total in zip(*chunk_sums))
    joined_vec_grad = jnp.stack(
        [
            joined_given[4].reshape(HEADS, HEAD_DIM),
            joined_given[5].reshape(HEADS, HEAD_DIM),
        ],
        axis=1,
    ).reshape(-1)
    input_grad = (middle_change + norm_back(own_change + returned, *normalize(values), gain_one)).astype(bf16)
    up_parts = up_core_grad.reshape(chips, 1, -1)
    up_vec_grad = jnp.concatenate(
        [jnp.where(core == which, up_parts, jnp.zeros_like(up_parts)) for which in range(2)], axis=1
    ).reshape(-1)
    vector_grads = (
        gain_one_grad, shift_one_grad, joined_vec_grad, dense_vec_grad, gain_two_grad, shift_two_grad, up_vec_grad,
        down_vec_grad,
    )
    cuts = np.cumsum([0] + counts)
    vector_rows = jnp.concatenate([v.reshape(grid.count, -1) for v in vector_grads], axis=1)
    owned = reduce_scatter_small(grid, after(vector_rows, *nears))
    owned = [owned[cuts[i] : cuts[i + 1]] for i in range(len(counts))]
    return (
        layer_output,
        input_grad,
        owned[0],
        owned[1],
        joined_grad,
        owned[2],
        dense_grad,
        owned[3],
        owned[4],
        owned[5],
        up_grad,
        owned[6],
        down_grad,
        owned[7],
    )


def solution(mesh):
    blocks, heads = mesh.devices.shape
    split = jax.sharding.Mesh(mesh.devices.reshape(2, blocks // 4, 2, heads), ALL)
    rows, vector, same = P(ALL, None), P(ALL), P()
    return jax.shard_map(
        on_device,
        mesh=split,
        in_specs=(
            rows, rows, same, same, vector, vector, rows, vector, rows, vector, vector, vector, rows, vector, rows, vector
        ),
        out_specs=(rows, rows, vector, vector, rows, vector, rows, vector, vector, vector, rows, vector, rows, vector),
        check_vma=False,
    )
```
